128 devices in a mesh: ctx: 8 (over z, core), fsdp: 16 (over y, x).
Axes of the slice: x: 4, y: 4, z: 4, core: 2. Of those that a mesh axis runs over, the one named last changes fastest.
Arguments:
- tokens: bfloat16 [16, 1024, 2048], P('fsdp', 'ctx'), may hold values from -6 to 6
- segments: int32 [16, 1024], P('fsdp', 'ctx'), may hold values from 0 to 3, as said below
- ln_gain: bfloat16 [2048], P('fsdp'), may hold values from 0.5 to 1.5
- ln_shift: bfloat16 [2048], P('fsdp'), may hold values from -3 to 3
- qkv_weight: bfloat16 [2048, 6144], P('fsdp'), may hold values from -0.125 to 0.125
- qkv_bias: bfloat16 [6144], P('fsdp'), may hold values from -3 to 3
- proj_weight: bfloat16 [2048, 2048], P('fsdp'), may hold values from -1 to 1
- proj_bias: bfloat16 [2048], P('fsdp'), may hold values from -3 to 3
- up_weight: bfloat16 [2048, 8192], P('fsdp'), may hold values from -0.125 to 0.125
- up_bias: bfloat16 [8192], P('fsdp'), may hold values from -3 to 3
- down_weight: bfloat16 [8192, 2048], P('fsdp'), may hold values from -0.0625 to 0.0625
- down_bias: bfloat16 [2048], P('fsdp'), may hold values from -3 to 3
- cotangent: bfloat16 [16, 1024, 2048], P('fsdp', 'ctx'), may hold values from -6 to 6
Outputs:
- block_out: bfloat16 [16, 1024, 2048], P('fsdp', 'ctx')
- token_grad: bfloat16 [16, 1024, 2048], P('fsdp', 'ctx')
- log_sums: float32 [16, 32, 1024], P('fsdp', None, 'ctx')
- gain_grad: float32 [2048], P('fsdp')
- shift_grad: float32 [2048], P('fsdp')
- qkv_weight_grad: float32 [2048, 6144], P('fsdp')
- qkv_bias_grad: float32 [6144], P('fsdp')
- proj_weight_grad: float32 [2048, 2048], P('fsdp')
- proj_bias_grad: float32 [2048], P('fsdp')
- up_weight_grad: float32 [2048, 8192], P('fsdp')
- up_bias_grad: float32 [8192], P('fsdp')
- down_weight_grad: float32 [8192, 2048], P('fsdp')
- down_bias_grad: float32 [2048], P('fsdp')
The draws below stay inside these ranges and needn't reach their ends.
Inputs may be any that keep to these rules, and one draw needn't show every extreme that they name: `segments`: along each sequence the ids never fall and every id from 0 to 3 forms one contiguous run; the run of id 1 begins at position 64 or earlier and ends within the last 128 positions.
All inputs are finite; a program needn't handle non-finite values.
Results may differ from the reference program's by a relative error of at most 0.02.
Values may be sent and summed in bfloat16 or wider, within the bound.
A program may use at most 640 MiB of HBM per device.

```python
import math
import jax
import jax.numpy as jnp
from jax import lax

D = 2048
HEADS = 32
HEAD = 64
ROT_DIMS = 32
FF = 8192
DOCS = 4
ROWS = 128
SEQ_LEN = 1024
SEQS = 16


def draw_segments(key, part):
    key = jax.random.fold_in(key, 11)
    subkeys = jax.random.split(key, 3)
    first_end = jax.random.randint(subkeys[0], (SEQS, 1), 1, ROWS // 2 + 1)
    tail_length = jax.random.randint(subkeys[1], (SEQS, 1), 2, ROWS)
    cut_length = jax.random.randint(subkeys[2], (SEQS, 1), 1, tail_length)
    row_index = jnp.arange(SEQ_LEN, dtype=jnp.int32)[None, :]
    long_end = SEQ_LEN - tail_length
    ids = (row_index >= first_end).astype(jnp.int32) + (row_index >= long_end).astype(jnp.int32)
    ids = ids + (row_index >= long_end + cut_length).astype(jnp.int32)
    return ids.astype(jnp.int32)


def strengthened(values, stream_key, source, target, parts, factor):
    owner, partner = [(jnp.arange(values.shape[axis_at]) // (values.shape[axis_at] // parts)).reshape([-1 if axis == axis_at else 1 for axis in range(values.ndim)]) for axis_at in (source, target)]
    chosen = jax.random.permutation(stream_key, parts)[partner]
    strong = (owner == chosen) | (owner == (partner + parts // 2) % parts)
    return jnp.where(strong, factor * values, values)


def shard_levels(key, dims, shards, smallest, largest):
    loudness, own = 1.0, jax.random.fold_in(key, 6)
    for axis_at, parts in shards:
        heights = jnp.exp(jax.random.uniform(jax.random.fold_in(own, axis_at), (parts,), jnp.float32, smallest / len(shards), largest / len(shards)))
        loudness = loudness * jnp.repeat(heights, dims[axis_at] // parts).reshape([-1 if axis == axis_at else 1 for axis in range(len(dims))])
    return loudness


def bell_draw(key, dims, spread, limit, shards=(), kind=jnp.bfloat16):
    values = spread * jax.random.normal(key, dims, jnp.float32)
    if shards:
        values = values * shard_levels(key, dims, shards, -0.22, 0.18)
    return jnp.clip(values, -limit, limit).astype(kind)


def noise_with(stream_key, shape, spread, bound, cuts, heavy, kind=jnp.bfloat16):
    entries = spread * jax.random.normal(stream_key, shape, jnp.float32)
    if cuts:
        entries = entries * shard_levels(stream_key, shape, cuts, -0.22, 0.18)
    return jnp.clip(strengthened(entries, jax.random.fold_in(stream_key, 3), *heavy), -bound, bound).astype(kind)


def setup_inputs(seed: int = 0) -> dict:
    key_of = jax.random.split(jax.random.key(seed), 14)
    tokens = noise_with(key_of[0], (SEQS, SEQ_LEN, D), 1.0, 6.0, ((0, 16), (1, 8)), (0, 2, 16, 2.0))
    segments = draw_segments(jax.random.fold_in(key_of[13], 71), 0)
    ln_gain = jnp.clip(1.0 + 0.1 * jax.random.normal(key_of[2], (D,), jnp.float32), 0.5, 1.5).astype(jnp.bfloat16)
    ln_shift = bell_draw(key_of[3], (D,), 0.3, 3.0, ((0, 16),))
    qkv_weight = bell_draw(key_of[4], (D, 3 * D), D ** -0.5, 0.125, ((0, 16),))
    qkv_bias = bell_draw(key_of[5], (3 * D,), 0.3, 3.0, ((0, 16),))
    proj_weight = bell_draw(key_of[6], (D, D), (D // 64) ** -0.5, 1.0, ((0, 16),))
    proj_bias = bell_draw(key_of[7], (D,), 0.3, 3.0, ((0, 16),))
    up_weight = bell_draw(key_of[8], (D, FF), D ** -0.5, 0.125, ((0, 16),))
    up_bias = bell_draw(key_of[9], (FF,), 0.3, 3.0, ((0, 16),))
    down_weight = bell_draw(key_of[10], (FF, D), FF ** -0.5, 0.0625, ((0, 16),))
    down_bias = bell_draw(key_of[11], (D,), 0.3, 3.0, ((0, 16),))
    cotangent = bell_draw(key_of[12], (SEQS, SEQ_LEN, D), 1.0, 6.0, ((0, 16), (1, 8)))
    return dict(tokens=tokens, segments=segments, ln_gain=ln_gain, ln_shift=ln_shift, qkv_weight=qkv_weight, qkv_bias=qkv_bias, proj_weight=proj_weight, proj_bias=proj_bias, up_weight=up_weight, up_bias=up_bias, down_weight=down_weight, down_bias=down_bias, cotangent=cotangent)


epsilon = 1e-05
precise = lax.Precision.HIGHEST
masked_score = -1e+30

@jax.custom_vjp
def low(v):
    return lax.optimization_barrier(v.astype(jnp.bfloat16)).astype(jnp.float32)

@jax.custom_vjp
def low_back(v):
    return v

def low_keep(v):
    return (low(v), None)

def low_pass(kept, grad):
    return (grad,)

def back_keep(v):
    return (v, None)

def back_low(kept, grad):
    return (low(grad),)
low.defvjp(low_keep, low_pass)
low_back.defvjp(back_keep, back_low)

def gelu_tanh(values):
    inner_arg = 0.7978845608028654 * (values + 0.044715 * values * values * values)
    return 0.5 * values * (1.0 + jnp.tanh(inner_arg))

def rotate_heads(fields, cosine_table, sine_table):
    half = ROT_DIMS // 2
    first_half = fields[..., :half]
    second_half = fields[..., half:ROT_DIMS]
    return jnp.concatenate([first_half * cosine_table - second_half * sine_table, second_half * cosine_table + first_half * sine_table, fields[..., ROT_DIMS:]], axis=-1)

def doc_begins(segments):
    doc_kinds = jnp.arange(DOCS, dtype=jnp.int32)
    onehot = (segments[:, :, None] == doc_kinds[None, None, :]).astype(jnp.int32)
    counts = lax.optimization_barrier(jnp.sum(onehot, axis=1))
    earlier = (doc_kinds[:, None] < doc_kinds[None, :]).astype(jnp.int32)
    firsts = lax.optimization_barrier(jnp.sum(counts[:, :, None] * earlier[None, :, :], axis=1))
    return lax.optimization_barrier(jnp.sum(onehot * firsts[:, None, :], axis=2))

def attend(packed):
    queries, key_rows, values, begins = packed
    row_index = jnp.arange(SEQ_LEN, dtype=jnp.int32)
    allowed = (row_index[None, :] <= row_index[:, None]) & (row_index[None, :] >= begins[:, None])
    scores = low_back(jnp.einsum('qhd,khd->hqk', queries, key_rows, precision=precise) * (1.0 / math.sqrt(HEAD)))
    scores = jnp.where(allowed[None], scores, masked_score)
    highest = lax.optimization_barrier(jnp.max(scores, axis=-1, keepdims=True))
    totals = lax.optimization_barrier(jnp.sum(jnp.exp(scores - highest), axis=-1, keepdims=True))
    logsum = highest + jnp.log(totals)
    weights = low(jnp.exp(scores - logsum))
    context = jnp.einsum('hqk,khd->qhd', weights, values, precision=precise)
    return (context, logsum[..., 0])

def forward(inputs, params, cosine_table, sine_table, begins):
    gain_vec, shift_vec, qkv_w, qkv_b, proj_w, proj_b, up_w, up_b, down_w, down_b = params
    average = lax.optimization_barrier(jnp.mean(inputs, axis=-1, keepdims=True))
    centered = inputs - average
    variance = lax.optimization_barrier(jnp.mean(centered * centered, axis=-1, keepdims=True))
    normed = low(centered * lax.rsqrt(variance + epsilon) * gain_vec + shift_vec)
    flat = normed.reshape(SEQS * SEQ_LEN, D)
    projected = low_back(jnp.dot(flat, qkv_w, precision=precise) + qkv_b)
    grouped = projected.reshape(SEQS, SEQ_LEN, 3, HEADS, HEAD)
    queries = low(rotate_heads(grouped[:, :, 0], cosine_table, sine_table))
    key_rows = low(rotate_heads(grouped[:, :, 1], cosine_table, sine_table))
    values = low(grouped[:, :, 2])
    context, logsum = lax.map(jax.checkpoint(attend), (queries, key_rows, values, begins))
    context = low(low_back(context)).reshape(SEQS * SEQ_LEN, D)
    attn_out = jnp.dot(context, proj_w, precision=precise) + proj_b
    hidden = low_back(jnp.dot(flat, up_w, precision=precise) + up_b)
    mlp_out = jnp.dot(low(gelu_tanh(hidden)), down_w, precision=precise) + down_b
    output = inputs.reshape(SEQS * SEQ_LEN, D) + attn_out + mlp_out
    return (output.reshape(SEQS, SEQ_LEN, D), logsum)

def reference(tokens, segments, ln_gain, ln_shift, qkv_weight, qkv_bias, proj_weight, proj_bias, up_weight, up_bias, down_weight, down_bias, cotangent):
    begins = doc_begins(segments)
    row_index = jnp.arange(SEQ_LEN, dtype=jnp.int32)
    positions = row_index[None, :] - begins
    inverse = jnp.exp(jnp.arange(ROT_DIMS // 2, dtype=jnp.float32) * (-math.log(10000.0) / (ROT_DIMS // 2)))
    angles = positions.astype(jnp.float32)[:, :, None, None] * inverse
    cosine_table = jnp.cos(angles)
    sine_table = jnp.sin(angles)
    params = tuple((argument.astype(jnp.float32) for argument in (ln_gain, ln_shift, qkv_weight, qkv_bias, proj_weight, proj_bias, up_weight, up_bias, down_weight, down_bias)))

    def wrapped(inputs, *weights):
        return forward(inputs, weights, cosine_table, sine_table, begins)
    output, pullback, logsum = jax.vjp(wrapped, tokens.astype(jnp.float32), *params, has_aux=True)
    gradients = pullback(cotangent.astype(jnp.float32))
    return (output.astype(jnp.bfloat16), gradients[0].astype(jnp.bfloat16), logsum, gradients[1], gradients[2], gradients[3], gradients[4], gradients[5], gradients[6], gradients[7], gradients[8], gradients[9], gradients[10])
```

```python
from functools import partial
import math

import jax
import jax.numpy as jnp
from jax import lax
from jax.sharding import PartitionSpec as P

HEAD = 64
ROT_DIMS = 32
DOCS = 4

epsilon = 1e-05
masked_score = -1e30
f32 = jnp.float32
bf16 = jnp.bfloat16


def gelu_tanh(values):
    inner_arg = 0.7978845608028654 * (values + 0.044715 * values * values * values)
    return 0.5 * values * (1.0 + jnp.tanh(inner_arg))


def rotate_heads(fields, cosine_table, sine_table):
    half = ROT_DIMS // 2
    first_half = fields[..., :half]
    second_half = fields[..., half:ROT_DIMS]
    return jnp.concatenate(
        [
            first_half * cosine_table - second_half * sine_table,
            second_half * cosine_table + first_half * sine_table,
            fields[..., ROT_DIMS:],
        ],
        axis=-1,
    )


def standardize(inputs):
    average = jnp.mean(inputs, axis=-1, keepdims=True)
    centered = inputs - average
    variance = jnp.mean(centered * centered, axis=-1, keepdims=True)
    return centered * lax.rsqrt(variance + epsilon)


def dot(a, b, ca, cb):
    return lax.dot_general(a, b, (((ca,), (cb,)), ((), ())), preferred_element_type=f32)


def local(
    tokens,
    segments,
    ln_gain,
    ln_shift,
    qkv_weight,
    qkv_bias,
    proj_weight,
    proj_bias,
    up_weight,
    up_bias,
    down_weight,
    down_bias,
    cotangent,
):
    rows = tokens.shape[1]
    width = tokens.shape[2]
    shard = ln_gain.shape[0]
    ring = lax.axis_size("ctx")
    shards = lax.axis_size("fsdp")
    c = lax.axis_index("ctx")
    f = lax.axis_index("fsdp")
    heads = width // HEAD
    own_heads = heads // ring
    cols = width // ring
    hidden_width = up_weight.shape[1]
    ratio = hidden_width // width
    strip = hidden_width // (shards * ring)
    seq = rows * ring

    packed = jnp.concatenate([ln_gain, ln_shift, proj_bias, down_bias, qkv_bias, up_bias])
    packed = lax.all_gather(packed, "fsdp", axis=0, tiled=False)
    gain = packed[:, :shard].reshape(width).astype(f32)
    shift = packed[:, shard : 2 * shard].reshape(width).astype(f32)
    proj_b = packed[:, 2 * shard : 3 * shard].reshape(width).astype(f32)
    down_b = packed[:, 3 * shard : 4 * shard].reshape(width).astype(f32)
    qkv_b = packed[:, 4 * shard : 7 * shard].reshape(3, ring, cols).astype(f32)
    up_b = packed[:, 7 * shard :].reshape(shards, ring, strip).astype(f32)
    qkv_b = lax.dynamic_index_in_dim(qkv_b, c, 1, False).reshape(3 * cols)
    up_b = lax.dynamic_index_in_dim(up_b, c, 1, False).reshape(shards * strip)

    own_qkv = lax.dynamic_index_in_dim(qkv_weight.reshape(shard, 3, ring, cols), c, 2, False)
    own_up = lax.dynamic_index_in_dim(up_weight.reshape(shard, shards, ring, strip), c, 2, False)
    own_down = lax.dynamic_index_in_dim(down_weight.reshape(ring, strip, width), c, 0, False)
    own_proj = jnp.where(
        (jnp.arange(cols // shard) + c * (cols // shard) == f)[:, None, None],
        proj_weight[None],
        jnp.zeros((), bf16),
    )
    qkv_w = lax.all_gather(own_qkv.reshape(shard, 3 * cols), "fsdp", axis=0, tiled=True)
    up_w = lax.all_gather(own_up.reshape(shard, shards * strip), "fsdp", axis=0, tiled=True)
    down_w = lax.all_gather(own_down, "fsdp", axis=0, tiled=True)
    proj_w = lax.psum(own_proj, "fsdp").reshape(cols, width)

    both = jnp.concatenate([tokens[0], cotangent[0]], axis=1)
    both = lax.all_gather(both, "ctx", axis=0, tiled=True)
    all_tokens, upstream = both[:, :width], both[:, width:]
    seg = lax.all_gather(segments[0], "ctx", axis=0, tiled=True)

    row_index = jnp.arange(seq, dtype=jnp.int32)
    begins = jnp.sum((seg[None, :] < seg[:, None]).astype(jnp.int32), axis=1)
    positions = row_index - begins
    inverse = jnp.exp(
        jnp.arange(ROT_DIMS // 2, dtype=f32) * (-math.log(10000.0) / (ROT_DIMS // 2))
    )
    angles = positions.astype(f32)[:, None, None] * inverse
    cosine_table = jnp.cos(angles)
    sine_table = jnp.sin(angles)

    normed = (standardize(all_tokens.astype(f32)) * gain + shift).astype(bf16)
    projected = dot(normed, qkv_w, 1, 0) + qkv_b
    hidden = dot(normed, up_w, 1, 0) + up_b
    grouped = projected.reshape(seq, 3, own_heads, HEAD)
    turner = partial(rotate_heads, cosine_table=cosine_table, sine_table=sine_table)
    queries_wide, query_pull = jax.vjp(turner, grouped[:, 0])
    key_wide, key_pull = jax.vjp(turner, grouped[:, 1])
    queries = queries_wide.astype(bf16)
    keys = key_wide.astype(bf16)
    values = grouped[:, 2].astype(bf16)
    scale = 1.0 / math.sqrt(HEAD)

    allowed = (row_index[None, :] <= row_index[:, None]) & (seg[None, :] == seg[:, None])
    scores = jnp.einsum("qhd,khd->hqk", queries, keys, preferred_element_type=f32) * scale
    scores = jnp.where(allowed[None], scores, masked_score)
    logsum = jax.nn.logsumexp(scores, axis=-1)
    probs = jnp.exp(scores - logsum[..., None])
    probs_low = probs.astype(bf16)
    context = jnp.einsum("hqk,khd->qhd", probs_low, values, preferred_element_type=f32)
    context = context.astype(bf16).reshape(seq, cols)
    active_wide, active_pull = jax.vjp(gelu_tanh, hidden)
    active = active_wide.astype(bf16)
    out_part = dot(context, proj_w, 1, 0) + dot(active, down_w, 1, 0)
    out_sum = lax.psum_scatter(out_part.astype(bf16), "ctx", scatter_dimension=0, tiled=True)
    inputs = tokens[0].astype(f32)
    block_out = (inputs + out_sum.astype(f32) + proj_b + down_b).astype(bf16)

    d_active = dot(upstream, down_w, 1, 1)
    d_context = dot(upstream, proj_w, 1, 1).astype(bf16).reshape(seq, own_heads, HEAD)
    d_hidden = active_pull(d_active)[0].astype(bf16)
    d_probs = jnp.einsum("qhd,khd->hqk", d_context, values, preferred_element_type=f32)
    delta = jnp.sum(probs * d_probs, axis=-1, keepdims=True)
    d_scores = (probs * (d_probs - delta)).astype(bf16)
    d_queries = jnp.einsum("hqk,khd->qhd", d_scores, keys, preferred_element_type=f32) * scale
    d_keys = jnp.einsum("hqk,qhd->khd", d_scores, queries, preferred_element_type=f32) * scale
    d_values = jnp.einsum("hqk,qhd->khd", probs_low, d_context, preferred_element_type=f32)
    d_projected = jnp.stack([query_pull(d_queries)[0], key_pull(d_keys)[0], d_values], axis=1)
    d_projected = d_projected.reshape(seq, 3 * cols).astype(bf16)

    d_normed = dot(d_projected, qkv_w, 1, 1) + dot(d_hidden, up_w, 1, 1)
    d_normed = lax.psum_scatter(d_normed.astype(bf16), "ctx", scatter_dimension=0, tiled=True)
    d_normed = d_normed.astype(f32)
    standard, standard_pull = jax.vjp(standardize, inputs)
    upstream_own = cotangent[0].astype(f32)
    token_grad = (upstream_own + standard_pull(d_normed * gain)[0]).astype(bf16)

    grad_down = dot(active, upstream, 0, 0).astype(bf16)
    grad_up = dot(normed, d_hidden, 0, 0).astype(bf16)
    grad_qkv = dot(normed, d_projected, 0, 0).astype(bf16)
    grad_proj = dot(context, upstream, 0, 0).astype(bf16)
    wide = jnp.concatenate([grad_qkv, grad_up], axis=1)
    wide = lax.psum_scatter(wide, "fsdp", scatter_dimension=0, tiled=True)
    grad_down = lax.psum_scatter(grad_down, "fsdp", scatter_dimension=0, tiled=True)
    grad_proj = lax.psum(grad_proj, "fsdp").reshape(cols // shard, shard, width)
    grad_proj = lax.dynamic_index_in_dim(grad_proj, f % (cols // shard), 0, False)
    grad_proj = jnp.where(c == f // (cols // shard), grad_proj, jnp.zeros((), bf16))
    proj_weight_grad = lax.psum(grad_proj, "ctx").astype(f32)
    wide = lax.all_gather(wide, "ctx", axis=0, tiled=False)
    down_weight_grad = lax.all_gather(grad_down, "ctx", axis=0, tiled=True).astype(f32)
    qkv_weight_grad = (
        jnp.transpose(wide[:, :, : 3 * cols].reshape(ring, shard, 3, cols), (1, 2, 0, 3))
        .reshape(shard, 3 * width)
        .astype(f32)
    )
    up_weight_grad = (
        jnp.transpose(wide[:, :, 3 * cols :].reshape(ring, shard, shards, strip), (1, 2, 0, 3))
        .reshape(shard, hidden_width)
        .astype(f32)
    )

    d_qkv_b = jnp.sum(d_projected.astype(f32), axis=0).reshape(3, 1, cols)
    d_up_b = jnp.sum(d_hidden.astype(f32), axis=0).reshape(shards, 1, strip)
    here = (jnp.arange(ring) == c)[None, :, None]
    d_out_b = jnp.sum(upstream_own, axis=0)
    vectors = jnp.concatenate(
        [
            jnp.sum(d_normed * standard, axis=0).reshape(shards, -1),
            jnp.sum(d_normed, axis=0).reshape(shards, -1),
            d_out_b.reshape(shards, -1),
            jnp.where(here, d_qkv_b, 0.0).reshape(shards, -1),
            jnp.where(here, d_up_b, 0.0).reshape(shards, -1),
        ],
        axis=1,
    )
    vectors = lax.psum(vectors, ("ctx", "fsdp"))
    vectors = lax.dynamic_index_in_dim(vectors, f, 0, False)
    return (
        block_out[None],
        token_grad[None],
        lax.all_to_all(
            logsum.reshape(1, own_heads, seq), "ctx", split_axis=2, concat_axis=1, tiled=True
        ),
        vectors[:shard],
        vectors[shard : 2 * shard],
        qkv_weight_grad,
        vectors[3 * shard : 6 * shard],
        proj_weight_grad,
        vectors[2 * shard : 3 * shard],
        up_weight_grad,
        vectors[6 * shard :],
        down_weight_grad,
        vectors[2 * shard : 3 * shard],
    )


def solution(mesh):
    in_specs = (
        P("fsdp", "ctx", None),
        P("fsdp", "ctx"),
        P("fsdp"),
        P("fsdp"),
        P("fsdp", None),
        P("fsdp"),
        P("fsdp", None),
        P("fsdp"),
        P("fsdp", None),
        P("fsdp"),
        P("fsdp", None),
        P("fsdp"),
        P("fsdp", "ctx", None),
    )
    out_specs = (
        P("fsdp", "ctx", None),
        P("fsdp", "ctx", None),
        P("fsdp", None, "ctx"),
        P("fsdp"),
        P("fsdp"),
        P("fsdp", None),
        P("fsdp"),
        P("fsdp", None),
        P("fsdp"),
        P("fsdp", None),
        P("fsdp"),
        P("fsdp", None),
        P("fsdp"),
    )
    return jax.shard_map(local, mesh=mesh, in_specs=in_specs, out_specs=out_specs, check_vma=False)
```

```python
from functools import partial
import math

import jax
import jax.numpy as jnp
from jax import lax
from jax.experimental import pallas as pl
from jax.experimental.pallas import tpu as pltpu
from jax.sharding import PartitionSpec as P

HEAD = 64
ROT_DIMS = 32
SEQ = 1024
WIDTH = 2048
HIDDEN = 8192
OWN_HEADS = 4
COLS = 256
UNITS = 1024

epsilon = 1e-05
masked_score = -1e30
f32 = jnp.float32
bf16 = jnp.bfloat16
MESH = pl.DeviceIdType.MESH
VM = pltpu.VMEM


def dot(a, b, ca, cb):
    return lax.dot_general(a, b, (((ca,), (cb,)), ((), ())), preferred_element_type=f32)


def place():
    c = lax.axis_index("ctx")
    f = lax.axis_index("fsdp")
    return c, f, c // 2, c % 2, f // 4, f % 4


def other_core():
    c, f, z, core, y, x = place()
    return (z * 2 + 1 - core, f)


def up1(i):
    return (i + 1) % 4


def down1(i):
    return (i + 3) % 4


def over(i):
    return (i + 2) % 4


class Copies:
    def __init__(self, send, recv):
        self.send, self.recv = send, recv
        self.started = []

    def start(self, k, src, dst, device):
        copy = pltpu.make_async_remote_copy(
            src_ref=src,
            dst_ref=dst,
            send_sem=self.send.at[k],
            recv_sem=self.recv.at[k],
            device_id=device,
            device_id_type=MESH,
        )
        copy.start()
        self.started.append(copy)

    def arrived(self, k, dst):
        pltpu.make_async_remote_copy(
            src_ref=dst,
            dst_ref=dst,
            send_sem=self.send.at[k],
            recv_sem=self.recv.at[k],
            device_id=other_core(),
            device_id_type=MESH,
        ).wait_recv()

    def sent(self):
        for copy in self.started:
            copy.wait_send()


def plane_gather(w, cuts, copies):
    c, f, z, core, y, x = place()
    r0, r1, r2, r3, r4 = cuts
    first, last = pl.ds(r0, r2 - r0), pl.ds(r2, r4 - r2)
    q0, q1, q2, q3 = (pl.ds(a, b - a) for a, b in zip(cuts[:-1], cuts[1:]))
    xu, xd, xo = up1(x), down1(x), over(x)
    yu, yd, yo = up1(y), down1(y), over(y)
    to_xu, to_xd = (c, y * 4 + xu), (c, y * 4 + xd)
    to_yu, to_yd = (c, yu * 4 + x), (c, yd * 4 + x)
    lo, hi = pl.ds(0, 2), pl.ds(2, 2)
    every = pl.ds(0, 4)

    def send(k, part, device):
        copies.start(k, w.at[part], w.at[part], device)

    def got(k, part):
        copies.arrived(k, w.at[part])

    send(0, (y, x, first), to_xu)
    send(1, (y, x, first), to_xd)
    send(2, (y, x, last), to_yu)
    send(3, (y, x, last), to_yd)
    yield
    got(0, (y, xd, first))
    send(4, (y, xd, q0), to_xu)
    got(1, (y, xu, first))
    send(5, (y, xu, q1), to_xd)
    got(2, (yd, x, last))
    send(6, (yd, x, q2), to_yu)
    got(3, (yu, x, last))
    send(7, (yu, x, q3), to_yd)
    yield
    got(4, (y, xo, q0))
    got(5, (y, xo, q1))
    send(8, (y, every, first), to_yu)
    send(9, (y, every, first), to_yd)
    got(6, (yo, x, q2))
    got(7, (yo, x, q3))
    send(10, (every, x, last), to_xu)
    send(11, (every, x, last), to_xd)
    yield
    got(8, (yd, every, first))
    send(12, (yd, lo, first), to_yu)
    got(9, (yu, every, first))
    send(13, (yu, hi, first), to_yd)
    got(10, (every, xd, last))
    send(14, (lo, xd, last), to_xu)
    got(11, (every, xu, last))
    send(15, (hi, xu, last), to_xd)
    yield
    got(12, (yo, lo, first))
    got(13, (yo, hi, first))
    got(14, (lo, xo, last))
    got(15, (hi, xo, last))
    yield


def line_gather(t, cuts, copies):
    c, f, z, core, y, x = place()
    r0, r1, r2 = cuts
    h0, h1 = pl.ds(r0, r1 - r0), pl.ds(r1, r2 - r1)
    zu, zd, zo = up1(z), down1(z), over(z)
    to_zu, to_zd, to_core = (zu * 2 + core, f), (zd * 2 + core, f), (z * 2 + 1 - core, f)
    other = 1 - core

    def send(k, part, device):
        copies.start(k, t.at[part], t.at[part], device)

    def got(k, part):
        copies.arrived(k, t.at[part])

    send(0, (z, core), to_zu)
    send(1, (z, core), to_zd)
    send(2, (z, core), to_core)
    yield
    got(0, (zd, core))
    send(3, (zd, core, h0), to_zu)
    got(1, (zu, core))
    send(4, (zu, core, h1), to_zd)
    send(5, (zd, core), to_core)
    send(6, (zu, core), to_core)
    yield
    got(3, (zo, core, h0))
    got(4, (zo, core, h1))
    send(7, (zo, core), to_core)
    yield
    got(2, (z, other))
    got(5, (zd, other))
    got(6, (zu, other))
    got(7, (zo, other))
    yield


def enter(owner_of_rows, rows_of_owner):
    c, f, z, core, y, x = place()
    barrier = pltpu.get_barrier_semaphore()
    for device in (
        (c, y * 4 + up1(x)),
        (c, y * 4 + down1(x)),
        (c, up1(y) * 4 + x),
        (c, down1(y) * 4 + x),
        (up1(z) * 2 + core, f),
        (down1(z) * 2 + core, f),
        (z * 2 + 1 - core, f),
    ):
        pl.semaphore_signal(barrier, inc=1, device_id=device, device_id_type=MESH)
    owner = c * 2 + f // 8
    if owner_of_rows:

        @pl.when(owner != f)
        def _():
            pl.semaphore_signal(barrier, inc=1, device_id=(c, owner), device_id_type=MESH)

    if rows_of_owner:
        for j in range(8):
            target = (f % 2) * 8 + j

            @pl.when((f // 2 == c) & (target != f))
            def _():
                pl.semaphore_signal(barrier, inc=1, device_id=(c, target), device_id_type=MESH)

    count = 7
    if owner_of_rows:
        count = count + jnp.where(f // 2 == c, jnp.where(f // 8 == f % 2, 7, 8), 0)
    if rows_of_owner:
        count = count + jnp.where(owner != f, 1, 0)
    pl.semaphore_wait(barrier, count)


CUTS1 = (0, 32, 64, 96, 144)
CUTS2 = (0, 16, 32, 48, 80)
CUTS3 = (0, 32, 64, 96, 128)


def turn(fields, cos, low_sin, high_sin):
    return (
        fields * cos + pltpu.roll(fields, 112, 1) * low_sin + pltpu.roll(fields, 16, 1) * high_sin
    )


def turn_back(grads, cos, low_sin, high_sin):
    return (
        grads * cos + pltpu.roll(grads * low_sin, 16, 1) + pltpu.roll(grads * high_sin, 112, 1)
    )


def halves_packed(a, b, odd, lane):
    moved_a, moved_b = pltpu.roll(a, 64, 1), pltpu.roll(b, 64, 1)
    return jnp.where(lane < 64, jnp.where(odd, moved_a, a), jnp.where(odd, b, moved_b))


def first_kernel(
    tokens,
    cotangent,
    qkv_weight,
    proj_weight,
    up_weight,
    down_weight,
    seg,
    vec,
    cos0,
    sin0,
    inv,
    n_out,
    w1_out,
    w2_out,
    w3_out,
    u_out,
    dproj_out,
    ctx_out,
    act_out,
    dhid_out,
    lse_out,
    w1,
    w2,
    w3,
    t,
    u,
    n,
    strips,
    vecs,
    tab,
    begin_col,
    q,
    k,
    v,
    dctx,
    dq,
    dk,
    dv,
    dproj,
    ctx_heads,
    ctx,
    act,
    dhid,
    lse,
    sem1,
    sem2,
    sem3,
    sem_t,
    sem_u,
    sem_p,
    sem_l,
    sem_o,
):
    c, f, z, core, y, x = place()
    lane = lax.broadcasted_iota(jnp.int32, (1, 128), 1)

    loads = [
        pltpu.make_async_copy(tokens, t.at[z, core, pl.ds(0, 128)], sem_l.at[0]),
        pltpu.make_async_copy(cotangent, u.at[z, core], sem_l.at[1]),
        pltpu.make_async_copy(
            down_weight.at[pl.ds(pl.multiple_of(c * 64, 64), 64)],
            w2.at[y, x, pl.ds(0, 64)],
            sem_l.at[2],
        ),
    ]
    for i in range(3):
        loads.append(
            pltpu.make_async_copy(
                qkv_weight.at[:, pl.ds(pl.multiple_of(i * WIDTH + c * COLS, 128), COLS)],
                w1.at[y, x, pl.ds(0, 128), pl.ds(i * COLS, COLS)],
                sem_l.at[3 + i],
            )
        )
    for copy in loads:
        copy.start()
    for i in range(16):
        pltpu.make_async_copy(
            up_weight.at[:, pl.ds(pl.multiple_of(i * 512 + (c // 2) * 128, 128), 128)],
            strips.at[i],
            sem_l.at[6],
        ).start()
    w1[y, x, 128:144, 0:128] = vec[...]
    w1[y, x, 128:144, 128:768] = jnp.zeros((16, 640), bf16)
    seg_rows = jnp.broadcast_to(seg[...].astype(f32), (16, 128)).astype(bf16)
    t[z, core, 128:144, 0:128] = seg_rows
    t[z, core, 128:144, 128:WIDTH] = jnp.zeros((16, WIDTH - 128), bf16)

    enter(True, False)

    copies1 = Copies(sem1.at[0], sem1.at[1])
    copies2 = Copies(sem2.at[0], sem2.at[1])
    copies3 = Copies(sem3.at[0], sem3.at[1])
    copies_t = Copies(sem_t.at[0], sem_t.at[1])
    copies_u = Copies(sem_u.at[0], sem_u.at[1])
    gather1 = plane_gather(w1, CUTS1, copies1)
    gather2 = plane_gather(w2, CUTS2, copies2)
    gather3 = plane_gather(w3, CUTS3, copies3)
    gather_t = line_gather(t, (0, 64, 144), copies_t)
    gather_u = line_gather(u, (0, 64, 128), copies_u)

    for i in (3, 4, 5):
        loads[i].wait()
    next(gather1)
    loads[0].wait()
    next(gather_t)

    owner = c * 2 + f // 8
    own_rows = f // 2 == c
    for j in range(8):
        target = (f % 2) * 8 + j
        rows = proj_weight.at[pl.ds(16 * j, 16)]

        @pl.when(own_rows & (target != f))
        def _():
            pltpu.make_async_remote_copy(
                src_ref=rows,
                dst_ref=w2.at[target // 4, target % 4, pl.ds(64, 16)],
                send_sem=sem_p.at[0, j],
                recv_sem=sem_p.at[1, 0],
                device_id=(c, target),
                device_id_type=MESH,
            ).start()

        @pl.when(own_rows & (target == f))
        def _():
            local = pltpu.make_async_copy(
                rows, w2.at[target // 4, target % 4, pl.ds(64, 16)], sem_p.at[1, 1]
            )
            local.start()
            local.wait()

    pltpu.make_async_copy(strips, strips, sem_l.at[6]).wait()
    odd = core == 1
    for m in range(8):
        packed = halves_packed(
            strips[2 * m].astype(f32), strips[2 * m + 1].astype(f32), odd, lane
        )
        w3[y, x, :, 128 * m : 128 * m + 128] = packed.astype(bf16)

    next(gather1)
    loads[2].wait()

    @pl.when(owner != f)
    def _():
        own = w2.at[y, x, pl.ds(64, 16)]
        pltpu.make_async_remote_copy(
            src_ref=own,
            dst_ref=own,
            send_sem=sem_p.at[0, 0],
            recv_sem=sem_p.at[1, 0],
            device_id=other_core(),
            device_id_type=MESH,
        ).wait_recv()

    next(gather_t)
    loads[1].wait()
    next(gather_u)
    next(gather1)
    next(gather2)
    next(gather_t)
    next(gather1)
    next(gather2)
    next(gather_t)
    next(gather1)

    outs = []

    def put(src, dst):
        copy = pltpu.make_async_copy(src, dst, sem_o.at[len(outs)])
        copy.start()
        outs.append(copy)

    put(w1, w1_out)

    vecs[...] = w1[:, :, 128:144, 0:128].reshape(16, 16, 128).astype(f32)
    gain = jnp.concatenate([vecs[i, 0:1, :] for i in range(16)], axis=1)
    shift = jnp.concatenate([vecs[i, 1:2, :] for i in range(16)], axis=1)

    def bias_rows(which):
        parts = []
        for i in range(2):
            row = which * 16 + c * 2 + i
            parts.append(vecs[row // 3, pl.ds(4 + row % 3, 1), :])
        return jnp.concatenate(parts, axis=1)

    qkv_bias = jnp.concatenate([bias_rows(i) for i in range(3)], axis=1)
    up_parts = []
    for m in range(8):
        a = vecs[2 * m, pl.ds(7 + c // 2, 1), :]
        b = vecs[2 * m + 1, pl.ds(7 + c // 2, 1), :]
        up_parts.append(halves_packed(a, b, odd, lane))
    up_bias = jnp.concatenate(up_parts, axis=1)

    seg_all = jnp.concatenate(
        [t[b // 2, b % 2, 128:144, 0:128][0:1].astype(f32) for b in range(8)], axis=0
    )
    seg_cols = jnp.transpose(seg_all)
    firsts = [
        jnp.sum((seg_all < float(d)).astype(f32), keepdims=True) for d in range(1, 4)
    ]
    angles = [first * inv[...] for first in firsts]
    first_cos = [jnp.cos(angle) for angle in angles]
    first_sin = [jnp.sin(angle) for angle in angles]
    in_head = lane % 64
    for b in range(8):
        rows = pl.ds(b * 128, 128)
        own = seg_cols[:, b : b + 1]
        cb, sb = jnp.ones((128, 128), f32), jnp.zeros((128, 128), f32)
        first_position = jnp.zeros((128, 1), f32)
        for d in range(1, 4):
            here = own == float(d)
            cb = jnp.where(here, first_cos[d - 1], cb)
            sb = jnp.where(here, first_sin[d - 1], sb)
            first_position = jnp.where(here, firsts[d - 1], first_position)
        base_cos, base_sin = cos0[rows, :], sin0[rows, :]
        cos = base_cos * cb + base_sin * sb
        sin = base_sin * cb - base_cos * sb
        tab[0, rows, :] = cos
        tab[1, rows, :] = jnp.where(in_head < 16, -sin, 0.0)
        tab[2, rows, :] = jnp.where((in_head >= 16) & (in_head < 32), sin, 0.0)
        begin_col[rows, :] = first_position

    def norm_rows(i, carry):
        b, part = i // 4, i % 4
        src = pl.ds(pl.multiple_of(part * 32, 32), 32)
        values = t[b // 2, b % 2, src, :].astype(f32)
        average = jnp.mean(values, axis=-1, keepdims=True)
        centered = values - average
        variance = jnp.mean(centered * centered, axis=-1, keepdims=True)
        standard = centered * lax.rsqrt(variance + epsilon)
        n[pl.ds(pl.multiple_of(i * 32, 32), 32), :] = (standard * gain + shift).astype(bf16)
        return carry

    lax.fori_loop(0, 32, norm_rows, 0)
    put(n, n_out)
    next(gather2)
    next(gather3)
    next(gather_u)

    def project(m, carry):
        rows = pl.ds(pl.multiple_of(m * 256, 256), 256)
        left = n[rows, :]
        tables = [tab[i, rows, :] for i in range(3)]
        for which in range(3):
            columns = pl.ds(which * COLS, COLS)
            right = w1[:, :, pl.ds(0, 128), columns].reshape(WIDTH, COLS)
            fields = dot(left, right, 1, 0) + qkv_bias[:, which * COLS : (which + 1) * COLS]
            for pair in range(2):
                both = fields[:, pair * 128 : pair * 128 + 128]
                if which < 2:
                    both = turn(both, *tables)
                if which == 0:
                    both = both * 0.125
                both = both.astype(bf16)
                target = (q, k, v)[which]
                target[2 * pair, rows, :] = both[:, :64]
                target[2 * pair + 1, rows, :] = both[:, 64:]
        return carry

    lax.fori_loop(0, 4, project, 0)
    next(gather2)
    next(gather3)
    next(gather_u)
    next(gather2)
    next(gather_u)
    put(w2, w2_out)
    put(u, u_out)

    def context_grad(m, carry):
        rows = pl.ds(pl.multiple_of(m * 256, 256), 256)
        left = u[m].reshape(256, WIDTH)
        right = w2[:, :, pl.ds(64, 16), :].reshape(COLS, WIDTH)
        grads = dot(left, right, 1, 1).astype(bf16)
        for head in range(4):
            dctx[head, rows, :] = grads[:, head * 64 : head * 64 + 64]
        return carry

    lax.fori_loop(0, 4, context_grad, 0)
    next(gather3)

    for block in (3, 2, 1, 0):
        reach = (block + 1) * 256
        rows = pl.ds(block * 256, 256)
        keys = pl.ds(0, reach)
        begins = begin_col[rows, :]
        key_index = lax.broadcasted_iota(jnp.int32, (1, reach), 1).astype(f32)
        row_index = (
            lax.broadcasted_iota(jnp.int32, (256, 1), 0) + block * 256
        ).astype(f32)

        def attend(head, carry, block=block, rows=rows, keys=keys, begins=begins):
            qh, kh, vh, dh = q[head, rows, :], k[head, keys, :], v[head, keys, :], dctx[head, rows, :]
            scores = dot(qh, kh, 1, 1)
            allowed = (key_index >= begins) & (key_index <= row_index)
            scores = jnp.where(allowed, scores, masked_score)
            highest = jnp.max(scores, axis=1, keepdims=True)
            weights = jnp.exp(scores - highest)
            total = jnp.sum(weights, axis=1, keepdims=True)
            probs = weights * (1.0 / total)
            log_sum = jnp.broadcast_to(highest + jnp.log(total), (256, 128))
            lse[pl.ds(head, 1), rows] = jnp.transpose(log_sum)[0:1, :]
            probs_low = probs.astype(bf16)
            ctx_heads[head, rows, :] = dot(probs_low, vh, 1, 0).astype(bf16)
            d_probs = dot(dh, vh, 1, 1)
            delta = jnp.sum(probs * d_probs, axis=1, keepdims=True)
            d_scores = (probs * (d_probs - delta)).astype(bf16)
            dq[head, rows, :] = dot(d_scores, kh, 1, 0)
            d_keys = dot(d_scores, qh, 0, 0)
            d_values = dot(probs_low, dh, 0, 0)
            if block == 3:
                dk[head, keys, :] = d_keys
                dv[head, keys, :] = d_values
            else:
                dk[head, keys, :] += d_keys
                dv[head, keys, :] += d_values
            return carry

        lax.fori_loop(0, 4, attend, 0)
        if block >= 2:
            next(gather3)
    put(w3, w3_out)

    def join(m, carry):
        rows = pl.ds(pl.multiple_of(m * 256, 256), 256)
        tables = [tab[i, rows, :] for i in range(3)]
        for pair in range(2):
            lanes = pl.ds(pair * 128, 128)
            ctx[rows, lanes] = jnp.concatenate(
                [ctx_heads[2 * pair, rows, :], ctx_heads[2 * pair + 1, rows, :]], axis=1
            )
            for which, source in ((0, dq), (1, dk), (2, dv)):
                both = jnp.concatenate(
                    [source[2 * pair, rows, :], source[2 * pair + 1, rows, :]], axis=1
                )
                if which == 0:
                    both = both * 0.125
                if which < 2:
                    both = turn_back(both, *tables)
                dproj[rows, pl.ds(which * COLS + pair * 128, 128)] = both.astype(bf16)
        return carry

    lax.fori_loop(0, 4, join, 0)
    put(dproj, dproj_out)
    put(ctx, ctx_out)
    put(lse, lse_out)

    for i in range(4):
        columns = pl.ds(i * 256, 256)
        bias = up_bias[:, i * 256 : (i + 1) * 256]

        def feed(m, carry, columns=columns, bias=bias, i=i):
            rows = pl.ds(pl.multiple_of(m * 256, 256), 256)
            right = w3[:, :, :, columns].reshape(WIDTH, 256)
            h = dot(n[rows, :], right, 1, 0) + bias
            d_act = dot(
                u[m].reshape(256, WIDTH), w2[i, :, pl.ds(0, 64), :].reshape(256, WIDTH), 1, 1
            )
            square = h * h
            tanh = jnp.tanh(0.7978845608028654 * (h + 0.044715 * square * h))
            half = 0.5 * (1.0 + tanh)
            slope = half + 0.5 * h * (1.0 - tanh * tanh) * (
                0.7978845608028654 * (1.0 + 3.0 * 0.044715 * square)
            )
            act[rows, columns] = (h * half).astype(bf16)
            dhid[rows, columns] = (d_act * slope).astype(bf16)
            return carry

        lax.fori_loop(0, 4, feed, 0)
    put(act, act_out)
    put(dhid, dhid_out)

    for copies in (copies1, copies2, copies3, copies_t, copies_u):
        copies.sent()
    for j in range(8):
        target = (f % 2) * 8 + j

        @pl.when(own_rows & (target != f))
        def _():
            pltpu.make_async_remote_copy(
                src_ref=proj_weight.at[pl.ds(16 * j, 16)],
                dst_ref=w2.at[target // 4, target % 4, pl.ds(64, 16)],
                send_sem=sem_p.at[0, j],
                recv_sem=sem_p.at[1, 0],
                device_id=(c, target),
                device_id_type=MESH,
            ).wait_send()

    for copy in outs:
        copy.wait()


def first_call(tokens, cotangent, qkv_weight, proj_weight, up_weight, down_weight, seg, vec):
    lanes = jnp.arange(128) % 64
    inverse = jnp.exp((lanes % 16).astype(f32) * (-math.log(10000.0) / (ROT_DIMS // 2)))
    inverse = jnp.where(lanes < ROT_DIMS, inverse, 0.0)[None, :]
    base = jnp.arange(SEQ, dtype=f32)[:, None] * inverse
    shapes = dict(
        n=((SEQ, WIDTH), bf16),
        w1=((4, 4, 144, 768), bf16),
        w2=((4, 4, 80, WIDTH), bf16),
        w3=((4, 4, 128, UNITS), bf16),
        u=((4, 2, 128, WIDTH), bf16),
        dproj=((SEQ, 768), bf16),
        ctx=((SEQ, COLS), bf16),
        act=((SEQ, UNITS), bf16),
        dhid=((SEQ, UNITS), bf16),
        lse=((8, SEQ), f32),
    )
    anyspace = pl.BlockSpec(memory_space=pl.ANY)
    vmem = pl.BlockSpec(memory_space=VM)
    return pl.pallas_call(
        first_kernel,
        out_shape=[jax.ShapeDtypeStruct(*s) for s in shapes.values()],
        in_specs=[anyspace] * 6 + [vmem] * 5,
        out_specs=[anyspace] * len(shapes),
        scratch_shapes=[
            VM(*shapes["w1"]),
            VM(*shapes["w2"]),
            VM(*shapes["w3"]),
            VM((4, 2, 144, WIDTH), bf16),
            VM(*shapes["u"]),
            VM(*shapes["n"]),
            VM((16, 128, 128), bf16),
            VM((16, 16, 128), f32),
            VM((3, SEQ, 128), f32),
            VM((SEQ, 1), f32),
            VM((4, SEQ, 64), bf16),
            VM((4, SEQ, 64), bf16),
            VM((4, SEQ, 64), bf16),
            VM((4, SEQ, 64), bf16),
            VM((4, SEQ, 64), f32),
            VM((4, SEQ, 64), f32),
            VM((4, SEQ, 64), f32),
            VM(*shapes["dproj"]),
            VM((4, SEQ, 64), bf16),
            VM(*shapes["ctx"]),
            VM(*shapes["act"]),
            VM(*shapes["dhid"]),
            VM(*shapes["lse"]),
            pltpu.SemaphoreType.DMA((2, 16)),
            pltpu.SemaphoreType.DMA((2, 16)),
            pltpu.SemaphoreType.DMA((2, 16)),
            pltpu.SemaphoreType.DMA((2, 8)),
            pltpu.SemaphoreType.DMA((2, 8)),
            pltpu.SemaphoreType.DMA((2, 8)),
            pltpu.SemaphoreType.DMA((7,)),
            pltpu.SemaphoreType.DMA((10,)),
        ],
        compiler_params=pltpu.CompilerParams(
            collective_id=1, has_side_effects=True, vmem_limit_bytes=60 * 1024 * 1024
        ),
        cost_estimate=pl.CostEstimate(
            flops=25 * 10**9, bytes_accessed=40 * 10**6, transcendentals=4 * 10**6
        ),
        name="first",
    )(
        tokens, cotangent, qkv_weight, proj_weight, up_weight, down_weight, seg, vec,
        jnp.cos(base), jnp.sin(base), inverse,
    )


def standardize(inputs):
    average = jnp.mean(inputs, axis=-1, keepdims=True)
    centered = inputs - average
    variance = jnp.mean(centered * centered, axis=-1, keepdims=True)
    return centered * lax.rsqrt(variance + epsilon)


def local(
    tokens,
    segments,
    ln_gain,
    ln_shift,
    qkv_weight,
    qkv_bias,
    proj_weight,
    proj_bias,
    up_weight,
    up_bias,
    down_weight,
    down_bias,
    cotangent,
):
    c, f, z, core, y, x = place()
    width, cols, shard, ring, shards, strip = WIDTH, COLS, 128, 8, 16, 64
    hidden_width = HIDDEN
    packed = jnp.concatenate([ln_gain, ln_shift, proj_bias, down_bias, qkv_bias, up_bias])
    vec = jnp.pad(packed.reshape(11, 128), ((0, 5), (0, 0)))
    normed, w1, w2, w3, u, d_projected, context, active, d_hidden, lse = first_call(
        tokens[0], cotangent[0], qkv_weight, proj_weight, up_weight, down_weight, segments, vec
    )
    vecs = w1[:, :, 128:, :128].reshape(16, 16, 128)
    gain = vecs[:, 0].reshape(width).astype(f32)
    proj_b = vecs[:, 2].reshape(width).astype(f32)
    down_b = vecs[:, 3].reshape(width).astype(f32)
    qkv_w = w1[:, :, :128].reshape(width, 3 * cols)
    up_w = w3.reshape(width, 1024)
    down_w = w2[:, :, :64].reshape(1024, width)
    proj_w = w2[:, :, 64:].reshape(cols, width)
    upstream = u.reshape(1024, width)
    logsum = lse[:4]
    seq = 1024
    inputs = tokens[0].astype(f32)
    out_part = dot(context, proj_w, 1, 0) + dot(active, down_w, 1, 0)
    out_sum = lax.psum_scatter(out_part.astype(bf16), "ctx", scatter_dimension=0, tiled=True)
    block_out = (inputs + out_sum.astype(f32) + proj_b + down_b).astype(bf16)
    d_normed = dot(d_projected, qkv_w, 1, 1) + dot(d_hidden, up_w, 1, 1)
    d_normed = lax.psum_scatter(d_normed.astype(bf16), "ctx", scatter_dimension=0, tiled=True)
    d_normed = d_normed.astype(f32)
    standard, standard_pull = jax.vjp(standardize, inputs)
    upstream_own = cotangent[0].astype(f32)
    token_grad = (upstream_own + standard_pull(d_normed * gain)[0]).astype(bf16)

    grad_down = dot(active, upstream, 0, 0).astype(bf16)
    grad_up = dot(normed, d_hidden, 0, 0).astype(bf16)
    grad_qkv = dot(normed, d_projected, 0, 0).astype(bf16)
    grad_proj = dot(context, upstream, 0, 0).astype(bf16)
    wide = jnp.concatenate([grad_qkv, grad_up], axis=1)
    wide = lax.psum_scatter(wide, "fsdp", scatter_dimension=0, tiled=True)
    grad_down = lax.psum_scatter(grad_down, "fsdp", scatter_dimension=0, tiled=True)
    grad_proj = lax.psum(grad_proj, "fsdp").reshape(cols // shard, shard, width)
    grad_proj = lax.dynamic_index_in_dim(grad_proj, f % (cols // shard), 0, False)
    grad_proj = jnp.where(c == f // (cols // shard), grad_proj, jnp.zeros((), bf16))
    proj_weight_grad = lax.psum(grad_proj, "ctx").astype(f32)
    wide = lax.all_gather(wide, "ctx", axis=0, tiled=False)
    down_weight_grad = lax.all_gather(grad_down, "ctx", axis=0, tiled=True).astype(f32)
    qkv_weight_grad = (
        jnp.transpose(wide[:, :, : 3 * cols].reshape(ring, shard, 3, cols), (1, 2, 0, 3))
        .reshape(shard, 3 * width)
        .astype(f32)
    )
    up_weight_grad = (
        jnp.transpose(wide[:, :, 3 * cols :].reshape(ring, shard, shards, strip), (1, 2, 0, 3))
        .reshape(shard, hidden_width)
        .astype(f32)
    )

    d_qkv_b = jnp.sum(d_projected.astype(f32), axis=0).reshape(3, 1, cols)
    d_up_b = jnp.sum(d_hidden.astype(f32), axis=0).reshape(shards, 1, strip)
    here = (jnp.arange(ring) == c)[None, :, None]
    d_out_b = jnp.sum(upstream_own, axis=0)
    vectors = jnp.concatenate(
        [
            jnp.sum(d_normed * standard, axis=0).reshape(shards, -1),
            jnp.sum(d_normed, axis=0).reshape(shards, -1),
            d_out_b.reshape(shards, -1),
            jnp.where(here, d_qkv_b, 0.0).reshape(shards, -1),
            jnp.where(here, d_up_b, 0.0).reshape(shards, -1),
        ],
        axis=1,
    )
    vectors = lax.psum(vectors, ("ctx", "fsdp"))
    vectors = lax.dynamic_index_in_dim(vectors, f, 0, False)
    return (
        block_out[None],
        token_grad[None],
        lax.all_to_all(
            logsum.reshape(1, 4, seq), "ctx", split_axis=2, concat_axis=1, tiled=True
        ),
        vectors[:shard],
        vectors[shard : 2 * shard],
        qkv_weight_grad,
        vectors[3 * shard : 6 * shard],
        proj_weight_grad,
        vectors[2 * shard : 3 * shard],
        up_weight_grad,
        vectors[6 * shard :],
        down_weight_grad,
        vectors[2 * shard : 3 * shard],
    )


def solution(mesh):
    in_specs = (
        P("fsdp", "ctx", None),
        P("fsdp", "ctx"),
        P("fsdp"),
        P("fsdp"),
        P("fsdp", None),
        P("fsdp"),
        P("fsdp", None),
        P("fsdp"),
        P("fsdp", None),
        P("fsdp"),
        P("fsdp", None),
        P("fsdp"),
        P("fsdp", "ctx", None),
    )
    out_specs = (
        P("fsdp", "ctx", None),
        P("fsdp", "ctx", None),
        P("fsdp", None, "ctx"),
        P("fsdp"),
        P("fsdp"),
        P("fsdp", None),
        P("fsdp"),
        P("fsdp", None),
        P("fsdp"),
        P("fsdp", None),
        P("fsdp"),
        P("fsdp", None),
        P("fsdp"),
    )
    return jax.shard_map(local, mesh=mesh, in_specs=in_specs, out_specs=out_specs, check_vma=False)
```

```python
from functools import partial
import math

import jax
import jax.numpy as jnp
from jax import lax
from jax.experimental import pallas as pl
from jax.experimental.pallas import tpu as pltpu
from jax.sharding import PartitionSpec as P

HEAD = 64
ROT_DIMS = 32
SEQ = 1024
WIDTH = 2048
HIDDEN = 8192
OWN_HEADS = 4
COLS = 256
UNITS = 1024

epsilon = 1e-05
masked_score = -1e30
f32 = jnp.float32
bf16 = jnp.bfloat16
MESH = pl.DeviceIdType.MESH
VM = pltpu.VMEM


def dot(a, b, ca, cb):
    return lax.dot_general(a, b, (((ca,), (cb,)), ((), ())), preferred_element_type=f32)


def place():
    c = lax.axis_index("ctx")
    f = lax.axis_index("fsdp")
    return c, f, c // 2, c % 2, f // 4, f % 4


def other_core():
    c, f, z, core, y, x = place()
    return (z * 2 + 1 - core, f)


def up1(i):
    return (i + 1) % 4


def down1(i):
    return (i + 3) % 4


def over(i):
    return (i + 2) % 4


class Copies:
    def __init__(self, send, recv):
        self.send, self.recv = send, recv
        self.started = []

    def start(self, k, src, dst, device):
        copy = pltpu.make_async_remote_copy(
            src_ref=src,
            dst_ref=dst,
            send_sem=self.send.at[k],
            recv_sem=self.recv.at[k],
            device_id=device,
            device_id_type=MESH,
        )
        copy.start()
        self.started.append(copy)

    def arrived(self, k, dst):
        pltpu.make_async_remote_copy(
            src_ref=dst,
            dst_ref=dst,
            send_sem=self.send.at[k],
            recv_sem=self.recv.at[k],
            device_id=other_core(),
            device_id_type=MESH,
        ).wait_recv()

    def sent(self):
        for copy in self.started:
            copy.wait_send()


def plane_gather(w, cuts, copies):
    c, f, z, core, y, x = place()
    r0, r1, r2, r3, r4 = cuts
    first, last = pl.ds(r0, r2 - r0), pl.ds(r2, r4 - r2)
    q0, q1, q2, q3 = (pl.ds(a, b - a) for a, b in zip(cuts[:-1], cuts[1:]))
    xu, xd, xo = up1(x), down1(x), over(x)
    yu, yd, yo = up1(y), down1(y), over(y)
    to_xu, to_xd = (c, y * 4 + xu), (c, y * 4 + xd)
    to_yu, to_yd = (c, yu * 4 + x), (c, yd * 4 + x)
    lo, hi = pl.ds(0, 2), pl.ds(2, 2)
    every = pl.ds(0, 4)

    def send(k, part, device):
        copies.start(k, w.at[part], w.at[part], device)

    def got(k, part):
        copies.arrived(k, w.at[part])

    send(0, (y, x, first), to_xu)
    send(1, (y, x, first), to_xd)
    send(2, (y, x, last), to_yu)
    send(3, (y, x, last), to_yd)
    yield
    got(0, (y, xd, first))
    send(4, (y, xd, q0), to_xu)
    got(1, (y, xu, first))
    send(5, (y, xu, q1), to_xd)
    got(2, (yd, x, last))
    send(6, (yd, x, q2), to_yu)
    got(3, (yu, x, last))
    send(7, (yu, x, q3), to_yd)
    yield
    got(4, (y, xo, q0))
    got(5, (y, xo, q1))
    send(8, (y, every, first), to_yu)
    send(9, (y, every, first), to_yd)
    got(6, (yo, x, q2))
    got(7, (yo, x, q3))
    send(10, (every, x, last), to_xu)
    send(11, (every, x, last), to_xd)
    yield
    got(8, (yd, every, first))
    send(12, (yd, lo, first), to_yu)
    got(9, (yu, every, first))
    send(13, (yu, hi, first), to_yd)
    got(10, (every, xd, last))
    send(14, (lo, xd, last), to_xu)
    got(11, (every, xu, last))
    send(15, (hi, xu, last), to_xd)
    yield
    got(12, (yo, lo, first))
    got(13, (yo, hi, first))
    got(14, (lo, xo, last))
    got(15, (hi, xo, last))
    yield


def line_gather(t, cuts, copies, own=None):
    c, f, z, core, y, x = place()
    r0, r1, r2 = cuts
    h0, h1 = pl.ds(r0, r1 - r0), pl.ds(r1, r2 - r1)
    zu, zd, zo = up1(z), down1(z), over(z)
    to_zu, to_zd, to_core = (zu * 2 + core, f), (zd * 2 + core, f), (z * 2 + 1 - core, f)
    other = 1 - core

    def send(k, part, device):
        copies.start(k, t.at[part], t.at[part], device)

    def got(k, part):
        copies.arrived(k, t.at[part])

    mine = t.at[z, core]
    own = mine if own is None else own
    copies.start(0, own, mine, to_zu)
    copies.start(1, own, mine, to_zd)
    copies.start(2, own, mine, to_core)
    yield
    got(0, (zd, core))
    send(3, (zd, core, h0), to_zu)
    got(1, (zu, core))
    send(4, (zu, core, h1), to_zd)
    send(5, (zd, core), to_core)
    send(6, (zu, core), to_core)
    yield
    got(3, (zo, core, h0))
    got(4, (zo, core, h1))
    send(7, (zo, core), to_core)
    yield
    got(2, (z, other))
    got(5, (zd, other))
    got(6, (zu, other))
    got(7, (zo, other))
    yield


def enter(owner_of_rows, rows_of_owner):
    c, f, z, core, y, x = place()
    barrier = pltpu.get_barrier_semaphore()
    for device in (
        (c, y * 4 + up1(x)),
        (c, y * 4 + down1(x)),
        (c, up1(y) * 4 + x),
        (c, down1(y) * 4 + x),
        (up1(z) * 2 + core, f),
        (down1(z) * 2 + core, f),
        (z * 2 + 1 - core, f),
    ):
        pl.semaphore_signal(barrier, inc=1, device_id=device, device_id_type=MESH)
    owner = c * 2 + f // 8
    if owner_of_rows:

        @pl.when(owner != f)
        def _():
            pl.semaphore_signal(barrier, inc=1, device_id=(c, owner), device_id_type=MESH)

    if rows_of_owner:
        for j in range(8):
            target = (f % 2) * 8 + j

            @pl.when((f // 2 == c) & (target != f))
            def _():
                pl.semaphore_signal(barrier, inc=1, device_id=(c, target), device_id_type=MESH)

    count = 7
    if owner_of_rows:
        count = count + jnp.where(f // 2 == c, jnp.where(f // 8 == f % 2, 7, 8), 0)
    if rows_of_owner:
        count = count + jnp.where(owner != f, 1, 0)
    pl.semaphore_wait(barrier, count)


CUTS1 = (0, 32, 64, 96, 144)
CUTS2 = (0, 16, 32, 48, 80)
CUTS3 = (0, 32, 64, 96, 128)


def turn(fields, cos, low_sin, high_sin):
    return (
        fields * cos + pltpu.roll(fields, 112, 1) * low_sin + pltpu.roll(fields, 16, 1) * high_sin
    )


def turn_back(grads, cos, low_sin, high_sin):
    return (
        grads * cos + pltpu.roll(grads * low_sin, 16, 1) + pltpu.roll(grads * high_sin, 112, 1)
    )


def halves_packed(a, b, odd, lane):
    moved_a, moved_b = pltpu.roll(a, 64, 1), pltpu.roll(b, 64, 1)
    return jnp.where(lane < 64, jnp.where(odd, moved_a, a), jnp.where(odd, b, moved_b))


def first_kernel(
    tokens,
    cotangent,
    qkv_weight,
    proj_weight,
    up_weight,
    down_weight,
    seg,
    vec,
    cos0,
    sin0,
    inv,
    n_out,
    w1_out,
    w2_out,
    w3_out,
    u_out,
    dproj_out,
    ctx_out,
    act_out,
    dhid_out,
    lse_out,
    w1,
    w2,
    w3,
    t,
    u,
    n,
    strips,
    vecs,
    tab,
    begin_col,
    q,
    k,
    v,
    dctx,
    dq,
    dk,
    dv,
    dproj,
    ctx_heads,
    ctx,
    act,
    dhid,
    lse,
    sem1,
    sem2,
    sem3,
    sem_t,
    sem_u,
    sem_p,
    sem_l,
    sem_o,
):
    c, f, z, core, y, x = place()
    lane = lax.broadcasted_iota(jnp.int32, (1, 128), 1)

    loads = [
        pltpu.make_async_copy(tokens, t.at[z, core, pl.ds(0, 128)], sem_l.at[0]),
        pltpu.make_async_copy(cotangent, u.at[z, core], sem_l.at[1]),
        pltpu.make_async_copy(
            down_weight.at[pl.ds(pl.multiple_of(c * 64, 64), 64)],
            w2.at[y, x, pl.ds(0, 64)],
            sem_l.at[2],
        ),
    ]
    for i in range(3):
        loads.append(
            pltpu.make_async_copy(
                qkv_weight.at[:, pl.ds(pl.multiple_of(i * WIDTH + c * COLS, 128), COLS)],
                w1.at[y, x, pl.ds(0, 128), pl.ds(i * COLS, COLS)],
                sem_l.at[3 + i],
            )
        )
    for copy in loads:
        copy.start()
    for i in range(16):
        pltpu.make_async_copy(
            up_weight.at[:, pl.ds(pl.multiple_of(i * 512 + (c // 2) * 128, 128), 128)],
            strips.at[i],
            sem_l.at[6],
        ).start()
    w1[y, x, 128:144, 0:128] = vec[...]
    w1[y, x, 128:144, 128:768] = jnp.zeros((16, 640), bf16)
    seg_rows = jnp.broadcast_to(seg[...].astype(f32), (16, 128)).astype(bf16)
    t[z, core, 128:144, 0:128] = seg_rows
    t[z, core, 128:144, 128:WIDTH] = jnp.zeros((16, WIDTH - 128), bf16)

    enter(True, False)

    copies1 = Copies(sem1.at[0], sem1.at[1])
    copies2 = Copies(sem2.at[0], sem2.at[1])
    copies3 = Copies(sem3.at[0], sem3.at[1])
    copies_t = Copies(sem_t.at[0], sem_t.at[1])
    copies_u = Copies(sem_u.at[0], sem_u.at[1])
    gather1 = plane_gather(w1, CUTS1, copies1)
    gather2 = plane_gather(w2, CUTS2, copies2)
    gather3 = plane_gather(w3, CUTS3, copies3)
    gather_t = line_gather(t, (0, 64, 144), copies_t)
    gather_u = line_gather(u, (0, 64, 128), copies_u)

    for i in (3, 4, 5):
        loads[i].wait()
    next(gather1)
    loads[0].wait()
    next(gather_t)

    owner = c * 2 + f // 8
    own_rows = f // 2 == c
    for j in range(8):
        target = (f % 2) * 8 + j
        rows = proj_weight.at[pl.ds(16 * j, 16)]

        @pl.when(own_rows & (target != f))
        def _():
            pltpu.make_async_remote_copy(
                src_ref=rows,
                dst_ref=w2.at[target // 4, target % 4, pl.ds(64, 16)],
                send_sem=sem_p.at[0, j],
                recv_sem=sem_p.at[1, 0],
                device_id=(c, target),
                device_id_type=MESH,
            ).start()

        @pl.when(own_rows & (target == f))
        def _():
            local = pltpu.make_async_copy(
                rows, w2.at[target // 4, target % 4, pl.ds(64, 16)], sem_p.at[1, 1]
            )
            local.start()
            local.wait()

    pltpu.make_async_copy(strips, strips, sem_l.at[6]).wait()
    odd = core == 1
    for m in range(8):
        packed = halves_packed(
            strips[2 * m].astype(f32), strips[2 * m + 1].astype(f32), odd, lane
        )
        w3[y, x, :, 128 * m : 128 * m + 128] = packed.astype(bf16)

    next(gather1)
    loads[2].wait()

    @pl.when(owner != f)
    def _():
        own = w2.at[y, x, pl.ds(64, 16)]
        pltpu.make_async_remote_copy(
            src_ref=own,
            dst_ref=own,
            send_sem=sem_p.at[0, 0],
            recv_sem=sem_p.at[1, 0],
            device_id=other_core(),
            device_id_type=MESH,
        ).wait_recv()

    next(gather_t)
    loads[1].wait()
    next(gather_u)
    next(gather1)
    next(gather2)
    next(gather_t)
    next(gather1)
    next(gather2)
    next(gather_t)
    next(gather1)

    outs = []

    def put(src, dst):
        copy = pltpu.make_async_copy(src, dst, sem_o.at[len(outs)])
        copy.start()
        outs.append(copy)

    put(w1, w1_out)

    vecs[...] = w1[:, :, 128:144, 0:128].reshape(16, 16, 128).astype(f32)
    gain = jnp.concatenate([vecs[i, 0:1, :] for i in range(16)], axis=1)
    shift = jnp.concatenate([vecs[i, 1:2, :] for i in range(16)], axis=1)

    def bias_rows(which):
        parts = []
        for i in range(2):
            row = which * 16 + c * 2 + i
            parts.append(vecs[row // 3, pl.ds(4 + row % 3, 1), :])
        return jnp.concatenate(parts, axis=1)

    qkv_bias = jnp.concatenate([bias_rows(i) for i in range(3)], axis=1)
    up_parts = []
    for m in range(8):
        a = vecs[2 * m, pl.ds(7 + c // 2, 1), :]
        b = vecs[2 * m + 1, pl.ds(7 + c // 2, 1), :]
        up_parts.append(halves_packed(a, b, odd, lane))
    up_bias = jnp.concatenate(up_parts, axis=1)

    seg_all = jnp.concatenate(
        [t[b // 2, b % 2, 128:144, 0:128][0:1].astype(f32) for b in range(8)], axis=0
    )
    seg_cols = jnp.transpose(seg_all)
    firsts = [
        jnp.sum((seg_all < float(d)).astype(f32), keepdims=True) for d in range(1, 4)
    ]
    angles = [first * inv[...] for first in firsts]
    first_cos = [jnp.cos(angle) for angle in angles]
    first_sin = [jnp.sin(angle) for angle in angles]
    in_head = lane % 64
    for b in range(8):
        rows = pl.ds(b * 128, 128)
        own = seg_cols[:, b : b + 1]
        cb, sb = jnp.ones((128, 128), f32), jnp.zeros((128, 128), f32)
        first_position = jnp.zeros((128, 1), f32)
        for d in range(1, 4):
            here = own == float(d)
            cb = jnp.where(here, first_cos[d - 1], cb)
            sb = jnp.where(here, first_sin[d - 1], sb)
            first_position = jnp.where(here, firsts[d - 1], first_position)
        base_cos, base_sin = cos0[rows, :], sin0[rows, :]
        cos = base_cos * cb + base_sin * sb
        sin = base_sin * cb - base_cos * sb
        tab[0, rows, :] = cos
        tab[1, rows, :] = jnp.where(in_head < 16, -sin, 0.0)
        tab[2, rows, :] = jnp.where((in_head >= 16) & (in_head < 32), sin, 0.0)
        begin_col[rows, :] = first_position

    def norm_rows(i, carry):
        b, part = i // 4, i % 4
        src = pl.ds(pl.multiple_of(part * 32, 32), 32)
        values = t[b // 2, b % 2, src, :].astype(f32)
        average = jnp.mean(values, axis=-1, keepdims=True)
        centered = values - average
        variance = jnp.mean(centered * centered, axis=-1, keepdims=True)
        standard = centered * lax.rsqrt(variance + epsilon)
        n[pl.ds(pl.multiple_of(i * 32, 32), 32), :] = (standard * gain + shift).astype(bf16)
        return carry

    lax.fori_loop(0, 32, norm_rows, 0)
    put(n, n_out)
    next(gather2)
    next(gather3)
    next(gather_u)

    def project(m, carry):
        rows = pl.ds(pl.multiple_of(m * 256, 256), 256)
        left = n[rows, :]
        tables = [tab[i, rows, :] for i in range(3)]
        for which in range(3):
            columns = pl.ds(which * COLS, COLS)
            right = w1[:, :, pl.ds(0, 128), columns].reshape(WIDTH, COLS)
            fields = dot(left, right, 1, 0) + qkv_bias[:, which * COLS : (which + 1) * COLS]
            for pair in range(2):
                both = fields[:, pair * 128 : pair * 128 + 128]
                if which < 2:
                    both = turn(both, *tables)
                if which == 0:
                    both = both * 0.125
                both = both.astype(bf16)
                target = (q, k, v)[which]
                target[2 * pair, rows, :] = both[:, :64]
                target[2 * pair + 1, rows, :] = both[:, 64:]
        return carry

    lax.fori_loop(0, 4, project, 0)
    next(gather2)
    next(gather3)
    next(gather_u)
    next(gather2)
    next(gather_u)
    put(w2, w2_out)
    put(u, u_out)

    def context_grad(m, carry):
        rows = pl.ds(pl.multiple_of(m * 256, 256), 256)
        left = u[m].reshape(256, WIDTH)
        right = w2[:, :, pl.ds(64, 16), :].reshape(COLS, WIDTH)
        grads = dot(left, right, 1, 1).astype(bf16)
        for head in range(4):
            dctx[head, rows, :] = grads[:, head * 64 : head * 64 + 64]
        return carry

    lax.fori_loop(0, 4, context_grad, 0)
    next(gather3)

    for block in (3, 2, 1, 0):
        reach = (block + 1) * 256
        rows = pl.ds(block * 256, 256)
        keys = pl.ds(0, reach)
        begins = begin_col[rows, :]
        key_index = lax.broadcasted_iota(jnp.int32, (1, reach), 1).astype(f32)
        row_index = (
            lax.broadcasted_iota(jnp.int32, (256, 1), 0) + block * 256
        ).astype(f32)

        def attend(head, carry, block=block, rows=rows, keys=keys, begins=begins):
            qh, kh, vh, dh = q[head, rows, :], k[head, keys, :], v[head, keys, :], dctx[head, rows, :]
            scores = dot(qh, kh, 1, 1)
            allowed = (key_index >= begins) & (key_index <= row_index)
            scores = jnp.where(allowed, scores, masked_score)
            highest = jnp.max(scores, axis=1, keepdims=True)
            weights = jnp.exp(scores - highest)
            total = jnp.sum(weights, axis=1, keepdims=True)
            probs = weights * (1.0 / total)
            log_sum = jnp.broadcast_to(highest + jnp.log(total), (256, 128))
            lse[pl.ds(head, 1), rows] = jnp.transpose(log_sum)[0:1, :]
            probs_low = probs.astype(bf16)
            ctx_heads[head, rows, :] = dot(probs_low, vh, 1, 0).astype(bf16)
            d_probs = dot(dh, vh, 1, 1)
            delta = jnp.sum(probs * d_probs, axis=1, keepdims=True)
            d_scores = (probs * (d_probs - delta)).astype(bf16)
            dq[head, rows, :] = dot(d_scores, kh, 1, 0)
            d_keys = dot(d_scores, qh, 0, 0)
            d_values = dot(probs_low, dh, 0, 0)
            if block == 3:
                dk[head, keys, :] = d_keys
                dv[head, keys, :] = d_values
            else:
                dk[head, keys, :] += d_keys
                dv[head, keys, :] += d_values
            return carry

        lax.fori_loop(0, 4, attend, 0)
        if block >= 2:
            next(gather3)
    put(w3, w3_out)

    def join(m, carry):
        rows = pl.ds(pl.multiple_of(m * 256, 256), 256)
        tables = [tab[i, rows, :] for i in range(3)]
        for pair in range(2):
            lanes = pl.ds(pair * 128, 128)
            ctx[rows, lanes] = jnp.concatenate(
                [ctx_heads[2 * pair, rows, :], ctx_heads[2 * pair + 1, rows, :]], axis=1
            )
            for which, source in ((0, dq), (1, dk), (2, dv)):
                both = jnp.concatenate(
                    [source[2 * pair, rows, :], source[2 * pair + 1, rows, :]], axis=1
                )
                if which == 0:
                    both = both * 0.125
                if which < 2:
                    both = turn_back(both, *tables)
                dproj[rows, pl.ds(which * COLS + pair * 128, 128)] = both.astype(bf16)
        return carry

    lax.fori_loop(0, 4, join, 0)
    put(dproj, dproj_out)
    put(ctx, ctx_out)
    put(lse, lse_out)

    for i in range(4):
        columns = pl.ds(i * 256, 256)
        bias = up_bias[:, i * 256 : (i + 1) * 256]

        def feed(m, carry, columns=columns, bias=bias, i=i):
            rows = pl.ds(pl.multiple_of(m * 256, 256), 256)
            right = w3[:, :, :, columns].reshape(WIDTH, 256)
            h = dot(n[rows, :], right, 1, 0) + bias
            d_act = dot(
                u[m].reshape(256, WIDTH), w2[i, :, pl.ds(0, 64), :].reshape(256, WIDTH), 1, 1
            )
            square = h * h
            tanh = jnp.tanh(0.7978845608028654 * (h + 0.044715 * square * h))
            half = 0.5 * (1.0 + tanh)
            slope = half + 0.5 * h * (1.0 - tanh * tanh) * (
                0.7978845608028654 * (1.0 + 3.0 * 0.044715 * square)
            )
            act[rows, columns] = (h * half).astype(bf16)
            dhid[rows, columns] = (d_act * slope).astype(bf16)
            return carry

        lax.fori_loop(0, 4, feed, 0)
    put(act, act_out)
    put(dhid, dhid_out)

    for copies in (copies1, copies2, copies3, copies_t, copies_u):
        copies.sent()
    for j in range(8):
        target = (f % 2) * 8 + j

        @pl.when(own_rows & (target != f))
        def _():
            pltpu.make_async_remote_copy(
                src_ref=proj_weight.at[pl.ds(16 * j, 16)],
                dst_ref=w2.at[target // 4, target % 4, pl.ds(64, 16)],
                send_sem=sem_p.at[0, j],
                recv_sem=sem_p.at[1, 0],
                device_id=(c, target),
                device_id_type=MESH,
            ).wait_send()

    for copy in outs:
        copy.wait()


def first_call(tokens, cotangent, qkv_weight, proj_weight, up_weight, down_weight, seg, vec):
    lanes = jnp.arange(128) % 64
    inverse = jnp.exp((lanes % 16).astype(f32) * (-math.log(10000.0) / (ROT_DIMS // 2)))
    inverse = jnp.where(lanes < ROT_DIMS, inverse, 0.0)[None, :]
    base = jnp.arange(SEQ, dtype=f32)[:, None] * inverse
    shapes = dict(
        n=((SEQ, WIDTH), bf16),
        w1=((4, 4, 144, 768), bf16),
        w2=((4, 4, 80, WIDTH), bf16),
        w3=((4, 4, 128, UNITS), bf16),
        u=((4, 2, 128, WIDTH), bf16),
        dproj=((SEQ, 768), bf16),
        ctx=((SEQ, COLS), bf16),
        act=((SEQ, UNITS), bf16),
        dhid=((SEQ, UNITS), bf16),
        lse=((8, SEQ), f32),
    )
    anyspace = pl.BlockSpec(memory_space=pl.ANY)
    vmem = pl.BlockSpec(memory_space=VM)
    return pl.pallas_call(
        first_kernel,
        out_shape=[jax.ShapeDtypeStruct(*s) for s in shapes.values()],
        in_specs=[anyspace] * 6 + [vmem] * 5,
        out_specs=[anyspace] * len(shapes),
        scratch_shapes=[
            VM(*shapes["w1"]),
            VM(*shapes["w2"]),
            VM(*shapes["w3"]),
            VM((4, 2, 144, WIDTH), bf16),
            VM(*shapes["u"]),
            VM(*shapes["n"]),
            VM((16, 128, 128), bf16),
            VM((16, 16, 128), f32),
            VM((3, SEQ, 128), f32),
            VM((SEQ, 1), f32),
            VM((4, SEQ, 64), bf16),
            VM((4, SEQ, 64), bf16),
            VM((4, SEQ, 64), bf16),
            VM((4, SEQ, 64), bf16),
            VM((4, SEQ, 64), f32),
            VM((4, SEQ, 64), f32),
            VM((4, SEQ, 64), f32),
            VM(*shapes["dproj"]),
            VM((4, SEQ, 64), bf16),
            VM(*shapes["ctx"]),
            VM(*shapes["act"]),
            VM(*shapes["dhid"]),
            VM(*shapes["lse"]),
            pltpu.SemaphoreType.DMA((2, 16)),
            pltpu.SemaphoreType.DMA((2, 16)),
            pltpu.SemaphoreType.DMA((2, 16)),
            pltpu.SemaphoreType.DMA((2, 8)),
            pltpu.SemaphoreType.DMA((2, 8)),
            pltpu.SemaphoreType.DMA((2, 8)),
            pltpu.SemaphoreType.DMA((7,)),
            pltpu.SemaphoreType.DMA((10,)),
        ],
        compiler_params=pltpu.CompilerParams(
            collective_id=1, has_side_effects=True, vmem_limit_bytes=60 * 1024 * 1024
        ),
        cost_estimate=pl.CostEstimate(
            flops=25 * 10**9, bytes_accessed=40 * 10**6, transcendentals=4 * 10**6
        ),
        name="first",
    )(
        tokens, cotangent, qkv_weight, proj_weight, up_weight, down_weight, seg, vec,
        jnp.cos(base), jnp.sin(base), inverse,
    )


def add_into(target, part, *others):
    total = target[part].astype(f32)
    for ref, piece in others:
        total = total + ref[piece].astype(f32)
    target[part] = total.astype(bf16)


def plane_reduce(g, cuts, ra, rb, copies):
    c, f, z, core, y, x = place()
    r0, r1, r2, r3, r4 = cuts
    first, last = pl.ds(r0, r2 - r0), pl.ds(r2, r4 - r2)
    q0, q1, q2, q3 = (pl.ds(a, b - a) for a, b in zip(cuts[:-1], cuts[1:]))
    s0, s1, s2, s3 = (pl.ds(0, b - a) for a, b in zip(cuts[:-1], cuts[1:]))
    xu, xd, xo = up1(x), down1(x), over(x)
    yu, yd, yo = up1(y), down1(y), over(y)
    to_xu, to_xd = (c, y * 4 + xu), (c, y * 4 + xd)
    to_yu, to_yd = (c, yu * 4 + x), (c, yd * 4 + x)
    lo, hi, every = pl.ds(0, 2), pl.ds(2, 2), pl.ds(0, 4)
    near, far = pl.ds(0, 2), pl.ds(2, 4)

    def send(k, part, ref, piece, device):
        copies.start(k, g.at[part], ref.at[piece], device)

    def got(k, ref, piece):
        copies.arrived(k, ref.at[piece])

    send(0, (yo, lo, first), ra, (0, near), to_yu)
    send(1, (yo, hi, first), ra, (1, near), to_yd)
    send(2, (lo, xo, last), rb, (0, near), to_xu)
    send(3, (hi, xo, last), rb, (1, near), to_xd)
    yield
    got(0, ra, (0, near))
    add_into(g, (yu, lo, first), (ra, (0, near)))
    send(4, (yu, every, first), ra, (0, far), to_yu)
    got(1, ra, (1, near))
    add_into(g, (yd, hi, first), (ra, (1, near)))
    send(5, (yd, every, first), ra, (1, far), to_yd)
    got(2, rb, (0, near))
    add_into(g, (lo, xu, last), (rb, (0, near)))
    send(6, (every, xu, last), rb, (0, far), to_xu)
    got(3, rb, (1, near))
    add_into(g, (hi, xd, last), (rb, (1, near)))
    send(7, (every, xd, last), rb, (1, far), to_xd)
    yield
    got(4, ra, (0, far))
    got(5, ra, (1, far))
    add_into(g, (y, every, first), (ra, (0, far)), (ra, (1, far)))
    send(8, (y, xo, q0), ra, (0, 6, s0), to_xu)
    send(9, (y, xo, q1), ra, (1, 6, s1), to_xd)
    got(6, rb, (0, far))
    got(7, rb, (1, far))
    add_into(g, (every, x, last), (rb, (0, far)), (rb, (1, far)))
    send(10, (yo, x, q2), rb, (0, 6, s2), to_yu)
    send(11, (yo, x, q3), rb, (1, 6, s3), to_yd)
    yield
    got(8, ra, (0, 6, s0))
    add_into(g, (y, xu, q0), (ra, (0, 6, s0)))
    send(12, (y, xu, first), ra, (0, 7), to_xu)
    got(9, ra, (1, 6, s1))
    add_into(g, (y, xd, q1), (ra, (1, 6, s1)))
    send(13, (y, xd, first), ra, (1, 7), to_xd)
    got(10, rb, (0, 6, s2))
    add_into(g, (yu, x, q2), (rb, (0, 6, s2)))
    send(14, (yu, x, last), rb, (0, 7), to_yu)
    got(11, rb, (1, 6, s3))
    add_into(g, (yd, x, q3), (rb, (1, 6, s3)))
    send(15, (yd, x, last), rb, (1, 7), to_yd)
    yield
    got(12, ra, (0, 7))
    got(13, ra, (1, 7))
    add_into(g, (y, x, first), (ra, (0, 7)), (ra, (1, 7)))
    got(14, rb, (0, 7))
    got(15, rb, (1, 7))
    add_into(g, (y, x, last), (rb, (0, 7)), (rb, (1, 7)))
    yield


def line_reduce(g, cuts, rc, r1, r2, copies):
    c, f, z, core, y, x = place()
    c0, c1, c2 = cuts
    h0, h1 = pl.ds(c0, c1 - c0), pl.ds(c1, c2 - c1)
    s0, s1 = pl.ds(0, c1 - c0), pl.ds(0, c2 - c1)
    zu, zd, zo = up1(z), down1(z), over(z)
    to_zu, to_zd, to_core = (zu * 2 + core, f), (zd * 2 + core, f), (z * 2 + 1 - core, f)
    every = pl.ds(0, 4)
    copies.start(0, g.at[every, 1 - core], rc, to_core)
    yield
    copies.arrived(0, rc)

    def add_row(i, carry):
        add_into(g, (i, core), (rc, (i,)))
        return carry

    lax.fori_loop(0, 4, add_row, 0)
    copies.start(1, g.at[zo, core, h0], r1.at[0, s0], to_zu)
    copies.start(2, g.at[zo, core, h1], r1.at[1, s1], to_zd)
    yield
    copies.arrived(1, r1.at[0, s0])
    add_into(g, (zu, core, h0), (r1, (0, s0)))
    copies.start(3, g.at[zu, core], r2.at[0], to_zu)
    copies.arrived(2, r1.at[1, s1])
    add_into(g, (zd, core, h1), (r1, (1, s1)))
    copies.start(4, g.at[zd, core], r2.at[1], to_zd)
    yield
    copies.arrived(3, r2.at[0])
    copies.arrived(4, r2.at[1])
    yield


def second_kernel(
    n_in,
    w1_in,
    w2_in,
    w3_in,
    u_in,
    dproj_in,
    ctx_in,
    act_in,
    dhid_in,
    tokens,
    cotangent,
    lse,
    block_out,
    token_grad,
    lse_out,
    gq_out,
    gu_out,
    gd_out,
    gp_out,
    w1,
    w2,
    w3,
    n,
    u,
    dproj,
    ctx,
    act,
    dhid,
    own_tokens,
    own_cot,
    vecs,
    vector_rows,
    zo_buf,
    zd_buf,
    zo_rc,
    zo_r1,
    zo_r2,
    zd_rc,
    zd_r1,
    zd_r2,
    ra1,
    rb1,
    ra2,
    rb2,
    ra3,
    rb3,
    gp,
    lse_own,
    sem1,
    sem2,
    sem3,
    sem_zo,
    sem_zd,
    sem_lq,
    sem_lu,
    sem_ld,
    sem_p,
    sem_b,
    sem_l,
    sem_o,
):
    c, f, z, core, y, x = place()
    lane = lax.broadcasted_iota(jnp.int32, (1, 128), 1)
    odd = core == 1
    owner = c * 2 + f // 8
    own_rows = f // 2 == c

    pairs = (
        (act_in, act),
        (w2_in, w2),
        (ctx_in, ctx),
        (u_in, u),
        (dproj_in, dproj),
        (w1_in, w1),
        (dhid_in, dhid),
        (w3_in, w3),
        (n_in, n),
        (tokens, own_tokens),
        (cotangent, own_cot),
    )
    loads = [pltpu.make_async_copy(a, b, sem_l.at[i]) for i, (a, b) in enumerate(pairs)]
    for copy in loads:
        copy.start()
    enter(False, True)

    copies1 = Copies(sem1.at[0], sem1.at[1])
    copies2 = Copies(sem2.at[0], sem2.at[1])
    copies3 = Copies(sem3.at[0], sem3.at[1])
    copies_zo = Copies(sem_zo.at[0], sem_zo.at[1])
    copies_zd = Copies(sem_zd.at[0], sem_zd.at[1])
    copies_lq = Copies(sem_lq.at[0], sem_lq.at[1])
    copies_lu = Copies(sem_lu.at[0], sem_lu.at[1])
    copies_ld = Copies(sem_ld.at[0], sem_ld.at[1])
    reduce1 = plane_reduce(w1, CUTS1, ra1, rb1, copies1)
    reduce2 = plane_reduce(w2, CUTS2, ra2, rb2, copies2)
    reduce3 = plane_reduce(w3, CUTS3, ra3, rb3, copies3)
    reduce_o = line_reduce(zo_buf, (0, 64, 144), zo_rc, zo_r1, zo_r2, copies_zo)
    reduce_d = line_reduce(zd_buf, (0, 64, 128), zd_rc, zd_r1, zd_r2, copies_zd)
    gather_q = line_gather(gq_out, (0, 64, 144), copies_lq, w1.at[y, x])
    gather_u = line_gather(gu_out, (0, 64, 128), copies_lu, w3.at[y, x])
    gather_d = line_gather(gd_out, (0, 32, 64), copies_ld, w2.at[y, x, pl.ds(0, 64)])
    outs = []

    def put(src, dst):
        copy = pltpu.make_async_copy(src, dst, sem_o.at[len(outs)])
        copy.start()
        outs.append(copy)

    for b in range(8):
        part = jnp.concatenate([lse[j : j + 1, b * 128 : b * 128 + 128] for j in range(4)], axis=1)
        wide = jnp.concatenate([jnp.where(c % 4 == s, part, 0.0) for s in range(4)], axis=1)
        high = wide.astype(bf16).astype(f32)
        row = lax.broadcasted_iota(jnp.int32, (16, 1), 0)
        both = jnp.where(row == c // 4, high, jnp.where(row == 2 + c // 4, wide - high, 0.0))
        zo_buf[b // 2, b % 2, 128:144, :] = both.astype(bf16)

    for i in range(3):
        loads[i].wait()

    def out_part(i, carry):
        columns = pl.ds(pl.multiple_of(i * 512, 512), 512)
        total = dot(act[...], w2[:, :, pl.ds(0, 64), columns].reshape(UNITS, 512), 1, 0)
        total = total + dot(ctx[...], w2[:, :, pl.ds(64, 16), columns].reshape(COLS, 512), 1, 0)
        zo_buf[:, :, pl.ds(0, 128), columns] = total.astype(bf16).reshape(4, 2, 128, 512)
        return carry

    lax.fori_loop(0, 4, out_part, 0)
    next(reduce_o)
    loads[3].wait()

    def down_part(i, carry):
        columns = pl.ds(pl.multiple_of(i * 512, 512), 512)
        right = u[:, :, :, columns].reshape(SEQ, 512)
        grads = dot(act[...], right, 0, 0).astype(bf16)
        w2[:, :, pl.ds(0, 64), columns] = grads.reshape(4, 4, 64, 512)
        grads = dot(ctx[...], right, 0, 0).astype(bf16)
        w2[:, :, pl.ds(64, 16), columns] = grads.reshape(4, 4, 16, 512)
        return carry

    lax.fori_loop(0, 4, down_part, 0)
    next(reduce2)
    next(reduce_o)
    for i in range(4, 8):
        loads[i].wait()
    vecs[...] = w1[:, :, 128:144, 0:128].reshape(16, 16, 128).astype(f32)
    gain = jnp.concatenate([vecs[i, 0:1, :] for i in range(16)], axis=1)

    def normed_part(i, carry):
        columns = pl.ds(pl.multiple_of(i * 512, 512), 512)
        total = dot(dproj[...], w1[i, :, pl.ds(0, 128), :].reshape(512, 768), 1, 1)
        total = total + dot(dhid[...], w3[i].reshape(512, UNITS), 1, 1)
        zd_buf[:, :, :, columns] = total.astype(bf16).reshape(4, 2, 128, 512)
        return carry

    lax.fori_loop(0, 2, normed_part, 0)
    next(reduce2)
    lax.fori_loop(2, 4, normed_part, 0)
    next(reduce_d)
    next(reduce_o)
    loads[8].wait()

    def up_part(i, carry):
        columns = pl.ds(pl.multiple_of(i * 512, 512), 512)
        grads = dot(n[:, columns], dhid[...], 0, 0).astype(bf16)
        w3[i] = grads.reshape(4, 128, UNITS)
        return carry

    lax.fori_loop(0, 2, up_part, 0)
    next(reduce2)
    lax.fori_loop(2, 4, up_part, 0)
    next(reduce3)
    next(reduce_d)
    next(reduce2)

    def qkv_part(i, carry):
        columns = pl.ds(pl.multiple_of(i * 512, 512), 512)
        grads = dot(n[:, columns], dproj[...], 0, 0).astype(bf16)
        w1[i, :, pl.ds(0, 128), :] = grads.reshape(4, 128, 768)
        return carry

    lax.fori_loop(0, 4, qkv_part, 0)
    next(reduce3)
    next(reduce_d)
    next(reduce2)

    next(gather_d)
    put(w2.at[y, x, pl.ds(0, 64)], gd_out.at[z, core])
    rows = w2.at[y, x, pl.ds(64, 16)]
    for j in range(8):
        slot = gp.at[pl.ds(16 * j, 16)]

        @pl.when((f % 8 == j) & (owner != f))
        def _():
            pltpu.make_async_remote_copy(
                src_ref=rows,
                dst_ref=slot,
                send_sem=sem_p.at[0, 0],
                recv_sem=sem_p.at[1, j],
                device_id=(c, owner),
                device_id_type=MESH,
            ).start()

        @pl.when((f % 8 == j) & (owner == f))
        def _():
            local = pltpu.make_async_copy(rows, slot, sem_p.at[0, 1])
            local.start()
            local.wait()

    loads[9].wait()
    loads[10].wait()
    next(reduce_o)
    proj_bias = jnp.concatenate([vecs[i, 2:3, :] for i in range(16)], axis=1)
    down_bias = jnp.concatenate([vecs[i, 3:4, :] for i in range(16)], axis=1)

    def finish_out(i, carry):
        part = pl.ds(pl.multiple_of(i * 32, 32), 32)
        total = zo_buf[z, core, part, :].astype(f32)
        total = total + zo_r2[0, part, :].astype(f32) + zo_r2[1, part, :].astype(f32)
        total = own_tokens[part, :].astype(f32) + total + proj_bias + down_bias
        zo_r2[0, part, :] = total.astype(bf16)
        return carry

    tail = pl.ds(128, 16)
    sums = zo_buf[z, core, tail, :].astype(f32)
    sums = sums + zo_r2[0, tail, :].astype(f32) + zo_r2[1, tail, :].astype(f32)
    sums = sums[0:2, :] + sums[2:4, :]
    for h in range(32):
        lse_own[h : h + 1, :] = sums[h // 16 : h // 16 + 1, (h % 16) * 128 : (h % 16) * 128 + 128]
    lax.fori_loop(0, 4, finish_out, 0)
    put(zo_r2.at[0, pl.ds(0, 128)], block_out)
    put(lse_own, lse_out)
    next(reduce3)

    next(reduce_d)
    zero = jnp.zeros((1, WIDTH), f32)

    def finish_grad(i, carry):
        d_gain, d_shift, d_bias = carry
        part = pl.ds(pl.multiple_of(i * 32, 32), 32)
        grads = zd_buf[z, core, part, :].astype(f32)
        grads = grads + zd_r2[0, part, :].astype(f32) + zd_r2[1, part, :].astype(f32)
        values = own_tokens[part, :].astype(f32)
        average = jnp.mean(values, axis=-1, keepdims=True)
        centered = values - average
        variance = jnp.mean(centered * centered, axis=-1, keepdims=True)
        scale = lax.rsqrt(variance + epsilon)
        standard = centered * scale
        d_gain = d_gain + jnp.sum(grads * standard, axis=0, keepdims=True)
        d_shift = d_shift + jnp.sum(grads, axis=0, keepdims=True)
        scaled = grads * gain
        inner = scaled - jnp.mean(scaled, axis=-1, keepdims=True)
        inner = inner - standard * jnp.mean(scaled * standard, axis=-1, keepdims=True)
        upstream = own_cot[part, :].astype(f32)
        d_bias = d_bias + jnp.sum(upstream, axis=0, keepdims=True)
        zd_r2[0, part, :] = (upstream + scale * inner).astype(bf16)
        return d_gain, d_shift, d_bias

    d_gain, d_shift, d_bias = lax.fori_loop(0, 4, finish_grad, (zero, zero, zero))
    put(zd_r2.at[0], token_grad)

    vector_rows[...] = jnp.zeros((16, 16, 128), f32)
    for i in range(16):
        lanes = slice(i * 128, i * 128 + 128)
        vector_rows[i, 0:1, :] = d_gain[:, lanes]
        vector_rows[i, 1:2, :] = d_shift[:, lanes]
        vector_rows[i, 2:3, :] = d_bias[:, lanes]
    ones = jnp.ones((8, SEQ), bf16)
    d_qkv = dot(ones, dproj[...], 1, 0)[0:1, :]
    d_up = dot(ones, dhid[...], 1, 0)[0:1, :]
    for which in range(3):
        for i in range(2):
            row = which * 16 + c * 2 + i
            start = which * COLS + i * 128
            vector_rows[row // 3, pl.ds(3 + row % 3, 1), :] = d_qkv[:, start : start + 128]
    for m in range(8):
        both = d_up[:, m * 128 : m * 128 + 128]
        moved = pltpu.roll(both, 64, 1)
        mine = (lane >= 64) == odd
        vector_rows[2 * m, pl.ds(6 + c // 2, 1), :] = jnp.where(
            mine, jnp.where(odd, moved, both), 0.0
        )
        vector_rows[2 * m + 1, pl.ds(6 + c // 2, 1), :] = jnp.where(
            mine, jnp.where(odd, both, moved), 0.0
        )
    w1[:, :, 128:144, 0:128] = vector_rows[...].reshape(4, 4, 16, 128).astype(bf16)
    w1[:, :, 128:144, 128:768] = jnp.zeros((4, 4, 16, 640), bf16)
    next(reduce1)
    next(gather_d)
    next(reduce3)
    next(reduce1)

    def trade(k, src, dst, device):
        return pltpu.make_async_remote_copy(
            src_ref=src,
            dst_ref=dst,
            send_sem=sem_b.at[0, k],
            recv_sem=sem_b.at[1, k],
            device_id=device,
            device_id_type=MESH,
        )

    for j in range(8):

        @pl.when(own_rows & ((f % 2) * 8 + j != f))
        def _():
            slot = gp.at[pl.ds(16 * j, 16)]
            pltpu.make_async_remote_copy(
                src_ref=slot,
                dst_ref=slot,
                send_sem=sem_p.at[0, 0],
                recv_sem=sem_p.at[1, j],
                device_id=other_core(),
                device_id_type=MESH,
            ).wait_recv()

    mine = core == x // 2
    turns = (z - y + 4) % 4
    to_zu, to_zd = (up1(z) * 2 + core, f), (down1(z) * 2 + core, f)
    to_core = other_core()
    h0, h1 = gp.at[pl.ds(0, 64)], gp.at[pl.ds(64, 64)]

    @pl.when(mine & (turns == 0))
    def _():
        trade(0, gp, gp, to_zu).start()
        trade(1, gp, gp, to_zd).start()

    @pl.when(mine & (turns == 1))
    def _():
        trade(0, gp, gp, to_core).wait_recv()
        trade(2, h0, h0, to_zu).start()

    @pl.when(mine & (turns == 3))
    def _():
        trade(1, gp, gp, to_core).wait_recv()
        trade(3, h1, h1, to_zd).start()

    next(gather_d)
    next(reduce3)
    next(gather_u)
    put(w3.at[y, x], gu_out.at[z, core])
    next(reduce1)

    @pl.when(mine & (turns == 2))
    def _():
        trade(2, h0, h0, to_core).wait_recv()
        trade(3, h1, h1, to_core).wait_recv()

    @pl.when(mine)
    def _():
        trade(4, gp, gp, to_core).start()

    next(gather_u)
    next(reduce1)
    next(gather_u)
    next(reduce1)
    next(gather_q)
    put(w1.at[y, x], gq_out.at[z, core])

    @pl.when(jnp.logical_not(mine))
    def _():
        trade(4, gp, gp, to_core).wait_recv()

    put(gp, gp_out)
    next(gather_q)
    next(gather_d)
    next(gather_u)
    next(gather_q)
    next(gather_q)

    for copies in (
        copies1, copies2, copies3, copies_zo, copies_zd, copies_lq, copies_lu, copies_ld
    ):
        copies.sent()

    @pl.when(owner != f)
    def _():
        pltpu.make_async_remote_copy(
            src_ref=rows,
            dst_ref=gp.at[pl.ds(0, 16)],
            send_sem=sem_p.at[0, 0],
            recv_sem=sem_p.at[1, 0],
            device_id=(c, owner),
            device_id_type=MESH,
        ).wait_send()

    @pl.when(mine & (turns == 0))
    def _():
        trade(0, gp, gp, to_zu).wait_send()
        trade(1, gp, gp, to_zd).wait_send()

    @pl.when(mine & (turns == 1))
    def _():
        trade(2, h0, h0, to_zu).wait_send()

    @pl.when(mine & (turns == 3))
    def _():
        trade(3, h1, h1, to_zd).wait_send()

    @pl.when(mine)
    def _():
        trade(4, gp, gp, to_core).wait_send()

    for copy in outs:
        copy.wait()


def second_call(n, w1, w2, w3, u, dproj, ctx, act, dhid, tokens, cotangent, lse):
    anyspace = pl.BlockSpec(memory_space=pl.ANY)
    vmem = pl.BlockSpec(memory_space=VM)
    dma = pltpu.SemaphoreType.DMA
    given = (w1, w2, w3, n, u, dproj, ctx, act, dhid, tokens, cotangent)
    return pl.pallas_call(
        second_kernel,
        out_shape=[
            jax.ShapeDtypeStruct((128, WIDTH), bf16),
            jax.ShapeDtypeStruct((128, WIDTH), bf16),
            jax.ShapeDtypeStruct((32, 128), f32),
            jax.ShapeDtypeStruct((4, 2, 144, 768), bf16),
            jax.ShapeDtypeStruct((4, 2, 128, UNITS), bf16),
            jax.ShapeDtypeStruct((4, 2, 64, WIDTH), bf16),
            jax.ShapeDtypeStruct((128, WIDTH), bf16),
        ],
        in_specs=[anyspace] * 11 + [vmem],
        out_specs=[anyspace] * 7,
        scratch_shapes=[VM(a.shape, a.dtype) for a in given]
        + [
            VM((16, 16, 128), f32),
            VM((16, 16, 128), f32),
            VM((4, 2, 144, WIDTH), bf16),
            VM((4, 2, 128, WIDTH), bf16),
            VM((4, 144, WIDTH), bf16),
            VM((2, 80, WIDTH), bf16),
            VM((2, 144, WIDTH), bf16),
            VM((4, 128, WIDTH), bf16),
            VM((2, 64, WIDTH), bf16),
            VM((2, 128, WIDTH), bf16),
            VM((2, 8, 64, 768), bf16),
            VM((2, 8, 80, 768), bf16),
            VM((2, 8, 32, WIDTH), bf16),
            VM((2, 8, 48, WIDTH), bf16),
            VM((2, 8, 64, UNITS), bf16),
            VM((2, 8, 64, UNITS), bf16),
            VM((128, WIDTH), bf16),
            VM((32, 128), f32),
            dma((2, 16)),
            dma((2, 16)),
            dma((2, 16)),
            dma((2, 5)),
            dma((2, 5)),
            dma((2, 8)),
            dma((2, 8)),
            dma((2, 8)),
            dma((2, 8)),
            dma((2, 5)),
            dma((11,)),
            dma((7,)),
        ],
        compiler_params=pltpu.CompilerParams(
            collective_id=2, has_side_effects=True, vmem_limit_bytes=62 * 1024 * 1024
        ),
        cost_estimate=pl.CostEstimate(
            flops=26 * 10**9, bytes_accessed=60 * 10**6, transcendentals=0
        ),
        name="second",
    )(n, w1, w2, w3, u, dproj, ctx, act, dhid, tokens, cotangent, lse)


def local(
    tokens,
    segments,
    ln_gain,
    ln_shift,
    qkv_weight,
    qkv_bias,
    proj_weight,
    proj_bias,
    up_weight,
    up_bias,
    down_weight,
    down_bias,
    cotangent,
):
    packed = jnp.concatenate([ln_gain, ln_shift, proj_bias, down_bias, qkv_bias, up_bias])
    vec = jnp.pad(packed.reshape(11, 128), ((0, 5), (0, 0)))
    n, w1, w2, w3, u, dproj, ctx, act, dhid, lse = first_call(
        tokens[0], cotangent[0], qkv_weight, proj_weight, up_weight, down_weight, segments, vec
    )
    block_out, token_grad, log_sums, gq, gu, gd, gp = second_call(
        n, w1, w2, w3, u, dproj, ctx, act, dhid, tokens[0], cotangent[0], lse
    )
    gq = gq.reshape(8, 144, 768)
    vectors = jnp.sum(gq[:, 128:, :128].astype(f32), axis=0)
    qkv_grad = jnp.transpose(gq[:, :128].reshape(8, 128, 3, COLS), (1, 2, 0, 3))
    up_grad = jnp.transpose(gu.reshape(8, 128, 16, 64), (1, 2, 0, 3))
    return (
        block_out[None],
        token_grad[None],
        log_sums[None],
        vectors[0],
        vectors[1],
        qkv_grad.reshape(128, 3 * WIDTH).astype(f32),
        vectors[3:6].reshape(384),
        gp.astype(f32),
        vectors[2],
        up_grad.reshape(128, HIDDEN).astype(f32),
        vectors[6:10].reshape(512),
        gd.reshape(512, WIDTH).astype(f32),
        vectors[2],
    )


def solution(mesh):
    in_specs = (
        P("fsdp", "ctx", None),
        P("fsdp", "ctx"),
        P("fsdp"),
        P("fsdp"),
        P("fsdp", None),
        P("fsdp"),
        P("fsdp", None),
        P("fsdp"),
        P("fsdp", None),
        P("fsdp"),
        P("fsdp", None),
        P("fsdp"),
        P("fsdp", "ctx", None),
    )
    out_specs = (
        P("fsdp", "ctx", None),
        P("fsdp", "ctx", None),
        P("fsdp", None, "ctx"),
        P("fsdp"),
        P("fsdp"),
        P("fsdp", None),
        P("fsdp"),
        P("fsdp", None),
        P("fsdp"),
        P("fsdp", None),
        P("fsdp"),
        P("fsdp", None),
        P("fsdp"),
    )
    return jax.shard_map(local, mesh=mesh, in_specs=in_specs, out_specs=out_specs, check_vma=False)
```

```python
from functools import partial
import math

import jax
import jax.numpy as jnp
from jax import lax
from jax.experimental import pallas as pl
from jax.experimental.pallas import tpu as pltpu
from jax.sharding import PartitionSpec as P

HEAD = 64
ROT_DIMS = 32
SEQ = 1024
WIDTH = 2048
HIDDEN = 8192
OWN_HEADS = 4
COLS = 256
UNITS = 1024

epsilon = 1e-05
masked_score = -1e30
f32 = jnp.float32
bf16 = jnp.bfloat16
MESH = pl.DeviceIdType.MESH
VM = pltpu.VMEM


def dot(a, b, ca, cb):
    return lax.dot_general(a, b, (((ca,), (cb,)), ((), ())), preferred_element_type=f32)


def place():
    c = lax.axis_index("ctx")
    f = lax.axis_index("fsdp")
    return c, f, c // 2, c % 2, f // 4, f % 4


def other_core():
    c, f, z, core, y, x = place()
    return (z * 2 + 1 - core, f)


def up1(i):
    return (i + 1) % 4


def down1(i):
    return (i + 3) % 4


def over(i):
    return (i + 2) % 4


class Copies:
    def __init__(self, send, recv):
        self.send, self.recv = send, recv
        self.started = []

    def start(self, k, src, dst, device):
        copy = pltpu.make_async_remote_copy(
            src_ref=src,
            dst_ref=dst,
            send_sem=self.send.at[k],
            recv_sem=self.recv.at[k],
            device_id=device,
            device_id_type=MESH,
        )
        copy.start()
        self.started.append(copy)

    def arrived(self, k, dst):
        pltpu.make_async_remote_copy(
            src_ref=dst,
            dst_ref=dst,
            send_sem=self.send.at[k],
            recv_sem=self.recv.at[k],
            device_id=other_core(),
            device_id_type=MESH,
        ).wait_recv()

    def sent(self):
        for copy in self.started:
            copy.wait_send()
        self.started = []


def plane_gather(w, cuts, copies):
    c, f, z, core, y, x = place()
    r0, r1, r2, r3, r4 = cuts
    first, last = pl.ds(r0, r2 - r0), pl.ds(r2, r4 - r2)
    q0, q1, q2, q3 = (pl.ds(a, b - a) for a, b in zip(cuts[:-1], cuts[1:]))
    xu, xd, xo = up1(x), down1(x), over(x)
    yu, yd, yo = up1(y), down1(y), over(y)
    to_xu, to_xd = (c, y * 4 + xu), (c, y * 4 + xd)
    to_yu, to_yd = (c, yu * 4 + x), (c, yd * 4 + x)
    lo, hi = pl.ds(0, 2), pl.ds(2, 2)
    every = pl.ds(0, 4)

    def send(k, part, device):
        copies.start(k, w.at[part], w.at[part], device)

    def got(k, part):
        copies.arrived(k, w.at[part])

    send(0, (y, x, first), to_xu)
    send(1, (y, x, first), to_xd)
    send(2, (y, x, last), to_yu)
    send(3, (y, x, last), to_yd)
    yield
    got(0, (y, xd, first))
    send(4, (y, xd, q0), to_xu)
    got(1, (y, xu, first))
    send(5, (y, xu, q1), to_xd)
    got(2, (yd, x, last))
    send(6, (yd, x, q2), to_yu)
    got(3, (yu, x, last))
    send(7, (yu, x, q3), to_yd)
    yield
    got(4, (y, xo, q0))
    got(5, (y, xo, q1))
    send(8, (y, every, first), to_yu)
    send(9, (y, every, first), to_yd)
    got(6, (yo, x, q2))
    got(7, (yo, x, q3))
    send(10, (every, x, last), to_xu)
    send(11, (every, x, last), to_xd)
    yield
    got(8, (yd, every, first))
    send(12, (yd, lo, first), to_yu)
    got(9, (yu, every, first))
    send(13, (yu, hi, first), to_yd)
    got(10, (every, xd, last))
    send(14, (lo, xd, last), to_xu)
    got(11, (every, xu, last))
    send(15, (hi, xu, last), to_xd)
    yield
    got(12, (yo, lo, first))
    got(13, (yo, hi, first))
    got(14, (lo, xo, last))
    got(15, (hi, xo, last))
    yield


def line_gather(t, cuts, copies, own=None):
    c, f, z, core, y, x = place()
    r0, r1, r2 = cuts
    h0, h1 = pl.ds(r0, r1 - r0), pl.ds(r1, r2 - r1)
    zu, zd, zo = up1(z), down1(z), over(z)
    to_zu, to_zd, to_core = (zu * 2 + core, f), (zd * 2 + core, f), (z * 2 + 1 - core, f)
    other = 1 - core

    def send(k, part, device):
        copies.start(k, t.at[part], t.at[part], device)

    def got(k, part):
        copies.arrived(k, t.at[part])

    mine = t.at[z, core]
    own = mine if own is None else own
    copies.start(0, own, mine, to_zu)
    copies.start(1, own, mine, to_zd)
    copies.start(2, own, mine, to_core)
    yield
    got(0, (zd, core))
    send(3, (zd, core, h0), to_zu)
    got(1, (zu, core))
    send(4, (zu, core, h1), to_zd)
    send(5, (zd, core), to_core)
    send(6, (zu, core), to_core)
    yield
    got(3, (zo, core, h0))
    got(4, (zo, core, h1))
    send(7, (zo, core), to_core)
    yield
    got(2, (z, other))
    got(5, (zd, other))
    got(6, (zu, other))
    got(7, (zo, other))
    yield


def enter():
    c, f, z, core, y, x = place()
    barrier = pltpu.get_barrier_semaphore()
    for device in (
        (c, y * 4 + up1(x)),
        (c, y * 4 + down1(x)),
        (c, up1(y) * 4 + x),
        (c, down1(y) * 4 + x),
        (up1(z) * 2 + core, f),
        (down1(z) * 2 + core, f),
        (z * 2 + 1 - core, f),
    ):
        pl.semaphore_signal(barrier, inc=1, device_id=device, device_id_type=MESH)
    owner = c * 2 + f // 8

    @pl.when(owner != f)
    def _():
        pl.semaphore_signal(barrier, inc=1, device_id=(c, owner), device_id_type=MESH)

    for j in range(8):
        target = (f % 2) * 8 + j

        @pl.when((f // 2 == c) & (target != f))
        def _():
            pl.semaphore_signal(barrier, inc=1, device_id=(c, target), device_id_type=MESH)

    count = 7 + jnp.where(f // 2 == c, jnp.where(f // 8 == f % 2, 7, 8), 0)
    count = count + jnp.where(owner != f, 1, 0)
    pl.semaphore_wait(barrier, count)


def turn(fields, cos, low_sin, high_sin):
    return (
        fields * cos + pltpu.roll(fields, 112, 1) * low_sin + pltpu.roll(fields, 16, 1) * high_sin
    )


def turn_back(grads, cos, low_sin, high_sin):
    return (
        grads * cos + pltpu.roll(grads * low_sin, 16, 1) + pltpu.roll(grads * high_sin, 112, 1)
    )


def halves_packed(a, b, odd, lane):
    moved_a, moved_b = pltpu.roll(a, 64, 1), pltpu.roll(b, 64, 1)
    return jnp.where(lane < 64, jnp.where(odd, moved_a, a), jnp.where(odd, b, moved_b))


def add_into(target, part, *others):
    total = target[part].astype(f32)
    for ref, piece in others:
        total = total + ref[piece].astype(f32)
    target[part] = total.astype(target.dtype)


def plane_reduce(g, cuts, ra, rb, copies):
    c, f, z, core, y, x = place()
    r0, r1, r2, r3, r4 = cuts
    first, last = pl.ds(r0, r2 - r0), pl.ds(r2, r4 - r2)
    q0, q1, q2, q3 = (pl.ds(a, b - a) for a, b in zip(cuts[:-1], cuts[1:]))
    s0, s1, s2, s3 = (pl.ds(0, b - a) for a, b in zip(cuts[:-1], cuts[1:]))
    xu, xd, xo = up1(x), down1(x), over(x)
    yu, yd, yo = up1(y), down1(y), over(y)
    to_xu, to_xd = (c, y * 4 + xu), (c, y * 4 + xd)
    to_yu, to_yd = (c, yu * 4 + x), (c, yd * 4 + x)
    lo, hi, every = pl.ds(0, 2), pl.ds(2, 2), pl.ds(0, 4)
    near, far = pl.ds(0, 2), pl.ds(2, 4)

    def send(k, part, ref, piece, device):
        copies.start(k, g.at[part], ref.at[piece], device)

    def got(k, ref, piece):
        copies.arrived(k, ref.at[piece])

    send(0, (yo, lo, first), ra, (0, near), to_yu)
    send(1, (yo, hi, first), ra, (1, near), to_yd)
    send(2, (lo, xo, last), rb, (0, near), to_xu)
    send(3, (hi, xo, last), rb, (1, near), to_xd)
    yield
    got(0, ra, (0, near))
    add_into(g, (yu, lo, first), (ra, (0, near)))
    send(4, (yu, every, first), ra, (0, far), to_yu)
    got(1, ra, (1, near))
    add_into(g, (yd, hi, first), (ra, (1, near)))
    send(5, (yd, every, first), ra, (1, far), to_yd)
    got(2, rb, (0, near))
    add_into(g, (lo, xu, last), (rb, (0, near)))
    send(6, (every, xu, last), rb, (0, far), to_xu)
    got(3, rb, (1, near))
    add_into(g, (hi, xd, last), (rb, (1, near)))
    send(7, (every, xd, last), rb, (1, far), to_xd)
    yield
    got(4, ra, (0, far))
    got(5, ra, (1, far))
    add_into(g, (y, every, first), (ra, (0, far)), (ra, (1, far)))
    send(8, (y, xo, q0), ra, (0, 6, s0), to_xu)
    send(9, (y, xo, q1), ra, (1, 6, s1), to_xd)
    got(6, rb, (0, far))
    got(7, rb, (1, far))
    add_into(g, (every, x, last), (rb, (0, far)), (rb, (1, far)))
    send(10, (yo, x, q2), rb, (0, 6, s2), to_yu)
    send(11, (yo, x, q3), rb, (1, 6, s3), to_yd)
    yield
    got(8, ra, (0, 6, s0))
    add_into(g, (y, xu, q0), (ra, (0, 6, s0)))
    send(12, (y, xu, first), ra, (0, 7), to_xu)
    got(9, ra, (1, 6, s1))
    add_into(g, (y, xd, q1), (ra, (1, 6, s1)))
    send(13, (y, xd, first), ra, (1, 7), to_xd)
    got(10, rb, (0, 6, s2))
    add_into(g, (yu, x, q2), (rb, (0, 6, s2)))
    send(14, (yu, x, last), rb, (0, 7), to_yu)
    got(11, rb, (1, 6, s3))
    add_into(g, (yd, x, q3), (rb, (1, 6, s3)))
    send(15, (yd, x, last), rb, (1, 7), to_yd)
    yield
    got(12, ra, (0, 7))
    got(13, ra, (1, 7))
    add_into(g, (y, x, first), (ra, (0, 7)), (ra, (1, 7)))
    got(14, rb, (0, 7))
    got(15, rb, (1, 7))
    add_into(g, (y, x, last), (rb, (0, 7)), (rb, (1, 7)))
    yield


def line_reduce(g, cuts, rc, r1, r2, copies):
    c, f, z, core, y, x = place()
    c0, c1, c2 = cuts
    h0, h1 = pl.ds(c0, c1 - c0), pl.ds(c1, c2 - c1)
    s0, s1 = pl.ds(0, c1 - c0), pl.ds(0, c2 - c1)
    zu, zd, zo = up1(z), down1(z), over(z)
    to_zu, to_zd, to_core = (zu * 2 + core, f), (zd * 2 + core, f), (z * 2 + 1 - core, f)
    every = pl.ds(0, 4)
    copies.start(0, g.at[every, 1 - core], rc, to_core)
    yield
    copies.arrived(0, rc)

    def add_row(i, carry):
        add_into(g, (i, core), (rc, (i,)))
        return carry

    lax.fori_loop(0, 4, add_row, 0)
    copies.start(1, g.at[zo, core, h0], r1.at[0, s0], to_zu)
    copies.start(2, g.at[zo, core, h1], r1.at[1, s1], to_zd)
    yield
    copies.arrived(1, r1.at[0, s0])
    add_into(g, (zu, core, h0), (r1, (0, s0)))
    copies.start(3, g.at[zu, core], r2.at[0], to_zu)
    copies.arrived(2, r1.at[1, s1])
    add_into(g, (zd, core, h1), (r1, (1, s1)))
    copies.start(4, g.at[zd, core], r2.at[1], to_zd)
    yield
    copies.arrived(3, r2.at[0])
    copies.arrived(4, r2.at[1])
    yield


def vector_reduce(g, ry, rx, copies):
    c, f, z, core, y, x = place()
    xu, xd, xo = up1(x), down1(x), over(x)
    yu, yd, yo = up1(y), down1(y), over(y)
    to_xu, to_xd = (c, y * 4 + xu), (c, y * 4 + xd)
    to_yu, to_yd = (c, yu * 4 + x), (c, yd * 4 + x)
    copies.start(0, g.at[yo], ry.at[0], to_yu)
    yield
    copies.arrived(0, ry.at[0])
    add_into(g, (yu,), (ry, (0,)))
    copies.start(1, g.at[yu], ry.at[1], to_yu)
    copies.start(2, g.at[yd], ry.at[2], to_yd)
    yield
    copies.arrived(1, ry.at[1])
    copies.arrived(2, ry.at[2])
    add_into(g, (y,), (ry, (1,)), (ry, (2,)))
    copies.start(3, g.at[y, xo], rx.at[0], to_xu)
    yield
    copies.arrived(3, rx.at[0])
    add_into(g, (y, xu), (rx, (0,)))
    copies.start(4, g.at[y, xu], rx.at[1], to_xu)
    copies.start(5, g.at[y, xd], rx.at[2], to_xd)
    yield
    copies.arrived(4, rx.at[1])
    copies.arrived(5, rx.at[2])
    add_into(g, (y, x), (rx, (1,)), (rx, (2,)))
    yield


GATHER1 = (0, 48, 96, 144, 192)
REDUCE1 = (0, 48, 96, 128, 176)
CUTS2 = (0, 16, 32, 48, 64)
CUTS3 = (0, 32, 64, 96, 128)
PROJ = ((0, 768), (768, 768), (1536, 512))


def layer_kernel(
    tokens,
    cotangent,
    qkv_weight,
    proj_weight,
    up_weight,
    down_weight,
    seg,
    gain_in,
    shift_in,
    proj_bias_in,
    down_bias_in,
    qkv_bias_in,
    up_bias_in,
    block_out,
    token_grad,
    lse_out,
    gq_out,
    gu_out,
    gd_out,
    gp_out,
    gv_out,
    w1,
    w2,
    w3,
    t,
    u,
    n,
    zd,
    rc,
    zo_r1,
    zo_r2,
    zd_r1,
    zd_r2,
    ra1,
    rb1,
    ra3,
    rb3,
    vecs,
    tab,
    begin_cols,
    q,
    k,
    v,
    dctx,
    ctx,
    dk,
    dv,
    dproj,
    act,
    dhid,
    lse,
    lse_own,
    pt,
    gp,
    gv,
    ry,
    rx,
    sem1,
    sem2,
    sem3,
    sem_t,
    sem_u,
    sem_r1,
    sem_r2,
    sem_r3,
    sem_v,
    sem_zo,
    sem_zd,
    sem_lq,
    sem_lu,
    sem_ld,
    sem_lv,
    sem_s,
    sem_p,
    sem_b,
    sem_l,
    sem_o,
    n_free,
    rc_free,
):
    c, f, z, core, y, x = place()
    lane = lax.broadcasted_iota(jnp.int32, (1, 128), 1)
    odd = core == 1
    owner = c * 2 + f // 8
    own_rows = f // 2 == c
    zo = t

    loads = [
        pltpu.make_async_copy(tokens, t.at[z, core, pl.ds(0, 128)], sem_l.at[0]),
        pltpu.make_async_copy(cotangent, u.at[z, core], sem_l.at[1]),
        pltpu.make_async_copy(
            down_weight.at[pl.ds(pl.multiple_of(c * 64, 64), 64)], w2.at[y, x], sem_l.at[2]
        ),
    ]
    for i in range(3):
        loads.append(
            pltpu.make_async_copy(
                qkv_weight.at[:, pl.ds(pl.multiple_of(i * WIDTH + c * COLS, 128), COLS)],
                w1.at[y, x, pl.ds(0, 128), pl.ds(i * COLS, COLS)],
                sem_l.at[3 + i],
            )
        )
    for copy in loads:
        copy.start()
    for i in range(16):
        pltpu.make_async_copy(
            up_weight.at[:, pl.ds(pl.multiple_of(i * 512 + (c // 2) * 128, 128), 128)],
            q.at[pl.ds(i // 2 * 128, 128), pl.ds(i % 2 * 128, 128)],
            sem_l.at[6],
        ).start()
    vector_list = [gain_in[...], shift_in[...], proj_bias_in[...], down_bias_in[...]]
    vector_list += [qkv_bias_in[:, 128 * i : 128 * i + 128] for i in range(3)]
    vector_list += [up_bias_in[:, 128 * i : 128 * i + 128] for i in range(4)]
    vector_list = [vector.astype(f32) for vector in vector_list] + [jnp.zeros((5, 128), f32)]
    w1[y, x, 176:192, 0:128] = jnp.concatenate(vector_list, axis=0).astype(bf16)
    w1[y, x, 176:192, 128:768] = jnp.zeros((16, 640), bf16)
    w1[y, x, 160:176, 512:768] = jnp.zeros((16, 256), bf16)
    seg_rows = jnp.broadcast_to(seg[...].astype(f32), (16, 128)).astype(bf16)
    t[z, core, 128:144, 0:128] = seg_rows
    t[z, core, 128:144, 128:WIDTH] = jnp.zeros((16, WIDTH - 128), bf16)

    enter()

    def both_ways(sems):
        return Copies(sems.at[0], sems.at[1])

    copies1, copies2, copies3 = both_ways(sem1), both_ways(sem2), both_ways(sem3)
    copies_t, copies_u = both_ways(sem_t), both_ways(sem_u)
    copies_r1, copies_r2, copies_r3 = both_ways(sem_r1), both_ways(sem_r2), both_ways(sem_r3)
    copies_v = both_ways(sem_v)
    copies_zo, copies_zd = both_ways(sem_zo), both_ways(sem_zd)
    copies_lq, copies_lu = both_ways(sem_lq), both_ways(sem_lu)
    copies_ld, copies_lv = both_ways(sem_ld), both_ways(sem_lv)
    gather1 = plane_gather(w1, GATHER1, copies1)
    gather2 = plane_gather(w2, CUTS2, copies2)
    gather3 = plane_gather(w3, CUTS3, copies3)
    gather_t = line_gather(t, (0, 64, 144), copies_t)
    gather_u = line_gather(u, (0, 64, 128), copies_u)
    reduce1 = plane_reduce(w1, REDUCE1, ra1, rb1, copies_r1)
    reduce2 = plane_reduce(w2, CUTS2, n.at[0], n.at[1], copies_r2)
    reduce3 = plane_reduce(w3, CUTS3, ra3, rb3, copies_r3)
    reduce_v = vector_reduce(gv, ry, rx, copies_v)
    reduce_o = line_reduce(zo, (0, 64, 144), rc, zo_r1, zo_r2, copies_zo)
    reduce_d = line_reduce(zd, (0, 64, 128), rc.at[:, pl.ds(0, 128)], zd_r1, zd_r2, copies_zd)
    spread_q = line_gather(gq_out, (0, 64, 128), copies_lq, w1.at[y, x, pl.ds(0, 128)])
    spread_u = line_gather(gu_out, (0, 64, 128), copies_lu, w3.at[y, x])
    spread_d = line_gather(gd_out, (0, 32, 64), copies_ld, w2.at[y, x])
    spread_v = line_gather(gv_out, (0, 8, 16), copies_lv, gv.at[y, x])

    outs = []

    def put(src, dst):
        copy = pltpu.make_async_copy(src, dst, sem_o.at[len(outs)])
        copy.start()
        outs.append(copy)

    def scatter(j, target):
        return pltpu.make_async_remote_copy(
            src_ref=proj_weight.at[pl.ds(16 * j, 16)],
            dst_ref=pt,
            send_sem=sem_s.at[0, j],
            recv_sem=sem_s.at[1, 0],
            device_id=(c, target),
            device_id_type=MESH,
        )

    for j in range(8):
        target = (f % 2) * 8 + j

        @pl.when(own_rows & (target != f))
        def _():
            scatter(j, target).start()

        @pl.when(own_rows & (target == f))
        def _():
            local = pltpu.make_async_copy(proj_weight.at[pl.ds(16 * j, 16)], pt, sem_s.at[1, 1])
            local.start()
            local.wait()

    loads[0].wait()
    next(gather_t)
    for i in (3, 4, 5):
        loads[i].wait()

    @pl.when(owner != f)
    def _():
        pltpu.make_async_remote_copy(
            src_ref=pt,
            dst_ref=pt,
            send_sem=sem_s.at[0, 0],
            recv_sem=sem_s.at[1, 0],
            device_id=other_core(),
            device_id_type=MESH,
        ).wait_recv()

    for j, (start, size) in enumerate(PROJ):
        w1[y, x, 128 + 16 * j : 144 + 16 * j, 0:size] = pt[:, start : start + size]
    next(gather1)

    pltpu.make_async_copy(q, q, sem_l.at[6]).wait()
    for m in range(8):
        strip = q[128 * m : 128 * m + 128, :].astype(f32)
        packed = halves_packed(strip[:, :128], strip[:, 128:], odd, lane)
        w3[y, x, :, 128 * m : 128 * m + 128] = packed.astype(bf16)

    in_head = lane % 64
    inverse = jnp.exp((lane % 16).astype(f32) * (-math.log(10000.0) / (ROT_DIMS // 2)))
    inverse = jnp.where(in_head < ROT_DIMS, inverse, 0.0)
    row_angles = lax.broadcasted_iota(jnp.int32, (128, 1), 0).astype(f32) * inverse
    tab[0, 0:128, :] = jnp.cos(row_angles)
    tab[1, 0:128, :] = jnp.sin(row_angles)

    next(gather_t)
    loads[1].wait()
    next(gather_u)
    next(gather1)
    next(gather3)
    next(gather_t)
    next(gather1)
    next(gather3)
    next(gather_u)
    loads[2].wait()
    next(gather1)
    next(gather3)
    next(gather2)
    next(gather_t)

    seg_all = jnp.concatenate(
        [t[b // 2, b % 2, 128:144, 0:128][0:1].astype(f32) for b in range(8)], axis=0
    )
    seg_cols = jnp.transpose(seg_all)
    firsts = [jnp.sum((seg_all < float(d)).astype(f32), keepdims=True) for d in range(1, 4)]
    begins = jnp.zeros((128, 8), f32)
    row = lax.broadcasted_iota(jnp.int32, (32, 1), 0)
    shifts = (row // 4 * 128).astype(f32)
    for d in range(1, 4):
        begins = jnp.where(seg_cols == float(d), firsts[d - 1], begins)
        shifts = shifts - jnp.where(row % 4 == d, firsts[d - 1], 0.0)
    begin_cols[:, 0:8] = begins
    shift_cos, shift_sin = jnp.cos(shifts * inverse), jnp.sin(shifts * inverse)
    row_cos, row_sin = tab[0, 0:128, :], tab[1, 0:128, :]
    for b in range(8):
        rows = pl.ds(b * 128, 128)
        own = seg_cols[:, b : b + 1]
        block_cos, block_sin = shift_cos[4 * b : 4 * b + 1], shift_sin[4 * b : 4 * b + 1]
        for d in range(1, 4):
            at = 4 * b + d
            block_cos = jnp.where(own == float(d), shift_cos[at : at + 1], block_cos)
            block_sin = jnp.where(own == float(d), shift_sin[at : at + 1], block_sin)
        sin = row_sin * block_cos + row_cos * block_sin
        tab[0, rows, :] = row_cos * block_cos - row_sin * block_sin
        tab[1, rows, :] = jnp.where(in_head < 16, -sin, 0.0)
        tab[2, rows, :] = jnp.where((in_head >= 16) & (in_head < 32), sin, 0.0)

    next(gather1)

    vecs[...] = w1[:, :, 176:192, 0:128].reshape(16, 16, 128).astype(f32)

    def joined(which):
        return jnp.concatenate([vecs[i, which : which + 1, :] for i in range(16)], axis=1)

    gain, shift = joined(0), joined(1)

    def bias_rows(which):
        parts = []
        for i in range(2):
            at = which * 16 + c * 2 + i
            parts.append(vecs[at // 3, pl.ds(4 + at % 3, 1), :])
        return jnp.concatenate(parts, axis=1)

    qkv_bias = jnp.concatenate([bias_rows(i) for i in range(3)], axis=1)
    up_parts = []
    for m in range(8):
        a = vecs[2 * m, pl.ds(7 + c // 2, 1), :]
        b = vecs[2 * m + 1, pl.ds(7 + c // 2, 1), :]
        up_parts.append(halves_packed(a, b, odd, lane))
    up_bias = jnp.concatenate(up_parts, axis=1)

    def norm_rows(i, carry):
        b, part = i // 8, i % 8
        values = t[b // 2, b % 2, pl.ds(pl.multiple_of(part * 16, 16), 16), :].astype(f32)
        average = jnp.mean(values, axis=-1, keepdims=True)
        centered = values - average
        variance = jnp.mean(centered * centered, axis=-1, keepdims=True)
        standard = centered * lax.rsqrt(variance + epsilon)
        rows = pl.ds(pl.multiple_of(i % 2 * 16, 16), 16)
        normed = (standard * gain + shift).astype(bf16)
        n[i // 32, i // 16 % 2, i // 2 % 8, rows, :] = normed
        return carry

    lax.fori_loop(0, 64, norm_rows, 0)
    next(gather_u)
    next(gather2)
    next(gather3)

    def project(m, carry):
        rows = pl.ds(pl.multiple_of(m * 512, 512), 512)
        tables = [tab[i, rows, :] for i in range(3)]
        right = w1[:, :, pl.ds(0, 128), :].reshape(WIDTH, 768)
        fields = dot(n[m].reshape(512, WIDTH), right, 1, 0) + qkv_bias
        for which, target in enumerate((q, k, v)):
            for pair in range(2):
                at = which * COLS + pair * 128
                both = fields[:, at : at + 128]
                if which < 2:
                    both = turn(both, *tables)
                if which == 0:
                    both = both * 0.125
                target[rows, pair * 128 : pair * 128 + 128] = both.astype(bf16)
        return carry

    lax.fori_loop(0, 2, project, 0)
    next(gather2)
    next(gather_u)

    grads = jnp.zeros((SEQ, COLS), f32)
    for j, (start, size) in enumerate(PROJ):
        left = u[:, :, :, pl.ds(start, size)].reshape(SEQ, size)
        right = w1[:, :, pl.ds(128 + 16 * j, 16), pl.ds(0, size)].reshape(COLS, size)
        grads = grads + dot(left, right, 1, 1)
    dctx[...] = grads.astype(bf16)

    for block in (3, 2, 1, 0):
        reach = (block + 1) * 256
        rows = pl.ds(block * 256, 256)
        keys = pl.ds(0, reach)
        begin = jnp.concatenate(
            [begin_cols[:, 2 * block + i : 2 * block + i + 1] for i in range(2)], axis=0
        )
        key_index = lax.broadcasted_iota(jnp.int32, (1, reach), 1).astype(f32)
        row_index = (lax.broadcasted_iota(jnp.int32, (256, 1), 0) + block * 256).astype(f32)

        def attend(pair, carry, block=block, rows=rows, keys=keys):
            lanes = pl.ds(pl.multiple_of(pair * 128, 128), 128)
            qp, kp, vp, dp = q[rows, lanes], k[keys, lanes], v[keys, lanes], dctx[rows, lanes]
            results = []
            for half in range(2):
                here = (lane >= 64) == (half == 1)
                qh = jnp.where(here, qp, jnp.zeros((), bf16))
                dh = jnp.where(here, dp, jnp.zeros((), bf16))
                scores = dot(qh, kp, 1, 1)
                allowed = (key_index >= begin) & (key_index <= row_index)
                scores = jnp.where(allowed, scores, masked_score)
                highest = jnp.max(scores, axis=1, keepdims=True)
                weights = jnp.exp(scores - highest)
                total = jnp.sum(weights, axis=1, keepdims=True)
                probs = weights * (1.0 / total)
                log_sum = jnp.broadcast_to(highest + jnp.log(total), (256, 128))
                lse[pl.ds(pair * 2 + half, 1), rows] = jnp.transpose(log_sum)[0:1, :]
                probs_low = probs.astype(bf16)
                d_probs = dot(dh, vp, 1, 1)
                delta = jnp.sum(probs * d_probs, axis=1, keepdims=True)
                d_scores = (probs * (d_probs - delta)).astype(bf16)
                results.append(
                    (
                        dot(probs_low, vp, 1, 0),
                        dot(d_scores, kp, 1, 0),
                        dot(d_scores, qp, 0, 0),
                        dot(probs_low, dp, 0, 0),
                    )
                )
            context, d_queries, d_keys, d_values = [
                jnp.where(lane < 64, a, b) for a, b in zip(*results)
            ]
            ctx[rows, lanes] = context.astype(bf16)
            tables = [tab[i, rows, :] for i in range(3)]
            dproj[rows, lanes] = turn_back(d_queries * 0.125, *tables).astype(bf16)
            if block == 3:
                dk[keys, lanes] = d_keys
                dv[keys, lanes] = d_values
            else:
                dk[keys, lanes] += d_keys
                dv[keys, lanes] += d_values
            return carry

        lax.fori_loop(0, 2, attend, 0)
        if block == 3:
            next(gather2)
        if block == 1:
            next(gather3)

    def join(m, carry):
        rows = pl.ds(pl.multiple_of(m * 256, 256), 256)
        tables = [tab[i, rows, :] for i in range(3)]
        for pair in range(2):
            lanes = pl.ds(pair * 128, 128)
            turned = turn_back(dk[rows, lanes], *tables)
            dproj[rows, pl.ds(COLS + pair * 128, 128)] = turned.astype(bf16)
            dproj[rows, pl.ds(2 * COLS + pair * 128, 128)] = dv[rows, lanes].astype(bf16)
        return carry

    lax.fori_loop(0, 4, join, 0)

    copies1.sent()
    copies_t.sent()

    def normed_part(i, carry):
        columns = pl.ds(pl.multiple_of(i * 512, 512), 512)
        total = dot(dproj[...], w1[i, :, pl.ds(0, 128), :].reshape(512, 768), 1, 1)
        zd[:, :, :, columns] = total.astype(bf16).reshape(4, 2, 128, 512)
        return carry

    lax.fori_loop(0, 4, normed_part, 0)

    def qkv_part(i, carry):
        columns = pl.ds(pl.multiple_of(i * 512, 512), 512)
        grads = dot(n[:, :, :, :, columns].reshape(SEQ, 512), dproj[...], 0, 0).astype(bf16)
        w1[i, :, pl.ds(0, 128), :] = grads.reshape(4, 128, 768)
        return carry

    lax.fori_loop(0, 4, qkv_part, 0)
    for j, (start, size) in enumerate(PROJ):
        columns = pl.ds(start, size)
        part = (slice(None), slice(None), pl.ds(128 + 16 * j, 16), pl.ds(0, size))
        total = dot(ctx[...], w1[part].reshape(COLS, size), 1, 0)
        zo[:, :, pl.ds(0, 128), columns] = total.astype(bf16).reshape(4, 2, 128, size)
        right = u[:, :, :, columns].reshape(SEQ, size)
        w1[part] = dot(ctx[...], right, 0, 0).astype(bf16).reshape(4, 4, 16, size)
    next(reduce1)

    for b in range(8):
        part = jnp.concatenate([lse[j : j + 1, b * 128 : b * 128 + 128] for j in range(4)], axis=1)
        wide = jnp.concatenate([jnp.where(c % 4 == s, part, 0.0) for s in range(4)], axis=1)
        high = wide.astype(bf16).astype(f32)
        at = lax.broadcasted_iota(jnp.int32, (16, 1), 0)
        both = jnp.where(at == c // 4, high, jnp.where(at == 2 + c // 4, wide - high, 0.0))
        zo[b // 2, b % 2, 128:144, :] = both.astype(bf16)

    def feed(i, carry):
        rows = pl.ds(pl.multiple_of(i // 2 * 512, 512), 512)
        columns = pl.ds(pl.multiple_of(i % 2 * 512, 512), 512)
        right = w3[:, :, :, columns].reshape(WIDTH, 512)
        bias = jnp.where(i % 2 == 0, up_bias[:, 0:512], up_bias[:, 512:1024])
        h = dot(n[i // 2].reshape(512, WIDTH), right, 1, 0) + bias
        square = h * h
        tanh = jnp.tanh(0.7978845608028654 * (h + 0.044715 * square * h))
        half = 0.5 * (1.0 + tanh)
        slope = half + 0.5 * h * (1.0 - tanh * tanh) * (
            0.7978845608028654 * (1.0 + 3.0 * 0.044715 * square)
        )
        act[rows, columns] = (h * half).astype(bf16)
        dhid[rows, columns] = slope.astype(bf16)
        return carry

    lax.fori_loop(0, 1, feed, 0)
    next(reduce1)
    lax.fori_loop(1, 3, feed, 0)
    next(reduce1)
    lax.fori_loop(3, 4, feed, 0)

    def feed_back(i, carry):
        rows = pl.ds(pl.multiple_of(i // 2 * 512, 512), 512)
        columns = pl.ds(pl.multiple_of(i % 2 * 512, 512), 512)
        left = u[pl.ds(i // 2 * 2, 2)].reshape(512, WIDTH)
        d_act = dot(left, w2[pl.ds(i % 2 * 2, 2)].reshape(512, WIDTH), 1, 1)
        dhid[rows, columns] = (d_act * dhid[rows, columns].astype(f32)).astype(bf16)
        return carry

    next(gather2)
    lax.fori_loop(0, 2, feed_back, 0)
    next(reduce1)
    lax.fori_loop(2, 4, feed_back, 0)

    def normed_more(i, carry):
        columns = pl.ds(pl.multiple_of(i * 512, 512), 512)
        total = dot(dhid[...], w3[i].reshape(512, UNITS), 1, 1).reshape(4, 2, 128, 512)
        total = total + zd[:, :, :, columns].astype(f32)
        zd[:, :, :, columns] = total.astype(bf16)
        return carry

    lax.fori_loop(0, 4, normed_more, 0)
    next(reduce_d)
    next(reduce1)

    next(spread_q)
    put(w1.at[y, x, pl.ds(0, 128)], gq_out.at[z, core])
    for j, (start, size) in enumerate(PROJ):
        pt[:, start : start + size] = w1[y, x, 128 + 16 * j : 144 + 16 * j, 0:size]

    def to_owner(j):
        return pltpu.make_async_remote_copy(
            src_ref=pt,
            dst_ref=gp.at[pl.ds(16 * j, 16)],
            send_sem=sem_p.at[0, 0],
            recv_sem=sem_p.at[1, j],
            device_id=(c, owner),
            device_id_type=MESH,
        )

    for j in range(8):

        @pl.when((f % 8 == j) & (owner != f))
        def _():
            to_owner(j).start()

        @pl.when((f % 8 == j) & (owner == f))
        def _():
            local = pltpu.make_async_copy(pt, gp.at[pl.ds(16 * j, 16)], sem_p.at[0, 1])
            local.start()
            local.wait()

    copies3.sent()

    def up_part(i, carry):
        columns = pl.ds(pl.multiple_of(i * 512, 512), 512)
        grads = dot(n[:, :, :, :, columns].reshape(SEQ, 512), dhid[...], 0, 0).astype(bf16)
        w3[i] = grads.reshape(4, 128, UNITS)
        return carry

    lax.fori_loop(0, 4, up_part, 0)
    for device in (
        (c, y * 4 + up1(x)),
        (c, y * 4 + down1(x)),
        (c, up1(y) * 4 + x),
        (c, down1(y) * 4 + x),
    ):
        pl.semaphore_signal(n_free, inc=1, device_id=device, device_id_type=MESH)
    next(reduce3)
    next(reduce_d)
    pl.semaphore_signal(rc_free, inc=1, device_id=other_core(), device_id_type=MESH)
    next(spread_q)

    def out_part(i, carry):
        columns = pl.ds(pl.multiple_of(i * 512, 512), 512)
        total = dot(act[...], w2[:, :, :, columns].reshape(UNITS, 512), 1, 0)
        total = total.reshape(4, 2, 128, 512) + zo[:, :, pl.ds(0, 128), columns].astype(f32)
        zo[:, :, pl.ds(0, 128), columns] = total.astype(bf16)
        return carry

    lax.fori_loop(0, 4, out_part, 0)
    pl.semaphore_wait(rc_free, 1)
    next(reduce_o)
    next(reduce3)
    next(reduce_d)
    next(spread_q)

    copies2.sent()

    def down_part(i, carry):
        columns = pl.ds(pl.multiple_of(i * 512, 512), 512)
        right = u[:, :, :, columns].reshape(SEQ, 512)
        w2[:, :, :, columns] = dot(act[...], right, 0, 0).astype(bf16).reshape(4, 4, 64, 512)
        return carry

    lax.fori_loop(0, 4, down_part, 0)
    copies_u.sent()
    own_tokens, own_cot = u.at[0, 0], u.at[0, 1]
    again = [
        pltpu.make_async_copy(tokens, own_tokens, sem_l.at[7]),
        pltpu.make_async_copy(cotangent, own_cot, sem_l.at[8]),
    ]
    for copy in again:
        copy.start()
    pl.semaphore_wait(n_free, 4)
    next(reduce3)
    next(reduce2)
    next(reduce_o)

    for copy in again:
        copy.wait()
    next(reduce_d)
    zero = jnp.zeros((1, WIDTH), f32)

    def finish_grad(i, carry):
        d_gain, d_shift, d_bias = carry
        part = pl.ds(pl.multiple_of(i * 16, 16), 16)
        grads = zd[z, core, part, :].astype(f32)
        grads = grads + zd_r2[0, part, :].astype(f32) + zd_r2[1, part, :].astype(f32)
        values = own_tokens[part, :].astype(f32)
        average = jnp.mean(values, axis=-1, keepdims=True)
        centered = values - average
        variance = jnp.mean(centered * centered, axis=-1, keepdims=True)
        scale = lax.rsqrt(variance + epsilon)
        standard = centered * scale
        d_gain = d_gain + jnp.sum(grads * standard, axis=0, keepdims=True)
        d_shift = d_shift + jnp.sum(grads, axis=0, keepdims=True)
        scaled = grads * gain
        inner = scaled - jnp.mean(scaled, axis=-1, keepdims=True)
        inner = inner - standard * jnp.mean(scaled * standard, axis=-1, keepdims=True)
        upstream = own_cot[part, :].astype(f32)
        d_bias = d_bias + jnp.sum(upstream, axis=0, keepdims=True)
        zd_r2[0, part, :] = (upstream + scale * inner).astype(bf16)
        return d_gain, d_shift, d_bias

    d_gain, d_shift, d_bias = lax.fori_loop(0, 8, finish_grad, (zero, zero, zero))
    put(zd_r2.at[0], token_grad)

    gv[...] = jnp.zeros((4, 4, 16, 128), f32)
    for i in range(16):
        lanes = slice(i * 128, i * 128 + 128)
        gv[i // 4, i % 4, 0:1, :] = d_gain[:, lanes]
        gv[i // 4, i % 4, 1:2, :] = d_shift[:, lanes]
        gv[i // 4, i % 4, 2:3, :] = d_bias[:, lanes]
    ones = jnp.ones((8, SEQ), bf16)
    d_qkv = dot(ones, dproj[...], 1, 0)[0:1, :]
    d_up = dot(ones, dhid[...], 1, 0)[0:1, :]
    for which in range(3):
        for i in range(2):
            at = which * 16 + c * 2 + i
            start = which * COLS + i * 128
            target = at // 3
            gv[target // 4, target % 4, pl.ds(3 + at % 3, 1), :] = d_qkv[:, start : start + 128]
    for m in range(8):
        both = d_up[:, m * 128 : m * 128 + 128]
        moved = pltpu.roll(both, 64, 1)
        here = (lane >= 64) == odd
        for i, (even_place, odd_place) in enumerate(((both, moved), (moved, both))):
            at = 2 * m + i
            term = jnp.where(here, jnp.where(odd, odd_place, even_place), 0.0)
            gv[at // 4, at % 4, pl.ds(6 + c // 2, 1), :] = term
    next(reduce_v)

    def trade(k, src, dst, device):
        return pltpu.make_async_remote_copy(
            src_ref=src,
            dst_ref=dst,
            send_sem=sem_b.at[0, k],
            recv_sem=sem_b.at[1, k],
            device_id=device,
            device_id_type=MESH,
        )

    for j in range(8):

        @pl.when(own_rows & ((f % 2) * 8 + j != f))
        def _():
            slot = gp.at[pl.ds(16 * j, 16)]
            pltpu.make_async_remote_copy(
                src_ref=slot,
                dst_ref=slot,
                send_sem=sem_p.at[0, 0],
                recv_sem=sem_p.at[1, j],
                device_id=other_core(),
                device_id_type=MESH,
            ).wait_recv()

    mine = core == x // 2
    turns = (z - y + 4) % 4
    to_zu, to_zd = (up1(z) * 2 + core, f), (down1(z) * 2 + core, f)
    to_core = other_core()
    h0, h1 = gp.at[pl.ds(0, 64)], gp.at[pl.ds(64, 64)]

    @pl.when(mine & (turns == 0))
    def _():
        trade(0, gp, gp, to_zu).start()
        trade(1, gp, gp, to_zd).start()

    @pl.when(mine & (turns == 1))
    def _():
        trade(0, gp, gp, to_core).wait_recv()
        trade(2, h0, h0, to_zu).start()

    @pl.when(mine & (turns == 3))
    def _():
        trade(1, gp, gp, to_core).wait_recv()
        trade(3, h1, h1, to_zd).start()

    next(spread_q)
    next(reduce_o)
    next(reduce_v)
    next(reduce3)
    next(reduce2)
    next(reduce_v)

    @pl.when(mine & (turns == 2))
    def _():
        trade(2, h0, h0, to_core).wait_recv()
        trade(3, h1, h1, to_core).wait_recv()

    @pl.when(mine)
    def _():
        trade(4, gp, gp, to_core).start()

    next(reduce_o)
    proj_bias, down_bias = joined(2), joined(3)

    def finish_out(i, carry):
        part = pl.ds(pl.multiple_of(i * 16, 16), 16)
        total = zo[z, core, part, :].astype(f32)
        total = total + zo_r2[0, part, :].astype(f32) + zo_r2[1, part, :].astype(f32)
        total = own_tokens[part, :].astype(f32) + total + proj_bias + down_bias
        zo_r2[0, part, :] = total.astype(bf16)
        return carry

    tail = pl.ds(128, 16)
    sums = zo[z, core, tail, :].astype(f32)
    sums = sums + zo_r2[0, tail, :].astype(f32) + zo_r2[1, tail, :].astype(f32)
    sums = sums[0:2, :] + sums[2:4, :]
    for h in range(32):
        lse_own[h : h + 1, :] = sums[h // 16 : h // 16 + 1, (h % 16) * 128 : (h % 16) * 128 + 128]
    lax.fori_loop(0, 8, finish_out, 0)
    put(zo_r2.at[0, pl.ds(0, 128)], block_out)
    put(lse_own, lse_out)

    next(reduce_v)
    next(reduce3)
    next(spread_u)
    put(w3.at[y, x], gu_out.at[z, core])
    next(reduce2)
    next(reduce_v)
    next(spread_v)
    put(gv.at[y, x], gv_out.at[z, core])
    next(spread_u)
    next(reduce2)
    next(spread_v)
    next(spread_u)
    next(reduce2)
    next(spread_d)
    put(w2.at[y, x], gd_out.at[z, core])

    @pl.when(jnp.logical_not(mine))
    def _():
        trade(4, gp, gp, to_core).wait_recv()

    put(gp, gp_out)
    next(spread_v)
    next(spread_d)
    next(spread_u)
    next(spread_v)
    next(spread_d)
    next(spread_d)

    for copies in (
        copies_r1, copies_r2, copies_r3, copies_v, copies_zo, copies_zd,
        copies_lq, copies_lu, copies_ld, copies_lv,
    ):
        copies.sent()
    for j in range(8):
        target = (f % 2) * 8 + j

        @pl.when(own_rows & (target != f))
        def _():
            scatter(j, target).wait_send()

    @pl.when(owner != f)
    def _():
        to_owner(0).wait_send()

    @pl.when(mine & (turns == 0))
    def _():
        trade(0, gp, gp, to_zu).wait_send()
        trade(1, gp, gp, to_zd).wait_send()

    @pl.when(mine & (turns == 1))
    def _():
        trade(2, h0, h0, to_zu).wait_send()

    @pl.when(mine & (turns == 3))
    def _():
        trade(3, h1, h1, to_zd).wait_send()

    @pl.when(mine)
    def _():
        trade(4, gp, gp, to_core).wait_send()

    for copy in outs:
        copy.wait()


def layer_call(*operands):
    anyspace = pl.BlockSpec(memory_space=pl.ANY)
    vmem = pl.BlockSpec(memory_space=VM)
    dma = pltpu.SemaphoreType.DMA
    return pl.pallas_call(
        layer_kernel,
        out_shape=[
            jax.ShapeDtypeStruct((128, WIDTH), bf16),
            jax.ShapeDtypeStruct((128, WIDTH), bf16),
            jax.ShapeDtypeStruct((32, 128), f32),
            jax.ShapeDtypeStruct((4, 2, 128, 768), bf16),
            jax.ShapeDtypeStruct((4, 2, 128, UNITS), bf16),
            jax.ShapeDtypeStruct((4, 2, 64, WIDTH), bf16),
            jax.ShapeDtypeStruct((128, WIDTH), bf16),
            jax.ShapeDtypeStruct((4, 2, 16, 128), f32),
        ],
        in_specs=[anyspace] * 6 + [vmem] * 7,
        out_specs=[anyspace] * 8,
        scratch_shapes=[
            VM((4, 4, 192, 768), bf16),
            VM((4, 4, 64, WIDTH), bf16),
            VM((4, 4, 128, UNITS), bf16),
            VM((4, 2, 144, WIDTH), bf16),
            VM((4, 2, 128, WIDTH), bf16),
            VM((2, 2, 8, 32, WIDTH), bf16),
            VM((4, 2, 128, WIDTH), bf16),
            VM((4, 144, WIDTH), bf16),
            VM((2, 80, WIDTH), bf16),
            VM((2, 144, WIDTH), bf16),
            VM((2, 64, WIDTH), bf16),
            VM((2, 128, WIDTH), bf16),
            VM((2, 8, 96, 768), bf16),
            VM((2, 8, 80, 768), bf16),
            VM((2, 8, 64, UNITS), bf16),
            VM((2, 8, 64, UNITS), bf16),
            VM((16, 16, 128), f32),
            VM((3, SEQ, 128), f32),
            VM((128, 128), f32),
            VM((SEQ, COLS), bf16),
            VM((SEQ, COLS), bf16),
            VM((SEQ, COLS), bf16),
            VM((SEQ, COLS), bf16),
            VM((SEQ, COLS), bf16),
            VM((SEQ, COLS), f32),
            VM((SEQ, COLS), f32),
            VM((SEQ, 768), bf16),
            VM((SEQ, UNITS), bf16),
            VM((SEQ, UNITS), bf16),
            VM((8, SEQ), f32),
            VM((32, 128), f32),
            VM((16, WIDTH), bf16),
            VM((128, WIDTH), bf16),
            VM((4, 4, 16, 128), f32),
            VM((3, 4, 16, 128), f32),
            VM((3, 16, 128), f32),
            dma((2, 16)),
            dma((2, 16)),
            dma((2, 16)),
            dma((2, 8)),
            dma((2, 8)),
            dma((2, 16)),
            dma((2, 16)),
            dma((2, 16)),
            dma((2, 6)),
            dma((2, 5)),
            dma((2, 5)),
            dma((2, 8)),
            dma((2, 8)),
            dma((2, 8)),
            dma((2, 8)),
            dma((2, 8)),
            dma((2, 8)),
            dma((2, 5)),
            dma((9,)),
            dma((8,)),
            pltpu.SemaphoreType.REGULAR,
            pltpu.SemaphoreType.REGULAR,
        ],
        compiler_params=pltpu.CompilerParams(
            collective_id=1, has_side_effects=True, vmem_limit_bytes=62 * 1024 * 1024
        ),
        cost_estimate=pl.CostEstimate(
            flops=45 * 10**9, bytes_accessed=40 * 10**6, transcendentals=4 * 10**6
        ),
        name="layer",
    )(*operands)


def finish_kernel(gq, gu, gd, gp, gv, qkv_out, up_out, down_out, proj_out, vec_out):
    lane = lax.broadcasted_iota(jnp.int32, (1, 128), 1)
    for which in range(3):
        for c in range(8):
            part = gq[c, :, which * COLS : which * COLS + COLS]
            qkv_out[:, which * WIDTH + c * COLS : which * WIDTH + (c + 1) * COLS] = part.astype(f32)
    for pair in range(4):
        for m in range(8):
            a = gu[2 * pair, :, 128 * m : 128 * m + 128].astype(f32)
            b = gu[2 * pair + 1, :, 128 * m : 128 * m + 128].astype(f32)
            for odd in range(2):
                at = (2 * m + odd) * 512 + pair * 128
                up_out[:, at : at + 128] = halves_packed(a, b, odd == 1, lane)
    down_out[...] = gd[0].astype(f32)
    proj_out[...] = gp[...].astype(f32)
    vec_out[...] = jnp.sum(gv[...], axis=0)


def finish_call(gq, gu, gd, gp, gv):
    steps = 4
    rows = 128 // steps
    return pl.pallas_call(
        finish_kernel,
        grid=(steps,),
        out_shape=[
            jax.ShapeDtypeStruct((128, 3 * WIDTH), f32),
            jax.ShapeDtypeStruct((128, HIDDEN), f32),
            jax.ShapeDtypeStruct((512, WIDTH), f32),
            jax.ShapeDtypeStruct((128, WIDTH), f32),
            jax.ShapeDtypeStruct((16, 128), f32),
        ],
        in_specs=[
            pl.BlockSpec((8, rows, 768), lambda i: (0, i, 0)),
            pl.BlockSpec((8, rows, UNITS), lambda i: (0, i, 0)),
            pl.BlockSpec((1, 128, WIDTH), lambda i: (i, 0, 0)),
            pl.BlockSpec((rows, WIDTH), lambda i: (i, 0)),
            pl.BlockSpec((8, 16, 128), lambda i: (0, 0, 0)),
        ],
        out_specs=[
            pl.BlockSpec((rows, 3 * WIDTH), lambda i: (i, 0)),
            pl.BlockSpec((rows, HIDDEN), lambda i: (i, 0)),
            pl.BlockSpec((128, WIDTH), lambda i: (i, 0)),
            pl.BlockSpec((rows, WIDTH), lambda i: (i, 0)),
            pl.BlockSpec((16, 128), lambda i: (0, 0)),
        ],
        compiler_params=pltpu.CompilerParams(vmem_limit_bytes=40 * 1024 * 1024),
        cost_estimate=pl.CostEstimate(
            flops=10**6, bytes_accessed=20 * 10**6, transcendentals=0
        ),
        name="finish",
    )(gq, gu, gd, gp, gv)


def local(
    tokens,
    segments,
    ln_gain,
    ln_shift,
    qkv_weight,
    qkv_bias,
    proj_weight,
    proj_bias,
    up_weight,
    up_bias,
    down_weight,
    down_bias,
    cotangent,
):
    block_out, token_grad, log_sums, gq, gu, gd, gp, gv = layer_call(
        tokens[0],
        cotangent[0],
        qkv_weight,
        proj_weight,
        up_weight,
        down_weight,
        segments,
        ln_gain[None],
        ln_shift[None],
        proj_bias[None],
        down_bias[None],
        qkv_bias[None],
        up_bias[None],
    )
    qkv_grad, up_grad, down_grad, proj_grad, vectors = finish_call(
        gq.reshape(8, 128, 768),
        gu.reshape(8, 128, UNITS),
        gd.reshape(4, 128, WIDTH),
        gp,
        gv.reshape(8, 16, 128),
    )
    return (
        block_out[None],
        token_grad[None],
        log_sums[None],
        vectors[0],
        vectors[1],
        qkv_grad,
        vectors[3:6].reshape(384),
        proj_grad,
        vectors[2],
        up_grad,
        vectors[6:10].reshape(512),
        down_grad,
        vectors[2],
    )


def solution(mesh):
    in_specs = (
        P("fsdp", "ctx", None),
        P("fsdp", "ctx"),
        P("fsdp"),
        P("fsdp"),
        P("fsdp", None),
        P("fsdp"),
        P("fsdp", None),
        P("fsdp"),
        P("fsdp", None),
        P("fsdp"),
        P("fsdp", None),
        P("fsdp"),
        P("fsdp", "ctx", None),
    )
    out_specs = (
        P("fsdp", "ctx", None),
        P("fsdp", "ctx", None),
        P("fsdp", None, "ctx"),
        P("fsdp"),
        P("fsdp"),
        P("fsdp", None),
        P("fsdp"),
        P("fsdp", None),
        P("fsdp"),
        P("fsdp", None),
        P("fsdp"),
        P("fsdp", None),
        P("fsdp"),
    )
    return jax.shard_map(local, mesh=mesh, in_specs=in_specs, out_specs=out_specs, check_vma=False)
```

```python
from functools import partial
import math

import jax
import jax.numpy as jnp
from jax import lax
from jax.experimental import pallas as pl
from jax.experimental.pallas import tpu as pltpu
from jax.sharding import PartitionSpec as P

HEAD = 64
ROT_DIMS = 32
SEQ = 1024
WIDTH = 2048
HIDDEN = 8192
OWN_HEADS = 4
COLS = 256
UNITS = 1024

epsilon = 1e-05
masked_score = -1e30
f32 = jnp.float32
bf16 = jnp.bfloat16
MESH = pl.DeviceIdType.MESH
VM = pltpu.VMEM


def dot(a, b, ca, cb):
    return lax.dot_general(a, b, (((ca,), (cb,)), ((), ())), preferred_element_type=f32)


def place():
    c = lax.axis_index("ctx")
    f = lax.axis_index("fsdp")
    return c, f, c // 2, c % 2, f // 4, f % 4


def other_core():
    c, f, z, core, y, x = place()
    return (z * 2 + 1 - core, f)


def up1(i):
    return (i + 1) % 4


def down1(i):
    return (i + 3) % 4


def over(i):
    return (i + 2) % 4


class Copies:
    def __init__(self, send, recv):
        self.send, self.recv = send, recv
        self.started = []

    def start(self, k, src, dst, device):
        copy = pltpu.make_async_remote_copy(
            src_ref=src,
            dst_ref=dst,
            send_sem=self.send.at[k],
            recv_sem=self.recv.at[k],
            device_id=device,
            device_id_type=MESH,
        )
        copy.start()
        self.started.append(copy)

    def arrived(self, k, dst):
        pltpu.make_async_remote_copy(
            src_ref=dst,
            dst_ref=dst,
            send_sem=self.send.at[k],
            recv_sem=self.recv.at[k],
            device_id=other_core(),
            device_id_type=MESH,
        ).wait_recv()

    def sent(self):
        for copy in self.started:
            copy.wait_send()
        self.started = []


def plane_gather(w, cuts, copies):
    c, f, z, core, y, x = place()
    r0, r1, r2, r3, r4 = cuts
    first, last = pl.ds(r0, r2 - r0), pl.ds(r2, r4 - r2)
    q0, q1, q2, q3 = (pl.ds(a, b - a) for a, b in zip(cuts[:-1], cuts[1:]))
    xu, xd, xo = up1(x), down1(x), over(x)
    yu, yd, yo = up1(y), down1(y), over(y)
    to_xu, to_xd = (c, y * 4 + xu), (c, y * 4 + xd)
    to_yu, to_yd = (c, yu * 4 + x), (c, yd * 4 + x)
    lo, hi = pl.ds(0, 2), pl.ds(2, 2)
    every = pl.ds(0, 4)

    def send(k, part, device):
        copies.start(k, w.at[part], w.at[part], device)

    def got(k, part):
        copies.arrived(k, w.at[part])

    send(0, (y, x, first), to_xu)
    send(1, (y, x, first), to_xd)
    send(2, (y, x, last), to_yu)
    send(3, (y, x, last), to_yd)
    yield
    got(0, (y, xd, first))
    send(4, (y, xd, q0), to_xu)
    got(1, (y, xu, first))
    send(5, (y, xu, q1), to_xd)
    got(2, (yd, x, last))
    send(6, (yd, x, q2), to_yu)
    got(3, (yu, x, last))
    send(7, (yu, x, q3), to_yd)
    yield
    got(4, (y, xo, q0))
    got(5, (y, xo, q1))
    send(8, (y, every, first), to_yu)
    send(9, (y, every, first), to_yd)
    got(6, (yo, x, q2))
    got(7, (yo, x, q3))
    send(10, (every, x, last), to_xu)
    send(11, (every, x, last), to_xd)
    yield
    got(8, (yd, every, first))
    send(12, (yd, lo, first), to_yu)
    got(9, (yu, every, first))
    send(13, (yu, hi, first), to_yd)
    got(10, (every, xd, last))
    send(14, (lo, xd, last), to_xu)
    got(11, (every, xu, last))
    send(15, (hi, xu, last), to_xd)
    yield
    got(12, (yo, lo, first))
    got(13, (yo, hi, first))
    got(14, (lo, xo, last))
    got(15, (hi, xo, last))
    yield


def line_gather(t, cuts, copies, own=None):
    c, f, z, core, y, x = place()
    r0, r1, r2 = cuts
    h0, h1 = pl.ds(r0, r1 - r0), pl.ds(r1, r2 - r1)
    zu, zd, zo = up1(z), down1(z), over(z)
    to_zu, to_zd, to_core = (zu * 2 + core, f), (zd * 2 + core, f), (z * 2 + 1 - core, f)
    other = 1 - core

    def send(k, part, device):
        copies.start(k, t.at[part], t.at[part], device)

    def got(k, part):
        copies.arrived(k, t.at[part])

    mine = t.at[z, core]
    own = mine if own is None else own
    copies.start(0, own, mine, to_zu)
    copies.start(1, own, mine, to_zd)
    copies.start(2, own, mine, to_core)
    yield
    got(0, (zd, core))
    send(3, (zd, core, h0), to_zu)
    got(1, (zu, core))
    send(4, (zu, core, h1), to_zd)
    send(5, (zd, core), to_core)
    send(6, (zu, core), to_core)
    yield
    got(3, (zo, core, h0))
    got(4, (zo, core, h1))
    send(7, (zo, core), to_core)
    yield
    got(2, (z, other))
    got(5, (zd, other))
    got(6, (zu, other))
    got(7, (zo, other))
    yield


def enter():
    c, f, z, core, y, x = place()
    barrier = pltpu.get_barrier_semaphore()
    for device in (
        (c, y * 4 + up1(x)),
        (c, y * 4 + down1(x)),
        (c, up1(y) * 4 + x),
        (c, down1(y) * 4 + x),
        (up1(z) * 2 + core, f),
        (down1(z) * 2 + core, f),
        (z * 2 + 1 - core, f),
    ):
        pl.semaphore_signal(barrier, inc=1, device_id=device, device_id_type=MESH)
    owner = c * 2 + f // 8

    @pl.when(owner != f)
    def _():
        pl.semaphore_signal(barrier, inc=1, device_id=(c, owner), device_id_type=MESH)

    for j in range(8):
        target = (f % 2) * 8 + j

        @pl.when((f // 2 == c) & (target != f))
        def _():
            pl.semaphore_signal(barrier, inc=1, device_id=(c, target), device_id_type=MESH)

    count = 7 + jnp.where(f // 2 == c, jnp.where(f // 8 == f % 2, 7, 8), 0)
    count = count + jnp.where(owner != f, 1, 0)
    pl.semaphore_wait(barrier, count)


def turn(fields, cos, low_sin, high_sin):
    return (
        fields * cos + pltpu.roll(fields, 112, 1) * low_sin + pltpu.roll(fields, 16, 1) * high_sin
    )


def turn_back(grads, cos, low_sin, high_sin):
    return (
        grads * cos + pltpu.roll(grads * low_sin, 16, 1) + pltpu.roll(grads * high_sin, 112, 1)
    )


def halves_packed(a, b, odd, lane):
    moved_a, moved_b = pltpu.roll(a, 64, 1), pltpu.roll(b, 64, 1)
    return jnp.where(lane < 64, jnp.where(odd, moved_a, a), jnp.where(odd, b, moved_b))


def add_into(target, part, *others):
    total = target[part].astype(f32)
    for ref, piece in others:
        total = total + ref[piece].astype(f32)
    target[part] = total.astype(target.dtype)


def plane_reduce(g, cuts, ra, rb, copies):
    c, f, z, core, y, x = place()
    r0, r1, r2, r3, r4 = cuts
    first, last = pl.ds(r0, r2 - r0), pl.ds(r2, r4 - r2)
    q0, q1, q2, q3 = (pl.ds(a, b - a) for a, b in zip(cuts[:-1], cuts[1:]))
    s0, s1, s2, s3 = (pl.ds(0, b - a) for a, b in zip(cuts[:-1], cuts[1:]))
    xu, xd, xo = up1(x), down1(x), over(x)
    yu, yd, yo = up1(y), down1(y), over(y)
    to_xu, to_xd = (c, y * 4 + xu), (c, y * 4 + xd)
    to_yu, to_yd = (c, yu * 4 + x), (c, yd * 4 + x)
    lo, hi, every = pl.ds(0, 2), pl.ds(2, 2), pl.ds(0, 4)
    near, far = pl.ds(0, 2), pl.ds(2, 4)

    def send(k, part, ref, piece, device):
        copies.start(k, g.at[part], ref.at[piece], device)

    def got(k, ref, piece):
        copies.arrived(k, ref.at[piece])

    send(0, (yo, lo, first), ra, (0, near), to_yu)
    send(1, (yo, hi, first), ra, (1, near), to_yd)
    send(2, (lo, xo, last), rb, (0, near), to_xu)
    send(3, (hi, xo, last), rb, (1, near), to_xd)
    yield
    got(0, ra, (0, near))
    add_into(g, (yu, lo, first), (ra, (0, near)))
    send(4, (yu, every, first), ra, (0, far), to_yu)
    got(1, ra, (1, near))
    add_into(g, (yd, hi, first), (ra, (1, near)))
    send(5, (yd, every, first), ra, (1, far), to_yd)
    got(2, rb, (0, near))
    add_into(g, (lo, xu, last), (rb, (0, near)))
    send(6, (every, xu, last), rb, (0, far), to_xu)
    got(3, rb, (1, near))
    add_into(g, (hi, xd, last), (rb, (1, near)))
    send(7, (every, xd, last), rb, (1, far), to_xd)
    yield
    got(4, ra, (0, far))
    got(5, ra, (1, far))
    add_into(g, (y, every, first), (ra, (0, far)), (ra, (1, far)))
    send(8, (y, xo, q0), ra, (0, 6, s0), to_xu)
    send(9, (y, xo, q1), ra, (1, 6, s1), to_xd)
    got(6, rb, (0, far))
    got(7, rb, (1, far))
    add_into(g, (every, x, last), (rb, (0, far)), (rb, (1, far)))
    send(10, (yo, x, q2), rb, (0, 6, s2), to_yu)
    send(11, (yo, x, q3), rb, (1, 6, s3), to_yd)
    yield
    got(8, ra, (0, 6, s0))
    add_into(g, (y, xu, q0), (ra, (0, 6, s0)))
    send(12, (y, xu, first), ra, (0, 7), to_xu)
    got(9, ra, (1, 6, s1))
    add_into(g, (y, xd, q1), (ra, (1, 6, s1)))
    send(13, (y, xd, first), ra, (1, 7), to_xd)
    got(10, rb, (0, 6, s2))
    add_into(g, (yu, x, q2), (rb, (0, 6, s2)))
    send(14, (yu, x, last), rb, (0, 7), to_yu)
    got(11, rb, (1, 6, s3))
    add_into(g, (yd, x, q3), (rb, (1, 6, s3)))
    send(15, (yd, x, last), rb, (1, 7), to_yd)
    yield
    got(12, ra, (0, 7))
    got(13, ra, (1, 7))
    add_into(g, (y, x, first), (ra, (0, 7)), (ra, (1, 7)))
    got(14, rb, (0, 7))
    got(15, rb, (1, 7))
    add_into(g, (y, x, last), (rb, (0, 7)), (rb, (1, 7)))
    yield


def line_reduce(g, cuts, rc, r1, r2, copies):
    c, f, z, core, y, x = place()
    c0, c1, c2 = cuts
    h0, h1 = pl.ds(c0, c1 - c0), pl.ds(c1, c2 - c1)
    s0, s1 = pl.ds(0, c1 - c0), pl.ds(0, c2 - c1)
    zu, zd, zo = up1(z), down1(z), over(z)
    to_zu, to_zd, to_core = (zu * 2 + core, f), (zd * 2 + core, f), (z * 2 + 1 - core, f)
    every = pl.ds(0, 4)
    copies.start(0, g.at[every, 1 - core], rc, to_core)
    yield
    copies.arrived(0, rc)

    def add_row(i, carry):
        add_into(g, (i, core), (rc, (i,)))
        return carry

    lax.fori_loop(0, 4, add_row, 0)
    copies.start(1, g.at[zo, core, h0], r1.at[0, s0], to_zu)
    copies.start(2, g.at[zo, core, h1], r1.at[1, s1], to_zd)
    yield
    copies.arrived(1, r1.at[0, s0])
    add_into(g, (zu, core, h0), (r1, (0, s0)))
    copies.start(3, g.at[zu, core], r2.at[0], to_zu)
    copies.arrived(2, r1.at[1, s1])
    add_into(g, (zd, core, h1), (r1, (1, s1)))
    copies.start(4, g.at[zd, core], r2.at[1], to_zd)
    yield
    copies.arrived(3, r2.at[0])
    copies.arrived(4, r2.at[1])
    yield


def vector_reduce(g, ry, rx, copies):
    c, f, z, core, y, x = place()
    xu, xd, xo = up1(x), down1(x), over(x)
    yu, yd, yo = up1(y), down1(y), over(y)
    to_xu, to_xd = (c, y * 4 + xu), (c, y * 4 + xd)
    to_yu, to_yd = (c, yu * 4 + x), (c, yd * 4 + x)
    copies.start(0, g.at[yo], ry.at[0], to_yu)
    yield
    copies.arrived(0, ry.at[0])
    add_into(g, (yu,), (ry, (0,)))
    copies.start(1, g.at[yu], ry.at[1], to_yu)
    copies.start(2, g.at[yd], ry.at[2], to_yd)
    yield
    copies.arrived(1, ry.at[1])
    copies.arrived(2, ry.at[2])
    add_into(g, (y,), (ry, (1,)), (ry, (2,)))
    copies.start(3, g.at[y, xo], rx.at[0], to_xu)
    yield
    copies.arrived(3, rx.at[0])
    add_into(g, (y, xu), (rx, (0,)))
    copies.start(4, g.at[y, xu], rx.at[1], to_xu)
    copies.start(5, g.at[y, xd], rx.at[2], to_xd)
    yield
    copies.arrived(4, rx.at[1])
    copies.arrived(5, rx.at[2])
    add_into(g, (y, x), (rx, (1,)), (rx, (2,)))
    yield


GATHER1 = (0, 48, 96, 144, 192)
REDUCE1 = (0, 48, 96, 128, 176)
CUTS2 = (0, 16, 32, 48, 64)
CUTS3 = (0, 32, 64, 96, 128)
PROJ = ((0, 768), (768, 768), (1536, 512))


ORDER = (
    "load_t", "gather_t", "load_1", "gather1", "pack", "load_2", "gather2", "gather1", "gather3",
    "gather1", "gather_t", "gather3", "load_u", "gather_u", "gather_t", "gather2", "gather_t",
    "gather1", "gather2", "gather3", "tables", "gather_u", "gather1", "norm", "gather_u",
    "project", "gather_u", "dctx", "att3", "att2", "gather3", "att1", "gather2", "att0", "gp",
    "join", "dn1a", "dn1b", "gqa", "gqb", "gather3", "reduce1", "up_bias", "ff1a", "ff1b", "ff1c",
    "ff1d", "gather2", "reduce1", "ff2a", "ff2b", "ff2c", "ff2d", "dn2a", "dn2b", "reduce_d",
    "sent3", "gua", "reduce1", "gub", "free_n", "reduce3", "reduce_d", "free_rc", "lse",
    "reduce1", "oa", "reduce3", "reduce_d", "ob", "wait_rc", "reduce_o", "sent2", "gda",
    "reduce1", "spread_q", "proj_owner", "gdb", "reload", "wait_n", "reduce2", "reduce_d",
    "reduce_o", "reduce3", "fgrad", "reduce2", "vec", "spread_q", "proj_along", "reduce_o",
    "reduce3", "spread_q", "proj_further", "reduce_v", "reduce2", "reduce3", "reduce_v",
    "spread_u", "put_u", "reduce2", "proj_across", "reduce2", "reduce_v", "spread_d", "put_d",
    "spread_u", "reduce_v", "reduce_o", "fout", "reduce_v", "spread_v", "put_v", "spread_d",
    "spread_u", "spread_v", "spread_u", "spread_d", "spread_v", "spread_q", "spread_d",
    "spread_v", "proj_end",
)


def layer_kernel(
    tokens,
    cotangent,
    qkv_weight,
    proj_weight,
    up_weight,
    down_weight,
    seg,
    gain_in,
    shift_in,
    proj_bias_in,
    down_bias_in,
    qkv_bias_in,
    up_bias_in,
    block_out,
    token_grad,
    lse_out,
    gq_out,
    gu_out,
    gd_out,
    gp_out,
    gv_out,
    w1,
    w2,
    w3,
    t,
    u,
    n,
    zd,
    rc,
    zo_r1,
    zo_r2,
    zd_r1,
    zd_r2,
    ra1,
    rb1,
    ra3,
    rb3,
    vecs,
    tab,
    begin_cols,
    q,
    k,
    v,
    dctx,
    ctx,
    dk,
    dv,
    dproj,
    act,
    dhid,
    lse,
    lse_own,
    pt,
    gp,
    gv,
    ry,
    rx,
    sem1,
    sem2,
    sem3,
    sem_t,
    sem_u,
    sem_r1,
    sem_r2,
    sem_r3,
    sem_v,
    sem_zo,
    sem_zd,
    sem_lq,
    sem_lu,
    sem_ld,
    sem_lv,
    sem_s,
    sem_p,
    sem_b,
    sem_l,
    sem_o,
    n_free,
    rc_free,
):
    c, f, z, core, y, x = place()
    lane = lax.broadcasted_iota(jnp.int32, (1, 128), 1)
    odd = core == 1
    owner = c * 2 + f // 8
    own_rows = f // 2 == c
    zo = t

    loads = [
        pltpu.make_async_copy(tokens, t.at[z, core, pl.ds(0, 128)], sem_l.at[0]),
        pltpu.make_async_copy(cotangent, u.at[z, core], sem_l.at[1]),
        pltpu.make_async_copy(
            down_weight.at[pl.ds(pl.multiple_of(c * 64, 64), 64)], w2.at[y, x], sem_l.at[2]
        ),
    ]
    for i in range(3):
        loads.append(
            pltpu.make_async_copy(
                qkv_weight.at[:, pl.ds(pl.multiple_of(i * WIDTH + c * COLS, 128), COLS)],
                w1.at[y, x, pl.ds(0, 128), pl.ds(i * COLS, COLS)],
                sem_l.at[3 + i],
            )
        )
    for copy in loads:
        copy.start()
    for i in range(16):
        pltpu.make_async_copy(
            up_weight.at[:, pl.ds(pl.multiple_of(i * 512 + (c // 2) * 128, 128), 128)],
            q.at[pl.ds(i // 2 * 128, 128), pl.ds(i % 2 * 128, 128)],
            sem_l.at[6],
        ).start()
    vector_list = [gain_in[...], shift_in[...], proj_bias_in[...], down_bias_in[...]]
    vector_list += [qkv_bias_in[128 * i : 128 * i + 128].reshape(1, 128) for i in range(3)]
    vector_list += [up_bias_in[128 * i : 128 * i + 128].reshape(1, 128) for i in range(4)]
    vector_list = [vector.astype(f32) for vector in vector_list] + [jnp.zeros((5, 128), f32)]
    w1[y, x, 176:192, 0:128] = jnp.concatenate(vector_list, axis=0).astype(bf16)
    w1[y, x, 176:192, 128:768] = jnp.zeros((16, 640), bf16)
    w1[y, x, 160:176, 512:768] = jnp.zeros((16, 256), bf16)
    seg_rows = jnp.broadcast_to(seg[...].astype(f32), (16, 128)).astype(bf16)
    t[z, core, 128:144, 0:128] = seg_rows
    t[z, core, 128:144, 128:WIDTH] = jnp.zeros((16, WIDTH - 128), bf16)

    enter()

    def both_ways(sems):
        return Copies(sems.at[0], sems.at[1])

    copies1, copies2, copies3 = both_ways(sem1), both_ways(sem2), both_ways(sem3)
    copies_t, copies_u = both_ways(sem_t), both_ways(sem_u)
    copies_r1, copies_r2, copies_r3 = both_ways(sem_r1), both_ways(sem_r2), both_ways(sem_r3)
    copies_v = both_ways(sem_v)
    copies_zo, copies_zd = both_ways(sem_zo), both_ways(sem_zd)
    copies_lq, copies_lu = both_ways(sem_lq), both_ways(sem_lu)
    copies_ld, copies_lv = both_ways(sem_ld), both_ways(sem_lv)
    gather1 = plane_gather(w1, GATHER1, copies1)
    gather2 = plane_gather(w2, CUTS2, copies2)
    gather3 = plane_gather(w3, CUTS3, copies3)
    gather_t = line_gather(t, (0, 64, 144), copies_t)
    gather_u = line_gather(u, (0, 64, 128), copies_u)
    reduce1 = plane_reduce(w1, REDUCE1, ra1, rb1, copies_r1)
    reduce2 = plane_reduce(w2, CUTS2, n.at[0], n.at[1], copies_r2)
    reduce3 = plane_reduce(w3, CUTS3, ra3, rb3, copies_r3)
    reduce_v = vector_reduce(gv, ry, rx, copies_v)
    reduce_o = line_reduce(zo, (0, 64, 144), rc, zo_r1, zo_r2, copies_zo)
    reduce_d = line_reduce(zd, (0, 64, 128), rc.at[:, pl.ds(0, 128)], zd_r1, zd_r2, copies_zd)
    spread_q = line_gather(gq_out, (0, 64, 128), copies_lq, w1.at[y, x, pl.ds(0, 128)])
    spread_u = line_gather(gu_out, (0, 64, 128), copies_lu, w3.at[y, x])
    spread_d = line_gather(gd_out, (0, 32, 64), copies_ld, w2.at[y, x])
    spread_v = line_gather(gv_out, (0, 8, 16), copies_lv, gv.at[y, x])

    outs = []

    def put(src, dst):
        copy = pltpu.make_async_copy(src, dst, sem_o.at[len(outs)])
        copy.start()
        outs.append(copy)

    kept = {}

    def scatter(j, target):
        return pltpu.make_async_remote_copy(
            src_ref=proj_weight.at[pl.ds(16 * j, 16)],
            dst_ref=pt,
            send_sem=sem_s.at[0, j],
            recv_sem=sem_s.at[1, 0],
            device_id=(c, target),
            device_id_type=MESH,
        )

    def load_1():
        for j in range(8):
            target = (f % 2) * 8 + j

            @pl.when(own_rows & (target != f))
            def _():
                scatter(j, target).start()

            @pl.when(own_rows & (target == f))
            def _():
                local = pltpu.make_async_copy(
                    proj_weight.at[pl.ds(16 * j, 16)], pt, sem_s.at[1, 1]
                )
                local.start()
                local.wait()

        for i in (3, 4, 5):
            loads[i].wait()

        @pl.when(owner != f)
        def _():
            pltpu.make_async_remote_copy(
                src_ref=pt,
                dst_ref=pt,
                send_sem=sem_s.at[0, 0],
                recv_sem=sem_s.at[1, 0],
                device_id=other_core(),
                device_id_type=MESH,
            ).wait_recv()

        for j, (start, size) in enumerate(PROJ):
            w1[y, x, 128 + 16 * j : 144 + 16 * j, 0:size] = pt[:, start : start + size]

    def pack():
        pltpu.make_async_copy(q, q, sem_l.at[6]).wait()
        for m in range(8):
            strip = q[128 * m : 128 * m + 128, :].astype(f32)
            packed = halves_packed(strip[:, :128], strip[:, 128:], odd, lane)
            w3[y, x, :, 128 * m : 128 * m + 128] = packed.astype(bf16)

    def tables():
        in_head = lane % 64
        inverse = jnp.exp((lane % 16).astype(f32) * (-math.log(10000.0) / (ROT_DIMS // 2)))
        inverse = jnp.where(in_head < ROT_DIMS, inverse, 0.0)
        row_angles = lax.broadcasted_iota(jnp.int32, (128, 1), 0).astype(f32) * inverse
        row_cos, row_sin = jnp.cos(row_angles), jnp.sin(row_angles)
        seg_all = jnp.concatenate(
            [t[b // 2, b % 2, 128:144, 0:128][0:1].astype(f32) for b in range(8)], axis=0
        )
        seg_cols = jnp.transpose(seg_all)
        firsts = [jnp.sum((seg_all < float(d)).astype(f32), keepdims=True) for d in range(1, 4)]
        begins = jnp.zeros((128, 8), f32)
        row = lax.broadcasted_iota(jnp.int32, (32, 1), 0)
        shifts = (row // 4 * 128).astype(f32)
        for d in range(1, 4):
            begins = jnp.where(seg_cols == float(d), firsts[d - 1], begins)
            shifts = shifts - jnp.where(row % 4 == d, firsts[d - 1], 0.0)
        begin_cols[:, 0:8] = begins
        shift_cos, shift_sin = jnp.cos(shifts * inverse), jnp.sin(shifts * inverse)
        for b in range(8):
            rows = pl.ds(b * 128, 128)
            own = seg_cols[:, b : b + 1]
            block_cos, block_sin = shift_cos[4 * b : 4 * b + 1], shift_sin[4 * b : 4 * b + 1]
            for d in range(1, 4):
                at = 4 * b + d
                block_cos = jnp.where(own == float(d), shift_cos[at : at + 1], block_cos)
                block_sin = jnp.where(own == float(d), shift_sin[at : at + 1], block_sin)
            sin = row_sin * block_cos + row_cos * block_sin
            tab[0, rows, :] = row_cos * block_cos - row_sin * block_sin
            tab[1, rows, :] = jnp.where(in_head < 16, -sin, 0.0)
            tab[2, rows, :] = jnp.where((in_head >= 16) & (in_head < 32), sin, 0.0)

    def joined(which):
        return jnp.concatenate([vecs[i, which : which + 1, :] for i in range(16)], axis=1)

    def norm():
        vecs[...] = w1[:, :, 176:192, 0:128].reshape(16, 16, 128).astype(f32)
        gain, shift = joined(0), joined(1)

        def norm_rows(i, carry):
            b, part = i // 2, i % 2
            values = t[b // 2, b % 2, pl.ds(pl.multiple_of(part * 64, 64), 64), :].astype(f32)
            average = jnp.mean(values, axis=-1, keepdims=True)
            centered = values - average
            variance = jnp.mean(centered * centered, axis=-1, keepdims=True)
            standard = centered * lax.rsqrt(variance + epsilon)
            normed = (standard * gain + shift).astype(bf16)
            n[i // 8, i // 4 % 2, pl.ds(i % 4 * 2, 2)] = normed.reshape(2, 32, WIDTH)
            return carry

        lax.fori_loop(0, 16, norm_rows, 0)

    def project():
        parts = []
        for which in range(3):
            for i in range(2):
                at = which * 16 + c * 2 + i
                parts.append(vecs[at // 3, pl.ds(4 + at % 3, 1), :])
        qkv_bias = jnp.concatenate(parts, axis=1)

        def project_rows(m, carry):
            rows = pl.ds(pl.multiple_of(m * 512, 512), 512)
            turns = [tab[i, rows, :] for i in range(3)]
            right = w1[:, :, pl.ds(0, 128), :].reshape(WIDTH, 768)
            fields = dot(n[m].reshape(512, WIDTH), right, 1, 0) + qkv_bias
            for which, target in enumerate((q, k, v)):
                for pair in range(2):
                    at = which * COLS + pair * 128
                    both = fields[:, at : at + 128]
                    if which < 2:
                        both = turn(both, *turns)
                    if which == 0:
                        both = both * 0.125
                    target[rows, pair * 128 : pair * 128 + 128] = both.astype(bf16)
            return carry

        lax.fori_loop(0, 2, project_rows, 0)

    def context_grad():
        grads = jnp.zeros((SEQ, COLS), f32)
        for j, (start, size) in enumerate(PROJ):
            left = u[:, :, :, pl.ds(start, size)].reshape(SEQ, size)
            right = w1[:, :, pl.ds(128 + 16 * j, 16), pl.ds(0, size)].reshape(COLS, size)
            grads = grads + dot(left, right, 1, 1)
        dctx[...] = grads.astype(bf16)

    def attention(block):
        reach = (block + 1) * 256
        rows = pl.ds(block * 256, 256)
        keys = pl.ds(0, reach)
        begin = jnp.concatenate(
            [begin_cols[:, 2 * block + i : 2 * block + i + 1] for i in range(2)], axis=0
        )
        key_index = lax.broadcasted_iota(jnp.int32, (1, reach), 1).astype(f32)
        row_index = (lax.broadcasted_iota(jnp.int32, (256, 1), 0) + block * 256).astype(f32)

        def attend(pair, carry):
            lanes = pl.ds(pl.multiple_of(pair * 128, 128), 128)
            qp, kp, vp, dp = q[rows, lanes], k[keys, lanes], v[keys, lanes], dctx[rows, lanes]
            results = []
            for half in range(2):
                here = (lane >= 64) == (half == 1)
                qh = jnp.where(here, qp, jnp.zeros((), bf16))
                dh = jnp.where(here, dp, jnp.zeros((), bf16))
                scores = dot(qh, kp, 1, 1)
                allowed = (key_index >= begin) & (key_index <= row_index)
                scores = jnp.where(allowed, scores, masked_score)
                highest = jnp.max(scores, axis=1, keepdims=True)
                weights = jnp.exp(scores - highest)
                total = jnp.sum(weights, axis=1, keepdims=True)
                probs = weights * (1.0 / total)
                log_sum = jnp.broadcast_to(highest + jnp.log(total), (256, 128))
                lse[pl.ds(pair * 2 + half, 1), rows] = jnp.transpose(log_sum)[0:1, :]
                probs_low = probs.astype(bf16)
                d_probs = dot(dh, vp, 1, 1)
                delta = jnp.sum(probs * d_probs, axis=1, keepdims=True)
                d_scores = (probs * (d_probs - delta)).astype(bf16)
                results.append(
                    (
                        dot(probs_low, vp, 1, 0),
                        dot(d_scores, kp, 1, 0),
                        dot(d_scores, qp, 0, 0),
                        dot(probs_low, dp, 0, 0),
                    )
                )
            context, d_queries, d_keys, d_values = [
                jnp.where(lane < 64, a, b) for a, b in zip(*results)
            ]
            ctx[rows, lanes] = context.astype(bf16)
            turns = [tab[i, rows, :] for i in range(3)]
            dproj[rows, lanes] = turn_back(d_queries * 0.125, *turns).astype(bf16)
            if block == 3:
                dk[keys, lanes] = d_keys
                dv[keys, lanes] = d_values
            else:
                dk[keys, lanes] += d_keys
                dv[keys, lanes] += d_values
            return carry

        lax.fori_loop(0, 2, attend, 0)

    def join():
        def join_rows(m, carry):
            rows = pl.ds(pl.multiple_of(m * 256, 256), 256)
            turns = [tab[i, rows, :] for i in range(3)]
            for pair in range(2):
                lanes = pl.ds(pair * 128, 128)
                turned = turn_back(dk[rows, lanes], *turns)
                dproj[rows, pl.ds(COLS + pair * 128, 128)] = turned.astype(bf16)
                dproj[rows, pl.ds(2 * COLS + pair * 128, 128)] = dv[rows, lanes].astype(bf16)
            return carry

        lax.fori_loop(0, 4, join_rows, 0)

    def normed_part(i, carry):
        columns = pl.ds(pl.multiple_of(i * 512, 512), 512)
        total = dot(dproj[...], w1[i, :, pl.ds(0, 128), :].reshape(512, 768), 1, 1)
        zd[:, :, :, columns] = total.astype(bf16).reshape(4, 2, 128, 512)
        return carry

    def qkv_part(i, carry):
        columns = pl.ds(pl.multiple_of(i * 512, 512), 512)
        grads = dot(n[:, :, :, :, columns].reshape(SEQ, 512), dproj[...], 0, 0).astype(bf16)
        w1[i, :, pl.ds(0, 128), :] = grads.reshape(4, 128, 768)
        return carry

    def proj_part():
        copies1.sent()
        copies_t.sent()
        for j, (start, size) in enumerate(PROJ):
            columns = pl.ds(start, size)
            part = (slice(None), slice(None), pl.ds(128 + 16 * j, 16), pl.ds(0, size))
            total = dot(ctx[...], w1[part].reshape(COLS, size), 1, 0)
            zo[:, :, pl.ds(0, 128), columns] = total.astype(bf16).reshape(4, 2, 128, size)
            right = u[:, :, :, columns].reshape(SEQ, size)
            w1[part] = dot(ctx[...], right, 0, 0).astype(bf16).reshape(4, 4, 16, size)

    def log_sums():
        for b in range(8):
            part = jnp.concatenate(
                [lse[j : j + 1, b * 128 : b * 128 + 128] for j in range(4)], axis=1
            )
            wide = jnp.concatenate([jnp.where(c % 4 == s, part, 0.0) for s in range(4)], axis=1)
            high = wide.astype(bf16).astype(f32)
            at = lax.broadcasted_iota(jnp.int32, (16, 1), 0)
            both = jnp.where(at == c // 4, high, jnp.where(at == 2 + c // 4, wide - high, 0.0))
            zo[b // 2, b % 2, 128:144, :] = both.astype(bf16)

    def feed(i, carry):
        rows = pl.ds(pl.multiple_of(i // 2 * 512, 512), 512)
        columns = pl.ds(pl.multiple_of(i % 2 * 512, 512), 512)
        right = w3[:, :, :, columns].reshape(WIDTH, 512)
        bias = jnp.where(i % 2 == 0, kept["up_bias"][:, 0:512], kept["up_bias"][:, 512:1024])
        h = dot(n[i // 2].reshape(512, WIDTH), right, 1, 0) + bias
        square = h * h
        tanh = jnp.tanh(0.7978845608028654 * (h + 0.044715 * square * h))
        half = 0.5 * (1.0 + tanh)
        slope = half + 0.5 * h * (1.0 - tanh * tanh) * (
            0.7978845608028654 * (1.0 + 3.0 * 0.044715 * square)
        )
        act[rows, columns] = (h * half).astype(bf16)
        dhid[rows, columns] = slope.astype(bf16)
        return carry

    def up_bias():
        parts = []
        for m in range(8):
            a = vecs[2 * m, pl.ds(7 + c // 2, 1), :]
            b = vecs[2 * m + 1, pl.ds(7 + c // 2, 1), :]
            parts.append(halves_packed(a, b, odd, lane))
        kept["up_bias"] = jnp.concatenate(parts, axis=1)

    def feed_back(i, carry):
        rows = pl.ds(pl.multiple_of(i // 2 * 512, 512), 512)
        columns = pl.ds(pl.multiple_of(i % 2 * 512, 512), 512)
        left = u[pl.ds(i // 2 * 2, 2)].reshape(512, WIDTH)
        d_act = dot(left, w2[pl.ds(i % 2 * 2, 2)].reshape(512, WIDTH), 1, 1)
        dhid[rows, columns] = (d_act * dhid[rows, columns].astype(f32)).astype(bf16)
        return carry

    def normed_more(i, carry):
        columns = pl.ds(pl.multiple_of(i * 512, 512), 512)
        total = dot(dhid[...], w3[i].reshape(512, UNITS), 1, 1).reshape(4, 2, 128, 512)
        total = total + zd[:, :, :, columns].astype(f32)
        zd[:, :, :, columns] = total.astype(bf16)
        return carry

    def up_part(i, carry):
        columns = pl.ds(pl.multiple_of(i * 512, 512), 512)
        grads = dot(n[:, :, :, :, columns].reshape(SEQ, 512), dhid[...], 0, 0).astype(bf16)
        w3[i] = grads.reshape(4, 128, UNITS)
        return carry

    def free_n():
        for device in (
            (c, y * 4 + up1(x)),
            (c, y * 4 + down1(x)),
            (c, up1(y) * 4 + x),
            (c, down1(y) * 4 + x),
        ):
            pl.semaphore_signal(n_free, inc=1, device_id=device, device_id_type=MESH)

    def free_rc():
        pl.semaphore_signal(rc_free, inc=1, device_id=other_core(), device_id_type=MESH)

    def out_part(i, carry):
        columns = pl.ds(pl.multiple_of(i * 512, 512), 512)
        total = dot(act[...], w2[:, :, :, columns].reshape(UNITS, 512), 1, 0)
        total = total.reshape(4, 2, 128, 512) + zo[:, :, pl.ds(0, 128), columns].astype(f32)
        zo[:, :, pl.ds(0, 128), columns] = total.astype(bf16)
        return carry

    def down_part(i, carry):
        columns = pl.ds(pl.multiple_of(i * 512, 512), 512)
        right = u[:, :, :, columns].reshape(SEQ, 512)
        w2[:, :, :, columns] = dot(act[...], right, 0, 0).astype(bf16).reshape(4, 4, 64, 512)
        return carry

    own_tokens, own_cot = u.at[0, 0], u.at[0, 1]
    again = [
        pltpu.make_async_copy(tokens, own_tokens, sem_l.at[7]),
        pltpu.make_async_copy(cotangent, own_cot, sem_l.at[8]),
    ]

    def reload():
        copies_u.sent()
        for copy in again:
            copy.start()

    def finish_grad():
        for copy in again:
            copy.wait()
        gain = joined(0)
        zero = jnp.zeros((1, WIDTH), f32)

        def finish_rows(i, carry):
            d_gain, d_shift, d_bias = carry
            part = pl.ds(pl.multiple_of(i * 32, 32), 32)
            grads = zd[z, core, part, :].astype(f32)
            grads = grads + zd_r2[0, part, :].astype(f32) + zd_r2[1, part, :].astype(f32)
            values = own_tokens[part, :].astype(f32)
            average = jnp.mean(values, axis=-1, keepdims=True)
            centered = values - average
            variance = jnp.mean(centered * centered, axis=-1, keepdims=True)
            scale = lax.rsqrt(variance + epsilon)
            standard = centered * scale
            d_gain = d_gain + jnp.sum(grads * standard, axis=0, keepdims=True)
            d_shift = d_shift + jnp.sum(grads, axis=0, keepdims=True)
            scaled = grads * gain
            inner = scaled - jnp.mean(scaled, axis=-1, keepdims=True)
            inner = inner - standard * jnp.mean(scaled * standard, axis=-1, keepdims=True)
            upstream = own_cot[part, :].astype(f32)
            d_bias = d_bias + jnp.sum(upstream, axis=0, keepdims=True)
            zd_r2[0, part, :] = (upstream + scale * inner).astype(bf16)
            return d_gain, d_shift, d_bias

        kept["sums"] = lax.fori_loop(0, 4, finish_rows, (zero, zero, zero))
        put(zd_r2.at[0], token_grad)

    def vector_terms():
        gv[...] = jnp.zeros((4, 4, 16, 128), f32)
        for i in range(16):
            lanes = slice(i * 128, i * 128 + 128)
            for at, sums in enumerate(kept["sums"]):
                gv[i // 4, i % 4, at : at + 1, :] = sums[:, lanes]
        ones = jnp.ones((8, SEQ), bf16)
        d_qkv = dot(ones, dproj[...], 1, 0)[0:1, :]
        d_up = dot(ones, dhid[...], 1, 0)[0:1, :]
        for which in range(3):
            for i in range(2):
                at = which * 16 + c * 2 + i
                start = which * COLS + i * 128
                target = at // 3
                term = d_qkv[:, start : start + 128]
                gv[target // 4, target % 4, pl.ds(3 + at % 3, 1), :] = term
        for m in range(8):
            both = d_up[:, m * 128 : m * 128 + 128]
            moved = pltpu.roll(both, 64, 1)
            here = (lane >= 64) == odd
            for i, (even_place, odd_place) in enumerate(((both, moved), (moved, both))):
                at = 2 * m + i
                term = jnp.where(here, jnp.where(odd, odd_place, even_place), 0.0)
                gv[at // 4, at % 4, pl.ds(6 + c // 2, 1), :] = term

    def to_owner(j):
        return pltpu.make_async_remote_copy(
            src_ref=pt,
            dst_ref=gp.at[pl.ds(16 * j, 16)],
            send_sem=sem_p.at[0, 0],
            recv_sem=sem_p.at[1, j],
            device_id=(c, owner),
            device_id_type=MESH,
        )

    def trade(k, src, dst, device):
        return pltpu.make_async_remote_copy(
            src_ref=src,
            dst_ref=dst,
            send_sem=sem_b.at[0, k],
            recv_sem=sem_b.at[1, k],
            device_id=device,
            device_id_type=MESH,
        )

    mine = core == x // 2
    turns_z = (z - y + 4) % 4
    to_zu, to_zd = (up1(z) * 2 + core, f), (down1(z) * 2 + core, f)
    to_core = other_core()
    h0, h1 = gp.at[pl.ds(0, 64)], gp.at[pl.ds(64, 64)]

    def proj_owner():
        put(w1.at[y, x, pl.ds(0, 128)], gq_out.at[z, core])
        for j, (start, size) in enumerate(PROJ):
            pt[:, start : start + size] = w1[y, x, 128 + 16 * j : 144 + 16 * j, 0:size]
        for j in range(8):

            @pl.when((f % 8 == j) & (owner != f))
            def _():
                to_owner(j).start()

            @pl.when((f % 8 == j) & (owner == f))
            def _():
                local = pltpu.make_async_copy(pt, gp.at[pl.ds(16 * j, 16)], sem_p.at[0, 1])
                local.start()
                local.wait()

    def proj_along():
        for j in range(8):

            @pl.when(own_rows & ((f % 2) * 8 + j != f))
            def _():
                slot = gp.at[pl.ds(16 * j, 16)]
                pltpu.make_async_remote_copy(
                    src_ref=slot,
                    dst_ref=slot,
                    send_sem=sem_p.at[0, 0],
                    recv_sem=sem_p.at[1, j],
                    device_id=other_core(),
                    device_id_type=MESH,
                ).wait_recv()

        @pl.when(mine & (turns_z == 0))
        def _():
            trade(0, gp, gp, to_zu).start()
            trade(1, gp, gp, to_zd).start()

    def proj_further():
        @pl.when(mine & (turns_z == 1))
        def _():
            trade(0, gp, gp, to_core).wait_recv()
            trade(2, h0, h0, to_zu).start()

        @pl.when(mine & (turns_z == 3))
        def _():
            trade(1, gp, gp, to_core).wait_recv()
            trade(3, h1, h1, to_zd).start()

    def proj_across():
        @pl.when(mine & (turns_z == 2))
        def _():
            trade(2, h0, h0, to_core).wait_recv()
            trade(3, h1, h1, to_core).wait_recv()

        @pl.when(mine)
        def _():
            trade(4, gp, gp, to_core).start()

    def proj_end():
        @pl.when(jnp.logical_not(mine))
        def _():
            trade(4, gp, gp, to_core).wait_recv()

        put(gp, gp_out)

    def finish_out():
        proj_bias, down_bias = joined(2), joined(3)
        tail = pl.ds(128, 16)
        sums = zo[z, core, tail, :].astype(f32)
        sums = sums + zo_r2[0, tail, :].astype(f32) + zo_r2[1, tail, :].astype(f32)
        sums = sums[0:2, :] + sums[2:4, :]
        for h in range(32):
            lanes = slice((h % 16) * 128, (h % 16) * 128 + 128)
            lse_own[h : h + 1, :] = sums[h // 16 : h // 16 + 1, lanes]

        def finish_rows(i, carry):
            part = pl.ds(pl.multiple_of(i * 32, 32), 32)
            total = zo[z, core, part, :].astype(f32)
            total = total + zo_r2[0, part, :].astype(f32) + zo_r2[1, part, :].astype(f32)
            total = own_tokens[part, :].astype(f32) + total + proj_bias + down_bias
            zo_r2[0, part, :] = total.astype(bf16)
            return carry

        lax.fori_loop(0, 4, finish_rows, 0)
        put(zo_r2.at[0, pl.ds(0, 128)], block_out)
        put(lse_own, lse_out)

    def loop(first, last, body):
        return lambda: lax.fori_loop(first, last, body, 0)

    actions = dict(
        gather1=gather1,
        gather2=gather2,
        gather3=gather3,
        gather_t=gather_t,
        gather_u=gather_u,
        reduce1=reduce1,
        reduce2=reduce2,
        reduce3=reduce3,
        reduce_o=reduce_o,
        reduce_d=reduce_d,
        reduce_v=reduce_v,
        spread_q=spread_q,
        spread_u=spread_u,
        spread_d=spread_d,
        spread_v=spread_v,
        load_t=loads[0].wait,
        load_u=loads[1].wait,
        load_2=loads[2].wait,
        load_1=load_1,
        pack=pack,
        tables=tables,
        norm=norm,
        up_bias=up_bias,
        project=project,
        dctx=context_grad,
        att3=lambda: attention(3),
        att2=lambda: attention(2),
        att1=lambda: attention(1),
        att0=lambda: attention(0),
        join=join,
        dn1a=loop(0, 2, normed_part),
        dn1b=loop(2, 4, normed_part),
        gqa=loop(0, 2, qkv_part),
        gqb=loop(2, 4, qkv_part),
        gp=proj_part,
        lse=log_sums,
        ff1a=loop(0, 1, feed),
        ff1b=loop(1, 2, feed),
        ff1c=loop(2, 3, feed),
        ff1d=loop(3, 4, feed),
        ff1=loop(0, 4, feed),
        ff2a=loop(0, 1, feed_back),
        ff2b=loop(1, 2, feed_back),
        ff2c=loop(2, 3, feed_back),
        ff2d=loop(3, 4, feed_back),
        ff2=loop(0, 4, feed_back),
        dn2a=loop(0, 2, normed_more),
        dn2b=loop(2, 4, normed_more),
        sent3=copies3.sent,
        gua=loop(0, 2, up_part),
        gub=loop(2, 4, up_part),
        free_n=free_n,
        free_rc=free_rc,
        oa=loop(0, 2, out_part),
        ob=loop(2, 4, out_part),
        wait_rc=lambda: pl.semaphore_wait(rc_free, 1),
        sent2=copies2.sent,
        gda=loop(0, 2, down_part),
        gdb=loop(2, 4, down_part),
        reload=reload,
        wait_n=lambda: pl.semaphore_wait(n_free, 4),
        fgrad=finish_grad,
        vec=vector_terms,
        proj_owner=proj_owner,
        proj_along=proj_along,
        proj_further=proj_further,
        proj_across=proj_across,
        proj_end=proj_end,
        fout=finish_out,
        put_u=lambda: put(w3.at[y, x], gu_out.at[z, core]),
        put_d=lambda: put(w2.at[y, x], gd_out.at[z, core]),
        put_v=lambda: put(gv.at[y, x], gv_out.at[z, core]),
    )
    for name in ORDER:
        action = actions[name]
        if callable(action):
            action()
        else:
            next(action)

    for copies in (
        copies_r1, copies_r2, copies_r3, copies_v, copies_zo, copies_zd,
        copies_lq, copies_lu, copies_ld, copies_lv,
    ):
        copies.sent()
    for j in range(8):
        target = (f % 2) * 8 + j

        @pl.when(own_rows & (target != f))
        def _():
            scatter(j, target).wait_send()

    @pl.when(owner != f)
    def _():
        to_owner(0).wait_send()

    @pl.when(mine & (turns_z == 0))
    def _():
        trade(0, gp, gp, to_zu).wait_send()
        trade(1, gp, gp, to_zd).wait_send()

    @pl.when(mine & (turns_z == 1))
    def _():
        trade(2, h0, h0, to_zu).wait_send()

    @pl.when(mine & (turns_z == 3))
    def _():
        trade(3, h1, h1, to_zd).wait_send()

    @pl.when(mine)
    def _():
        trade(4, gp, gp, to_core).wait_send()

    for copy in outs:
        copy.wait()


def layer_call(*operands):
    anyspace = pl.BlockSpec(memory_space=pl.ANY)
    vmem = pl.BlockSpec(memory_space=VM)
    dma = pltpu.SemaphoreType.DMA
    return pl.pallas_call(
        layer_kernel,
        out_shape=[
            jax.ShapeDtypeStruct((128, WIDTH), bf16),
            jax.ShapeDtypeStruct((128, WIDTH), bf16),
            jax.ShapeDtypeStruct((32, 128), f32),
            jax.ShapeDtypeStruct((4, 2, 128, 768), bf16),
            jax.ShapeDtypeStruct((4, 2, 128, UNITS), bf16),
            jax.ShapeDtypeStruct((4, 2, 64, WIDTH), bf16),
            jax.ShapeDtypeStruct((128, WIDTH), bf16),
            jax.ShapeDtypeStruct((4, 2, 16, 128), f32),
        ],
        in_specs=[anyspace] * 6 + [vmem] * 7,
        out_specs=[anyspace] * 8,
        scratch_shapes=[
            VM((4, 4, 192, 768), bf16),
            VM((4, 4, 64, WIDTH), bf16),
            VM((4, 4, 128, UNITS), bf16),
            VM((4, 2, 144, WIDTH), bf16),
            VM((4, 2, 128, WIDTH), bf16),
            VM((2, 2, 8, 32, WIDTH), bf16),
            VM((4, 2, 128, WIDTH), bf16),
            VM((4, 144, WIDTH), bf16),
            VM((2, 80, WIDTH), bf16),
            VM((2, 144, WIDTH), bf16),
            VM((2, 64, WIDTH), bf16),
            VM((2, 128, WIDTH), bf16),
            VM((2, 8, 96, 768), bf16),
            VM((2, 8, 80, 768), bf16),
            VM((2, 8, 64, UNITS), bf16),
            VM((2, 8, 64, UNITS), bf16),
            VM((16, 16, 128), f32),
            VM((3, SEQ, 128), f32),
            VM((128, 128), f32),
            VM((SEQ, COLS), bf16),
            VM((SEQ, COLS), bf16),
            VM((SEQ, COLS), bf16),
            VM((SEQ, COLS), bf16),
            VM((SEQ, COLS), bf16),
            VM((SEQ, COLS), f32),
            VM((SEQ, COLS), f32),
            VM((SEQ, 768), bf16),
            VM((SEQ, UNITS), bf16),
            VM((SEQ, UNITS), bf16),
            VM((8, SEQ), f32),
            VM((32, 128), f32),
            VM((16, WIDTH), bf16),
            VM((128, WIDTH), bf16),
            VM((4, 4, 16, 128), f32),
            VM((3, 4, 16, 128), f32),
            VM((3, 16, 128), f32),
            dma((2, 16)),
            dma((2, 16)),
            dma((2, 16)),
            dma((2, 8)),
            dma((2, 8)),
            dma((2, 16)),
            dma((2, 16)),
            dma((2, 16)),
            dma((2, 6)),
            dma((2, 5)),
            dma((2, 5)),
            dma((2, 8)),
            dma((2, 8)),
            dma((2, 8)),
            dma((2, 8)),
            dma((2, 8)),
            dma((2, 8)),
            dma((2, 5)),
            dma((9,)),
            dma((8,)),
            pltpu.SemaphoreType.REGULAR,
            pltpu.SemaphoreType.REGULAR,
        ],
        compiler_params=pltpu.CompilerParams(
            collective_id=1, has_side_effects=True, vmem_limit_bytes=62 * 1024 * 1024
        ),
        cost_estimate=pl.CostEstimate(
            flops=45 * 10**9, bytes_accessed=40 * 10**6, transcendentals=4 * 10**6
        ),
        name="layer",
    )(*operands)


def finish_kernel(
    gq,
    gu,
    gd,
    gp,
    gv,
    qkv_out,
    up_out,
    down_out,
    proj_out,
    gain_out,
    shift_out,
    proj_bias_out,
    down_bias_out,
    qkv_bias_out,
    up_bias_out,
):
    lane = lax.broadcasted_iota(jnp.int32, (1, 128), 1)
    for which in range(3):
        for c in range(8):
            part = gq[c, :, which * COLS : which * COLS + COLS]
            qkv_out[:, which * WIDTH + c * COLS : which * WIDTH + (c + 1) * COLS] = part.astype(f32)
    for pair in range(4):
        for m in range(8):
            a = gu[2 * pair, :, 128 * m : 128 * m + 128].astype(f32)
            b = gu[2 * pair + 1, :, 128 * m : 128 * m + 128].astype(f32)
            for odd in range(2):
                at = (2 * m + odd) * 512 + pair * 128
                up_out[:, at : at + 128] = halves_packed(a, b, odd == 1, lane)
    down_out[...] = gd[0].astype(f32)
    proj_out[...] = gp[...].astype(f32)
    sums = jnp.sum(gv[...], axis=0)
    gain_out[...] = sums[0]
    shift_out[...] = sums[1]
    proj_bias_out[...] = sums[2]
    down_bias_out[...] = sums[2]
    for i in range(3):
        qkv_bias_out[128 * i : 128 * i + 128] = sums[3 + i]
    for i in range(4):
        up_bias_out[128 * i : 128 * i + 128] = sums[6 + i]


def finish_call(gq, gu, gd, gp, gv):
    steps = 4
    rows = 128 // steps
    return pl.pallas_call(
        finish_kernel,
        grid=(steps,),
        out_shape=[
            jax.ShapeDtypeStruct((128, 3 * WIDTH), f32),
            jax.ShapeDtypeStruct((128, HIDDEN), f32),
            jax.ShapeDtypeStruct((512, WIDTH), f32),
            jax.ShapeDtypeStruct((128, WIDTH), f32),
            jax.ShapeDtypeStruct((128,), f32),
            jax.ShapeDtypeStruct((128,), f32),
            jax.ShapeDtypeStruct((128,), f32),
            jax.ShapeDtypeStruct((128,), f32),
            jax.ShapeDtypeStruct((384,), f32),
            jax.ShapeDtypeStruct((512,), f32),
        ],
        in_specs=[
            pl.BlockSpec((8, rows, 768), lambda i: (0, i, 0)),
            pl.BlockSpec((8, rows, UNITS), lambda i: (0, i, 0)),
            pl.BlockSpec((1, 128, WIDTH), lambda i: (i, 0, 0)),
            pl.BlockSpec((rows, WIDTH), lambda i: (i, 0)),
            pl.BlockSpec((8, 16, 128), lambda i: (0, 0, 0)),
        ],
        out_specs=[
            pl.BlockSpec((rows, 3 * WIDTH), lambda i: (i, 0)),
            pl.BlockSpec((rows, HIDDEN), lambda i: (i, 0)),
            pl.BlockSpec((128, WIDTH), lambda i: (i, 0)),
            pl.BlockSpec((rows, WIDTH), lambda i: (i, 0)),
            pl.BlockSpec((128,), lambda i: (0,)),
            pl.BlockSpec((128,), lambda i: (0,)),
            pl.BlockSpec((128,), lambda i: (0,)),
            pl.BlockSpec((128,), lambda i: (0,)),
            pl.BlockSpec((384,), lambda i: (0,)),
            pl.BlockSpec((512,), lambda i: (0,)),
        ],
        compiler_params=pltpu.CompilerParams(vmem_limit_bytes=62 * 1024 * 1024),
        cost_estimate=pl.CostEstimate(
            flops=10**6, bytes_accessed=20 * 10**6, transcendentals=0
        ),
        name="finish",
    )(gq, gu, gd, gp, gv)


def local(
    tokens,
    segments,
    ln_gain,
    ln_shift,
    qkv_weight,
    qkv_bias,
    proj_weight,
    proj_bias,
    up_weight,
    up_bias,
    down_weight,
    down_bias,
    cotangent,
):
    block_out, token_grad, log_sums, gq, gu, gd, gp, gv = layer_call(
        tokens[0],
        cotangent[0],
        qkv_weight,
        proj_weight,
        up_weight,
        down_weight,
        segments,
        ln_gain[None],
        ln_shift[None],
        proj_bias[None],
        down_bias[None],
        qkv_bias,
        up_bias,
    )
    qkv_grad, up_grad, down_grad, proj_grad, *vectors = finish_call(
        gq.reshape(8, 128, 768),
        gu.reshape(8, 128, UNITS),
        gd.reshape(4, 128, WIDTH),
        gp,
        gv.reshape(8, 16, 128),
    )
    return (
        block_out[None],
        token_grad[None],
        log_sums[None],
        vectors[0],
        vectors[1],
        qkv_grad,
        vectors[4],
        proj_grad,
        vectors[2],
        up_grad,
        vectors[5],
        down_grad,
        vectors[3],
    )


def solution(mesh):
    in_specs = (
        P("fsdp", "ctx", None),
        P("fsdp", "ctx"),
        P("fsdp"),
        P("fsdp"),
        P("fsdp", None),
        P("fsdp"),
        P("fsdp", None),
        P("fsdp"),
        P("fsdp", None),
        P("fsdp"),
        P("fsdp", None),
        P("fsdp"),
        P("fsdp", "ctx", None),
    )
    out_specs = (
        P("fsdp", "ctx", None),
        P("fsdp", "ctx", None),
        P("fsdp", None, "ctx"),
        P("fsdp"),
        P("fsdp"),
        P("fsdp", None),
        P("fsdp"),
        P("fsdp", None),
        P("fsdp"),
        P("fsdp", None),
        P("fsdp"),
        P("fsdp", None),
        P("fsdp"),
    )
    return jax.shard_map(local, mesh=mesh, in_specs=in_specs, out_specs=out_specs, check_vma=False)
```

```python
from functools import partial
import math

import jax
import jax.numpy as jnp
from jax import lax
from jax.experimental import pallas as pl
from jax.experimental.pallas import tpu as pltpu
from jax.sharding import PartitionSpec as P

HEAD = 64
ROT_DIMS = 32
SEQ = 1024
WIDTH = 2048
HIDDEN = 8192
OWN_HEADS = 4
COLS = 256
UNITS = 1024

epsilon = 1e-05
masked_score = -1e30
f32 = jnp.float32
bf16 = jnp.bfloat16
MESH = pl.DeviceIdType.MESH
VM = pltpu.VMEM


def dot(a, b, ca, cb):
    return lax.dot_general(a, b, (((ca,), (cb,)), ((), ())), preferred_element_type=f32)


def place():
    c = lax.axis_index("ctx")
    f = lax.axis_index("fsdp")
    return c, f, c // 2, c % 2, f // 4, f % 4


def other_core():
    c, f, z, core, y, x = place()
    return (z * 2 + 1 - core, f)


def up1(i):
    return (i + 1) % 4


def down1(i):
    return (i + 3) % 4


def over(i):
    return (i + 2) % 4


class Copies:
    def __init__(self, send, recv):
        self.send, self.recv = send, recv
        self.started = []

    def start(self, k, src, dst, device):
        copy = pltpu.make_async_remote_copy(
            src_ref=src,
            dst_ref=dst,
            send_sem=self.send.at[k],
            recv_sem=self.recv.at[k],
            device_id=device,
            device_id_type=MESH,
        )
        copy.start()
        self.started.append(copy)

    def arrived(self, k, dst):
        pltpu.make_async_remote_copy(
            src_ref=dst,
            dst_ref=dst,
            send_sem=self.send.at[k],
            recv_sem=self.recv.at[k],
            device_id=other_core(),
            device_id_type=MESH,
        ).wait_recv()

    def sent(self):
        for copy in self.started:
            copy.wait_send()
        self.started = []


def plane_gather(w, cuts, copies):
    c, f, z, core, y, x = place()
    r0, r1, r2, r3, r4 = cuts
    first, last = pl.ds(r0, r2 - r0), pl.ds(r2, r4 - r2)
    q0, q1, q2, q3 = (pl.ds(a, b - a) for a, b in zip(cuts[:-1], cuts[1:]))
    xu, xd, xo = up1(x), down1(x), over(x)
    yu, yd, yo = up1(y), down1(y), over(y)
    to_xu, to_xd = (c, y * 4 + xu), (c, y * 4 + xd)
    to_yu, to_yd = (c, yu * 4 + x), (c, yd * 4 + x)
    lo, hi = pl.ds(0, 2), pl.ds(2, 2)
    every = pl.ds(0, 4)

    def send(k, part, device):
        copies.start(k, w.at[part], w.at[part], device)

    def got(k, part):
        copies.arrived(k, w.at[part])

    send(0, (y, x, first), to_xu)
    send(1, (y, x, first), to_xd)
    send(2, (y, x, last), to_yu)
    send(3, (y, x, last), to_yd)
    yield
    got(0, (y, xd, first))
    send(4, (y, xd, q0), to_xu)
    got(1, (y, xu, first))
    send(5, (y, xu, q1), to_xd)
    got(2, (yd, x, last))
    send(6, (yd, x, q2), to_yu)
    got(3, (yu, x, last))
    send(7, (yu, x, q3), to_yd)
    yield
    got(4, (y, xo, q0))
    got(5, (y, xo, q1))
    send(8, (y, every, first), to_yu)
    send(9, (y, every, first), to_yd)
    got(6, (yo, x, q2))
    got(7, (yo, x, q3))
    send(10, (every, x, last), to_xu)
    send(11, (every, x, last), to_xd)
    yield
    got(8, (yd, every, first))
    send(12, (yd, lo, first), to_yu)
    got(9, (yu, every, first))
    send(13, (yu, hi, first), to_yd)
    got(10, (every, xd, last))
    send(14, (lo, xd, last), to_xu)
    got(11, (every, xu, last))
    send(15, (hi, xu, last), to_xd)
    yield
    got(12, (yo, lo, first))
    got(13, (yo, hi, first))
    got(14, (lo, xo, last))
    got(15, (hi, xo, last))
    yield


def line_gather(t, cuts, copies, own=None):
    c, f, z, core, y, x = place()
    r0, r1, r2 = cuts
    h0, h1 = pl.ds(r0, r1 - r0), pl.ds(r1, r2 - r1)
    zu, zd, zo = up1(z), down1(z), over(z)
    to_zu, to_zd, to_core = (zu * 2 + core, f), (zd * 2 + core, f), (z * 2 + 1 - core, f)
    other = 1 - core

    def send(k, part, device):
        copies.start(k, t.at[part], t.at[part], device)

    def got(k, part):
        copies.arrived(k, t.at[part])

    mine = t.at[z, core]
    own = mine if own is None else own
    copies.start(0, own, mine, to_zu)
    copies.start(1, own, mine, to_zd)
    copies.start(2, own, mine, to_core)
    yield
    got(0, (zd, core))
    send(3, (zd, core, h0), to_zu)
    got(1, (zu, core))
    send(4, (zu, core, h1), to_zd)
    send(5, (zd, core), to_core)
    send(6, (zu, core), to_core)
    yield
    got(3, (zo, core, h0))
    got(4, (zo, core, h1))
    send(7, (zo, core), to_core)
    yield
    got(2, (z, other))
    got(5, (zd, other))
    got(6, (zu, other))
    got(7, (zo, other))
    yield


def enter():
    c, f, z, core, y, x = place()
    barrier = pltpu.get_barrier_semaphore()
    for device in (
        (c, y * 4 + up1(x)),
        (c, y * 4 + down1(x)),
        (c, up1(y) * 4 + x),
        (c, down1(y) * 4 + x),
        (up1(z) * 2 + core, f),
        (down1(z) * 2 + core, f),
        (z * 2 + 1 - core, f),
    ):
        pl.semaphore_signal(barrier, inc=1, device_id=device, device_id_type=MESH)
    owner = c * 2 + f // 8

    @pl.when(owner != f)
    def _():
        pl.semaphore_signal(barrier, inc=1, device_id=(c, owner), device_id_type=MESH)

    for j in range(8):
        target = (f % 2) * 8 + j

        @pl.when((f // 2 == c) & (target != f))
        def _():
            pl.semaphore_signal(barrier, inc=1, device_id=(c, target), device_id_type=MESH)

    count = 7 + jnp.where(f // 2 == c, jnp.where(f // 8 == f % 2, 7, 8), 0)
    count = count + jnp.where(owner != f, 1, 0)
    pl.semaphore_wait(barrier, count)


def turn(fields, cos, low_sin, high_sin):
    return (
        fields * cos + pltpu.roll(fields, 112, 1) * low_sin + pltpu.roll(fields, 16, 1) * high_sin
    )


def turn_back(grads, cos, low_sin, high_sin):
    return (
        grads * cos + pltpu.roll(grads * low_sin, 16, 1) + pltpu.roll(grads * high_sin, 112, 1)
    )


def halves_packed(a, b, odd, lane):
    moved_a, moved_b = pltpu.roll(a, 64, 1), pltpu.roll(b, 64, 1)
    return jnp.where(lane < 64, jnp.where(odd, moved_a, a), jnp.where(odd, b, moved_b))


def add_into(target, part, *others):
    total = target[part].astype(f32)
    for ref, piece in others:
        total = total + ref[piece].astype(f32)
    target[part] = total.astype(target.dtype)


def plane_reduce(g, cuts, ra, rb, copies):
    c, f, z, core, y, x = place()
    r0, r1, r2, r3, r4 = cuts
    first, last = pl.ds(r0, r2 - r0), pl.ds(r2, r4 - r2)
    q0, q1, q2, q3 = (pl.ds(a, b - a) for a, b in zip(cuts[:-1], cuts[1:]))
    s0, s1, s2, s3 = (pl.ds(0, b - a) for a, b in zip(cuts[:-1], cuts[1:]))
    xu, xd, xo = up1(x), down1(x), over(x)
    yu, yd, yo = up1(y), down1(y), over(y)
    to_xu, to_xd = (c, y * 4 + xu), (c, y * 4 + xd)
    to_yu, to_yd = (c, yu * 4 + x), (c, yd * 4 + x)
    lo, hi, every = pl.ds(0, 2), pl.ds(2, 2), pl.ds(0, 4)
    near, far = pl.ds(0, 2), pl.ds(2, 4)

    def send(k, part, ref, piece, device):
        copies.start(k, g.at[part], ref.at[piece], device)

    def got(k, ref, piece):
        copies.arrived(k, ref.at[piece])

    send(0, (yo, lo, first), ra, (0, near), to_yu)
    send(1, (yo, hi, first), ra, (1, near), to_yd)
    send(2, (lo, xo, last), rb, (0, near), to_xu)
    send(3, (hi, xo, last), rb, (1, near), to_xd)
    yield
    got(0, ra, (0, near))
    add_into(g, (yu, lo, first), (ra, (0, near)))
    send(4, (yu, every, first), ra, (0, far), to_yu)
    got(1, ra, (1, near))
    add_into(g, (yd, hi, first), (ra, (1, near)))
    send(5, (yd, every, first), ra, (1, far), to_yd)
    got(2, rb, (0, near))
    add_into(g, (lo, xu, last), (rb, (0, near)))
    send(6, (every, xu, last), rb, (0, far), to_xu)
    got(3, rb, (1, near))
    add_into(g, (hi, xd, last), (rb, (1, near)))
    send(7, (every, xd, last), rb, (1, far), to_xd)
    yield
    got(4, ra, (0, far))
    got(5, ra, (1, far))
    add_into(g, (y, every, first), (ra, (0, far)), (ra, (1, far)))
    send(8, (y, xo, q0), ra, (0, 6, s0), to_xu)
    send(9, (y, xo, q1), ra, (1, 6, s1), to_xd)
    got(6, rb, (0, far))
    got(7, rb, (1, far))
    add_into(g, (every, x, last), (rb, (0, far)), (rb, (1, far)))
    send(10, (yo, x, q2), rb, (0, 6, s2), to_yu)
    send(11, (yo, x, q3), rb, (1, 6, s3), to_yd)
    yield
    got(8, ra, (0, 6, s0))
    add_into(g, (y, xu, q0), (ra, (0, 6, s0)))
    send(12, (y, xu, first), ra, (0, 7), to_xu)
    got(9, ra, (1, 6, s1))
    add_into(g, (y, xd, q1), (ra, (1, 6, s1)))
    send(13, (y, xd, first), ra, (1, 7), to_xd)
    got(10, rb, (0, 6, s2))
    add_into(g, (yu, x, q2), (rb, (0, 6, s2)))
    send(14, (yu, x, last), rb, (0, 7), to_yu)
    got(11, rb, (1, 6, s3))
    add_into(g, (yd, x, q3), (rb, (1, 6, s3)))
    send(15, (yd, x, last), rb, (1, 7), to_yd)
    yield
    got(12, ra, (0, 7))
    got(13, ra, (1, 7))
    add_into(g, (y, x, first), (ra, (0, 7)), (ra, (1, 7)))
    got(14, rb, (0, 7))
    got(15, rb, (1, 7))
    add_into(g, (y, x, last), (rb, (0, 7)), (rb, (1, 7)))
    yield


def line_reduce(g, cuts, rc, r1, r2, copies):
    c, f, z, core, y, x = place()
    c0, c1, c2 = cuts
    h0, h1 = pl.ds(c0, c1 - c0), pl.ds(c1, c2 - c1)
    s0, s1 = pl.ds(0, c1 - c0), pl.ds(0, c2 - c1)
    zu, zd, zo = up1(z), down1(z), over(z)
    to_zu, to_zd, to_core = (zu * 2 + core, f), (zd * 2 + core, f), (z * 2 + 1 - core, f)
    every = pl.ds(0, 4)
    copies.start(0, g.at[every, 1 - core], rc, to_core)
    yield
    copies.arrived(0, rc)

    def add_row(i, carry):
        add_into(g, (i, core), (rc, (i,)))
        return carry

    lax.fori_loop(0, 4, add_row, 0)
    copies.start(1, g.at[zo, core, h0], r1.at[0, s0], to_zu)
    copies.start(2, g.at[zo, core, h1], r1.at[1, s1], to_zd)
    yield
    copies.arrived(1, r1.at[0, s0])
    add_into(g, (zu, core, h0), (r1, (0, s0)))
    copies.start(3, g.at[zu, core], r2.at[0], to_zu)
    copies.arrived(2, r1.at[1, s1])
    add_into(g, (zd, core, h1), (r1, (1, s1)))
    copies.start(4, g.at[zd, core], r2.at[1], to_zd)
    yield
    copies.arrived(3, r2.at[0])
    copies.arrived(4, r2.at[1])
    yield


def vector_reduce(g, ry, rx, copies):
    c, f, z, core, y, x = place()
    xu, xd, xo = up1(x), down1(x), over(x)
    yu, yd, yo = up1(y), down1(y), over(y)
    to_xu, to_xd = (c, y * 4 + xu), (c, y * 4 + xd)
    to_yu, to_yd = (c, yu * 4 + x), (c, yd * 4 + x)
    copies.start(0, g.at[yo], ry.at[0], to_yu)
    yield
    copies.arrived(0, ry.at[0])
    add_into(g, (yu,), (ry, (0,)))
    copies.start(1, g.at[yu], ry.at[1], to_yu)
    copies.start(2, g.at[yd], ry.at[2], to_yd)
    yield
    copies.arrived(1, ry.at[1])
    copies.arrived(2, ry.at[2])
    add_into(g, (y,), (ry, (1,)), (ry, (2,)))
    copies.start(3, g.at[y, xo], rx.at[0], to_xu)
    yield
    copies.arrived(3, rx.at[0])
    add_into(g, (y, xu), (rx, (0,)))
    copies.start(4, g.at[y, xu], rx.at[1], to_xu)
    copies.start(5, g.at[y, xd], rx.at[2], to_xd)
    yield
    copies.arrived(4, rx.at[1])
    copies.arrived(5, rx.at[2])
    add_into(g, (y, x), (rx, (1,)), (rx, (2,)))
    yield


GATHER1 = (0, 48, 96, 144, 192)
REDUCE1 = (0, 48, 96, 128, 176)
CUTS2 = (0, 16, 32, 48, 64)
CUTS3 = (0, 32, 64, 96, 128)
PROJ = ((0, 768), (768, 768), (1536, 512))


ORDER = (
    "load_t", "gather_t", "gather_s", "load_1", "gather1", "pack", "load_2", "gather2", "gather1",
    "gather3", "gather1", "gather_t", "gather_s", "gather3", "load_u", "gather_u", "gather_t",
    "gather_s", "gather2", "gather_t", "gather_s", "gather1", "gather2", "gather3", "tables",
    "gather_u", "gather1", "stats", "norm", "gather_u", "project", "gather_u", "dctx", "att3",
    "att2", "gather3", "att1", "gather2", "att0", "gp", "join", "dn1a", "dn1b", "gqa", "gqb",
    "gather3", "reduce1", "up_bias", "ff1a", "ff1b", "ff1c", "ff1d", "gather2", "reduce1", "ff2a",
    "ff2b", "ff2c", "ff2d", "dn2a", "dn2b", "reduce_d", "sent3", "gua", "reduce1", "gub",
    "free_n", "reduce3", "reduce_d", "free_rc", "lse", "reduce1", "oa", "reduce3", "reduce_d",
    "ob", "wait_rc", "reduce_o", "sent2", "gda", "reduce1", "spread_q", "proj_owner", "gdb",
    "reload", "wait_n", "reduce2", "reduce_d", "reduce_o", "reduce3", "fgrad", "reduce2", "vec",
    "spread_q", "proj_along", "reduce_o", "reduce3", "spread_q", "proj_further", "reduce_v",
    "reduce2", "reduce3", "reduce_v", "spread_u", "proj_across", "put_u", "reduce2", "reduce2",
    "reduce_v", "spread_d", "put_d", "spread_u", "reduce_v", "reduce_o", "fout", "reduce_v",
    "spread_v", "put_v", "spread_d", "spread_u", "spread_v", "spread_u", "spread_d", "spread_v",
    "spread_q", "spread_d", "spread_v", "proj_end",
)


def layer_kernel(
    tokens,
    cotangent,
    qkv_weight,
    proj_weight,
    up_weight,
    down_weight,
    seg,
    gain_in,
    shift_in,
    proj_bias_in,
    down_bias_in,
    qkv_bias_in,
    up_bias_in,
    block_out,
    token_grad,
    lse_out,
    gq_out,
    gu_out,
    gd_out,
    gp_out,
    gv_out,
    w1,
    w2,
    w3,
    t,
    ids,
    u,
    n,
    zd,
    rc,
    zo_r1,
    zo_r2,
    zd_r1,
    zd_r2,
    ra1,
    rb1,
    ra3,
    rb3,
    vecs,
    tab,
    begin_cols,
    q,
    k,
    v,
    dctx,
    ctx,
    dk,
    dv,
    dproj,
    act,
    dhid,
    lse,
    lse_own,
    pt,
    gp,
    gv,
    ry,
    rx,
    sem1,
    sem2,
    sem3,
    sem_t,
    sem_u,
    sem_i,
    sem_r1,
    sem_r2,
    sem_r3,
    sem_v,
    sem_zo,
    sem_zd,
    sem_lq,
    sem_lu,
    sem_ld,
    sem_lv,
    sem_r5,
    sem_le,
    sem_s,
    sem_p,
    sem_b,
    sem_l,
    sem_o,
    n_free,
    rc_free,
):
    c, f, z, core, y, x = place()
    lane = lax.broadcasted_iota(jnp.int32, (1, 128), 1)
    odd = core == 1
    owner = c * 2 + f // 8
    own_rows = f // 2 == c
    zo = t

    loads = [
        pltpu.make_async_copy(tokens, t.at[z, core, pl.ds(0, 128)], sem_l.at[0]),
        pltpu.make_async_copy(cotangent, u.at[z, core], sem_l.at[1]),
        pltpu.make_async_copy(
            down_weight.at[pl.ds(pl.multiple_of(c * 64, 64), 64)], w2.at[y, x], sem_l.at[2]
        ),
    ]
    for i in range(3):
        loads.append(
            pltpu.make_async_copy(
                qkv_weight.at[:, pl.ds(pl.multiple_of(i * WIDTH + c * COLS, 128), COLS)],
                w1.at[y, x, pl.ds(0, 128), pl.ds(i * COLS, COLS)],
                sem_l.at[3 + i],
            )
        )
    for copy in loads:
        copy.start()
    for i in range(16):
        pltpu.make_async_copy(
            up_weight.at[:, pl.ds(pl.multiple_of(i * 512 + (c // 2) * 128, 128), 128)],
            q.at[pl.ds(i // 2 * 128, 128), pl.ds(i % 2 * 128, 128)],
            sem_l.at[6],
        ).start()
    vector_list = [gain_in[...], shift_in[...], proj_bias_in[...], down_bias_in[...]]
    vector_list += [qkv_bias_in[128 * i : 128 * i + 128].reshape(1, 128) for i in range(3)]
    vector_list += [up_bias_in[128 * i : 128 * i + 128].reshape(1, 128) for i in range(4)]
    vector_list = [vector.astype(f32) for vector in vector_list] + [jnp.zeros((5, 128), f32)]
    w1[y, x, 176:192, 0:128] = jnp.concatenate(vector_list, axis=0).astype(bf16)
    w1[y, x, 176:192, 128:768] = jnp.zeros((16, 640), bf16)
    w1[y, x, 160:176, 512:768] = jnp.zeros((16, 256), bf16)
    seg_rows = jnp.broadcast_to(seg[...].astype(f32), (16, 128)).astype(bf16)
    ids[z, core] = seg_rows

    enter()

    def both_ways(sems):
        return Copies(sems.at[0], sems.at[1])

    copies1, copies2, copies3 = both_ways(sem1), both_ways(sem2), both_ways(sem3)
    copies_t, copies_u, copies_s = both_ways(sem_t), both_ways(sem_u), both_ways(sem_i)
    copies_r1, copies_r2, copies_r3 = both_ways(sem_r1), both_ways(sem_r2), both_ways(sem_r3)
    copies_v = both_ways(sem_v)
    copies_zo, copies_zd = both_ways(sem_zo), both_ways(sem_zd)
    copies_lq, copies_lu = both_ways(sem_lq), both_ways(sem_lu)
    copies_ld, copies_lv = both_ways(sem_ld), both_ways(sem_lv)
    copies_r5, copies_le = both_ways(sem_r5), both_ways(sem_le)
    gather1 = plane_gather(w1, GATHER1, copies1)
    gather2 = plane_gather(w2, CUTS2, copies2)
    gather3 = plane_gather(w3, CUTS3, copies3)
    gather_t = line_gather(t.at[:, :, pl.ds(0, 128)], (0, 64, 128), copies_t)
    gather_s = line_gather(ids, (0, 8, 16), copies_s)
    gather_u = line_gather(u, (0, 64, 128), copies_u)
    reduce1 = plane_reduce(w1, REDUCE1, ra1, rb1, copies_r1)
    left, right = pl.ds(0, 1024), pl.ds(1024, 1024)
    into = (slice(None),) * 3
    reduce2a, reduce2b = [
        plane_reduce(
            w2.at[into + (part,)],
            CUTS2,
            n.at[(0,) + into + (part,)],
            n.at[(1,) + into + (part,)],
            copies,
        )
        for part, copies in ((left, copies_r2), (right, copies_r5))
    ]
    reduce3 = plane_reduce(w3, CUTS3, ra3, rb3, copies_r3)
    reduce_v = vector_reduce(gv, ry, rx, copies_v)
    reduce_o = line_reduce(zo, (0, 64, 144), rc, zo_r1, zo_r2, copies_zo)
    reduce_d = line_reduce(zd, (0, 64, 128), rc.at[:, pl.ds(0, 128)], zd_r1, zd_r2, copies_zd)
    spread_q = line_gather(gq_out, (0, 64, 128), copies_lq, w1.at[y, x, pl.ds(0, 128)])
    spread_u = line_gather(gu_out, (0, 64, 128), copies_lu, w3.at[y, x])
    reduce2 = plane_reduce(w2, CUTS2, n.at[0], n.at[1], copies_r2)
    spread_d = line_gather(gd_out, (0, 32, 64), copies_ld, w2.at[y, x])
    spread_da, spread_db = [
        line_gather(gd_out.at[into + (part,)], (0, 32, 64), copies, w2.at[y, x, :, part])
        for part, copies in ((left, copies_ld), (right, copies_le))
    ]
    spread_v = line_gather(gv_out, (0, 8, 16), copies_lv, gv.at[y, x])

    outs = []

    def put(src, dst):
        copy = pltpu.make_async_copy(src, dst, sem_o.at[len(outs)])
        copy.start()
        outs.append(copy)

    kept = {}

    def scatter(j, target):
        return pltpu.make_async_remote_copy(
            src_ref=proj_weight.at[pl.ds(16 * j, 16)],
            dst_ref=pt,
            send_sem=sem_s.at[0, j],
            recv_sem=sem_s.at[1, 0],
            device_id=(c, target),
            device_id_type=MESH,
        )

    def load_1():
        for j in range(8):
            target = (f % 2) * 8 + j

            @pl.when(own_rows & (target != f))
            def _():
                scatter(j, target).start()

            @pl.when(own_rows & (target == f))
            def _():
                local = pltpu.make_async_copy(
                    proj_weight.at[pl.ds(16 * j, 16)], pt, sem_s.at[1, 1]
                )
                local.start()
                local.wait()

        for i in (3, 4, 5):
            loads[i].wait()

        @pl.when(owner != f)
        def _():
            pltpu.make_async_remote_copy(
                src_ref=pt,
                dst_ref=pt,
                send_sem=sem_s.at[0, 0],
                recv_sem=sem_s.at[1, 0],
                device_id=other_core(),
                device_id_type=MESH,
            ).wait_recv()

        for j, (start, size) in enumerate(PROJ):
            w1[y, x, 128 + 16 * j : 144 + 16 * j, 0:size] = pt[:, start : start + size]

    def pack():
        pltpu.make_async_copy(q, q, sem_l.at[6]).wait()
        for m in range(8):
            strip = q[128 * m : 128 * m + 128, :].astype(f32)
            packed = halves_packed(strip[:, :128], strip[:, 128:], odd, lane)
            w3[y, x, :, 128 * m : 128 * m + 128] = packed.astype(bf16)

    def tables():
        in_head = lane % 64
        inverse = jnp.exp((lane % 16).astype(f32) * (-math.log(10000.0) / (ROT_DIMS // 2)))
        inverse = jnp.where(in_head < ROT_DIMS, inverse, 0.0)
        row_angles = lax.broadcasted_iota(jnp.int32, (128, 1), 0).astype(f32) * inverse
        row_cos, row_sin = jnp.cos(row_angles), jnp.sin(row_angles)
        seg_all = jnp.concatenate(
            [ids[b // 2, b % 2][0:1].astype(f32) for b in range(8)], axis=0
        )
        seg_cols = jnp.transpose(seg_all)
        firsts = [jnp.sum((seg_all < float(d)).astype(f32), keepdims=True) for d in range(1, 4)]
        begins = jnp.zeros((128, 8), f32)
        row = lax.broadcasted_iota(jnp.int32, (32, 1), 0)
        shifts = (row // 4 * 128).astype(f32)
        for d in range(1, 4):
            begins = jnp.where(seg_cols == float(d), firsts[d - 1], begins)
            shifts = shifts - jnp.where(row % 4 == d, firsts[d - 1], 0.0)
        begin_cols[:, 0:8] = begins
        shift_cos, shift_sin = jnp.cos(shifts * inverse), jnp.sin(shifts * inverse)
        for b in range(8):
            rows = pl.ds(b * 128, 128)
            own = seg_cols[:, b : b + 1]
            block_cos, block_sin = shift_cos[4 * b : 4 * b + 1], shift_sin[4 * b : 4 * b + 1]
            for d in range(1, 4):
                at = 4 * b + d
                block_cos = jnp.where(own == float(d), shift_cos[at : at + 1], block_cos)
                block_sin = jnp.where(own == float(d), shift_sin[at : at + 1], block_sin)
            sin = row_sin * block_cos + row_cos * block_sin
            tab[0, rows, :] = row_cos * block_cos - row_sin * block_sin
            tab[1, rows, :] = jnp.where(in_head < 16, -sin, 0.0)
            tab[2, rows, :] = jnp.where((in_head >= 16) & (in_head < 32), sin, 0.0)

    def joined(which):
        return jnp.concatenate([vecs[i, which : which + 1, :] for i in range(16)], axis=1)

    def norm_source(i):
        return t[i // 4, i // 2 % 2, pl.ds(pl.multiple_of(i % 2 * 64, 64), 64), :].astype(f32)

    def statistics():
        def row_statistics(i, carry):
            values = norm_source(i)
            average = jnp.mean(values, axis=-1, keepdims=True)
            centered = values - average
            variance = jnp.mean(centered * centered, axis=-1, keepdims=True)
            rows = pl.ds(pl.multiple_of(i * 64, 64), 64)
            dk[rows, 0:128] = jnp.broadcast_to(average, (64, 128))
            dk[rows, 128:256] = jnp.broadcast_to(lax.rsqrt(variance + epsilon), (64, 128))
            return carry

        lax.fori_loop(0, 16, row_statistics, 0)

    def norm():
        vecs[...] = w1[:, :, 176:192, 0:128].reshape(16, 16, 128).astype(f32)
        gain, shift = joined(0), joined(1)

        def norm_rows(i, carry):
            rows = pl.ds(pl.multiple_of(i * 64, 64), 64)
            standard = (norm_source(i) - dk[rows, 0:1]) * dk[rows, 128:129]
            normed = (standard * gain + shift).astype(bf16)
            n[i // 8, i // 4 % 2, pl.ds(i % 4 * 2, 2)] = normed.reshape(2, 32, WIDTH)
            return carry

        lax.fori_loop(0, 16, norm_rows, 0)

    def project():
        parts = []
        for which in range(3):
            for i in range(2):
                at = which * 16 + c * 2 + i
                parts.append(vecs[at // 3, pl.ds(4 + at % 3, 1), :])
        qkv_bias = jnp.concatenate(parts, axis=1)

        def project_rows(m, carry):
            rows = pl.ds(pl.multiple_of(m * 512, 512), 512)
            turns = [tab[i, rows, :] for i in range(3)]
            right = w1[:, :, pl.ds(0, 128), :].reshape(WIDTH, 768)
            fields = dot(n[m].reshape(512, WIDTH), right, 1, 0) + qkv_bias
            for which, target in enumerate((q, k, v)):
                for pair in range(2):
                    at = which * COLS + pair * 128
                    both = fields[:, at : at + 128]
                    if which < 2:
                        both = turn(both, *turns)
                    if which == 0:
                        both = both * 0.125
                    target[rows, pair * 128 : pair * 128 + 128] = both.astype(bf16)
            return carry

        lax.fori_loop(0, 2, project_rows, 0)

    def context_grad():
        grads = jnp.zeros((SEQ, COLS), f32)
        for j, (start, size) in enumerate(PROJ):
            left = u[:, :, :, pl.ds(start, size)].reshape(SEQ, size)
            right = w1[:, :, pl.ds(128 + 16 * j, 16), pl.ds(0, size)].reshape(COLS, size)
            grads = grads + dot(left, right, 1, 1)
        dctx[...] = grads.astype(bf16)

    def attention(block):
        reach = (block + 1) * 256
        rows = pl.ds(block * 256, 256)
        keys = pl.ds(0, reach)
        begin = jnp.concatenate(
            [begin_cols[:, 2 * block + i : 2 * block + i + 1] for i in range(2)], axis=0
        )
        key_index = lax.broadcasted_iota(jnp.int32, (1, reach), 1).astype(f32)
        row_index = (lax.broadcasted_iota(jnp.int32, (256, 1), 0) + block * 256).astype(f32)

        def attend(pair, carry):
            lanes = pl.ds(pl.multiple_of(pair * 128, 128), 128)
            qp, kp, vp, dp = q[rows, lanes], k[keys, lanes], v[keys, lanes], dctx[rows, lanes]
            results = []
            for half in range(2):
                here = (lane >= 64) == (half == 1)
                qh = jnp.where(here, qp, jnp.zeros((), bf16))
                dh = jnp.where(here, dp, jnp.zeros((), bf16))
                scores = dot(qh, kp, 1, 1)
                allowed = (key_index >= begin) & (key_index <= row_index)
                scores = jnp.where(allowed, scores, masked_score)
                highest = jnp.max(scores, axis=1, keepdims=True)
                weights = jnp.exp(scores - highest)
                total = jnp.sum(weights, axis=1, keepdims=True)
                probs = weights * (1.0 / total)
                log_sum = jnp.broadcast_to(highest + jnp.log(total), (256, 128))
                lse[pl.ds(pair * 2 + half, 1), rows] = jnp.transpose(log_sum)[0:1, :]
                probs_low = probs.astype(bf16)
                d_probs = dot(dh, vp, 1, 1)
                delta = jnp.sum(probs * d_probs, axis=1, keepdims=True)
                d_scores = (probs * (d_probs - delta)).astype(bf16)
                results.append(
                    (
                        dot(probs_low, vp, 1, 0),
                        dot(d_scores, kp, 1, 0),
                        dot(d_scores, qp, 0, 0),
                        dot(probs_low, dp, 0, 0),
                    )
                )
            context, d_queries, d_keys, d_values = [
                jnp.where(lane < 64, a, b) for a, b in zip(*results)
            ]
            ctx[rows, lanes] = context.astype(bf16)
            turns = [tab[i, rows, :] for i in range(3)]
            dproj[rows, lanes] = turn_back(d_queries * 0.125, *turns).astype(bf16)
            if block == 3:
                dk[keys, lanes] = d_keys
                dv[keys, lanes] = d_values
            else:
                dk[keys, lanes] += d_keys
                dv[keys, lanes] += d_values
            return carry

        lax.fori_loop(0, 2, attend, 0)

    def join():
        def join_rows(m, carry):
            rows = pl.ds(pl.multiple_of(m * 256, 256), 256)
            turns = [tab[i, rows, :] for i in range(3)]
            for pair in range(2):
                lanes = pl.ds(pair * 128, 128)
                turned = turn_back(dk[rows, lanes], *turns)
                dproj[rows, pl.ds(COLS + pair * 128, 128)] = turned.astype(bf16)
                dproj[rows, pl.ds(2 * COLS + pair * 128, 128)] = dv[rows, lanes].astype(bf16)
            return carry

        lax.fori_loop(0, 4, join_rows, 0)

    def normed_part(i, carry):
        columns = pl.ds(pl.multiple_of(i * 512, 512), 512)
        total = dot(dproj[...], w1[i, :, pl.ds(0, 128), :].reshape(512, 768), 1, 1)
        zd[:, :, :, columns] = total.astype(bf16).reshape(4, 2, 128, 512)
        return carry

    def qkv_part(i, carry):
        columns = pl.ds(pl.multiple_of(i * 512, 512), 512)
        grads = dot(n[:, :, :, :, columns].reshape(SEQ, 512), dproj[...], 0, 0).astype(bf16)
        w1[i, :, pl.ds(0, 128), :] = grads.reshape(4, 128, 768)
        return carry

    def proj_part():
        copies1.sent()
        copies_t.sent()
        for j, (start, size) in enumerate(PROJ):
            columns = pl.ds(start, size)
            part = (slice(None), slice(None), pl.ds(128 + 16 * j, 16), pl.ds(0, size))
            total = dot(ctx[...], w1[part].reshape(COLS, size), 1, 0)
            zo[:, :, pl.ds(0, 128), columns] = total.astype(bf16).reshape(4, 2, 128, size)
            right = u[:, :, :, columns].reshape(SEQ, size)
            w1[part] = dot(ctx[...], right, 0, 0).astype(bf16).reshape(4, 4, 16, size)

    def log_sums():
        for b in range(8):
            part = jnp.concatenate(
                [lse[j : j + 1, b * 128 : b * 128 + 128] for j in range(4)], axis=1
            )
            wide = jnp.concatenate([jnp.where(c % 4 == s, part, 0.0) for s in range(4)], axis=1)
            high = wide.astype(bf16).astype(f32)
            at = lax.broadcasted_iota(jnp.int32, (16, 1), 0)
            both = jnp.where(at == c // 4, high, jnp.where(at == 2 + c // 4, wide - high, 0.0))
            zo[b // 2, b % 2, 128:144, :] = both.astype(bf16)

    def feed(i, carry):
        rows = pl.ds(pl.multiple_of(i // 2 * 512, 512), 512)
        columns = pl.ds(pl.multiple_of(i % 2 * 512, 512), 512)
        right = w3[:, :, :, columns].reshape(WIDTH, 512)
        bias = jnp.where(i % 2 == 0, kept["up_bias"][:, 0:512], kept["up_bias"][:, 512:1024])
        h = dot(n[i // 2].reshape(512, WIDTH), right, 1, 0) + bias
        square = h * h
        tanh = jnp.tanh(0.7978845608028654 * (h + 0.044715 * square * h))
        half = 0.5 * (1.0 + tanh)
        slope = half + 0.5 * h * (1.0 - tanh * tanh) * (
            0.7978845608028654 * (1.0 + 3.0 * 0.044715 * square)
        )
        act[rows, columns] = (h * half).astype(bf16)
        dhid[rows, columns] = slope.astype(bf16)
        return carry

    def up_bias():
        parts = []
        for m in range(8):
            a = vecs[2 * m, pl.ds(7 + c // 2, 1), :]
            b = vecs[2 * m + 1, pl.ds(7 + c // 2, 1), :]
            parts.append(halves_packed(a, b, odd, lane))
        kept["up_bias"] = jnp.concatenate(parts, axis=1)

    def feed_back(i, carry):
        rows = pl.ds(pl.multiple_of(i // 2 * 512, 512), 512)
        columns = pl.ds(pl.multiple_of(i % 2 * 512, 512), 512)
        left = u[pl.ds(i // 2 * 2, 2)].reshape(512, WIDTH)
        d_act = dot(left, w2[pl.ds(i % 2 * 2, 2)].reshape(512, WIDTH), 1, 1)
        dhid[rows, columns] = (d_act * dhid[rows, columns].astype(f32)).astype(bf16)
        return carry

    def normed_more(i, carry):
        columns = pl.ds(pl.multiple_of(i * 512, 512), 512)
        total = dot(dhid[...], w3[i].reshape(512, UNITS), 1, 1).reshape(4, 2, 128, 512)
        total = total + zd[:, :, :, columns].astype(f32)
        zd[:, :, :, columns] = total.astype(bf16)
        return carry

    def up_part(i, carry):
        columns = pl.ds(pl.multiple_of(i * 512, 512), 512)
        grads = dot(n[:, :, :, :, columns].reshape(SEQ, 512), dhid[...], 0, 0).astype(bf16)
        w3[i] = grads.reshape(4, 128, UNITS)
        return carry

    def free_n():
        for device in (
            (c, y * 4 + up1(x)),
            (c, y * 4 + down1(x)),
            (c, up1(y) * 4 + x),
            (c, down1(y) * 4 + x),
        ):
            pl.semaphore_signal(n_free, inc=1, device_id=device, device_id_type=MESH)

    def free_rc():
        pl.semaphore_signal(rc_free, inc=1, device_id=other_core(), device_id_type=MESH)

    def out_part(i, carry):
        columns = pl.ds(pl.multiple_of(i * 512, 512), 512)
        total = dot(act[...], w2[:, :, :, columns].reshape(UNITS, 512), 1, 0)
        total = total.reshape(4, 2, 128, 512) + zo[:, :, pl.ds(0, 128), columns].astype(f32)
        zo[:, :, pl.ds(0, 128), columns] = total.astype(bf16)
        return carry

    def down_part(i, carry):
        columns = pl.ds(pl.multiple_of(i * 512, 512), 512)
        right = u[:, :, :, columns].reshape(SEQ, 512)
        w2[:, :, :, columns] = dot(act[...], right, 0, 0).astype(bf16).reshape(4, 4, 64, 512)
        return carry

    own_tokens, own_cot = u.at[0, 0], u.at[0, 1]
    again = [
        pltpu.make_async_copy(tokens, own_tokens, sem_l.at[7]),
        pltpu.make_async_copy(cotangent, own_cot, sem_l.at[8]),
    ]

    def reload():
        copies_u.sent()
        for copy in again:
            copy.start()

    def finish_grad():
        for copy in again:
            copy.wait()
        gain = joined(0)
        zero = jnp.zeros((1, WIDTH), f32)

        def finish_rows(i, carry):
            d_gain, d_shift, d_bias = carry
            part = pl.ds(pl.multiple_of(i * 32, 32), 32)
            grads = zd[z, core, part, :].astype(f32)
            grads = grads + zd_r2[0, part, :].astype(f32) + zd_r2[1, part, :].astype(f32)
            values = own_tokens[part, :].astype(f32)
            average = jnp.mean(values, axis=-1, keepdims=True)
            centered = values - average
            variance = jnp.mean(centered * centered, axis=-1, keepdims=True)
            scale = lax.rsqrt(variance + epsilon)
            standard = centered * scale
            d_gain = d_gain + jnp.sum(grads * standard, axis=0, keepdims=True)
            d_shift = d_shift + jnp.sum(grads, axis=0, keepdims=True)
            scaled = grads * gain
            inner = scaled - jnp.mean(scaled, axis=-1, keepdims=True)
            inner = inner - standard * jnp.mean(scaled * standard, axis=-1, keepdims=True)
            upstream = own_cot[part, :].astype(f32)
            d_bias = d_bias + jnp.sum(upstream, axis=0, keepdims=True)
            zd_r2[0, part, :] = (upstream + scale * inner).astype(bf16)
            return d_gain, d_shift, d_bias

        kept["sums"] = lax.fori_loop(0, 4, finish_rows, (zero, zero, zero))
        put(zd_r2.at[0], token_grad)

    def vector_terms():
        gv[...] = jnp.zeros((4, 4, 16, 128), f32)
        for i in range(16):
            lanes = slice(i * 128, i * 128 + 128)
            for at, sums in enumerate(kept["sums"]):
                gv[i // 4, i % 4, at : at + 1, :] = sums[:, lanes]
        ones = jnp.ones((8, SEQ), bf16)
        d_qkv = dot(ones, dproj[...], 1, 0)[0:1, :]
        d_up = dot(ones, dhid[...], 1, 0)[0:1, :]
        for which in range(3):
            for i in range(2):
                at = which * 16 + c * 2 + i
                start = which * COLS + i * 128
                target = at // 3
                term = d_qkv[:, start : start + 128]
                gv[target // 4, target % 4, pl.ds(3 + at % 3, 1), :] = term
        for m in range(8):
            both = d_up[:, m * 128 : m * 128 + 128]
            moved = pltpu.roll(both, 64, 1)
            here = (lane >= 64) == odd
            for i, (even_place, odd_place) in enumerate(((both, moved), (moved, both))):
                at = 2 * m + i
                term = jnp.where(here, jnp.where(odd, odd_place, even_place), 0.0)
                gv[at // 4, at % 4, pl.ds(6 + c // 2, 1), :] = term

    def to_owner(j):
        return pltpu.make_async_remote_copy(
            src_ref=pt,
            dst_ref=gp.at[pl.ds(16 * j, 16)],
            send_sem=sem_p.at[0, 0],
            recv_sem=sem_p.at[1, j],
            device_id=(c, owner),
            device_id_type=MESH,
        )

    def trade(k, src, dst, device):
        return pltpu.make_async_remote_copy(
            src_ref=src,
            dst_ref=dst,
            send_sem=sem_b.at[0, k],
            recv_sem=sem_b.at[1, k],
            device_id=device,
            device_id_type=MESH,
        )

    mine = core == x // 2
    turns_z = (z - y + 4) % 4
    to_zu, to_zd = (up1(z) * 2 + core, f), (down1(z) * 2 + core, f)
    to_core = other_core()
    h0, h1 = gp.at[pl.ds(0, 64)], gp.at[pl.ds(64, 64)]

    def proj_owner():
        put(w1.at[y, x, pl.ds(0, 128)], gq_out.at[z, core])
        for j, (start, size) in enumerate(PROJ):
            pt[:, start : start + size] = w1[y, x, 128 + 16 * j : 144 + 16 * j, 0:size]
        for j in range(8):

            @pl.when((f % 8 == j) & (owner != f))
            def _():
                to_owner(j).start()

            @pl.when((f % 8 == j) & (owner == f))
            def _():
                local = pltpu.make_async_copy(pt, gp.at[pl.ds(16 * j, 16)], sem_p.at[0, 1])
                local.start()
                local.wait()

    def proj_along():
        for j in range(8):

            @pl.when(own_rows & ((f % 2) * 8 + j != f))
            def _():
                slot = gp.at[pl.ds(16 * j, 16)]
                pltpu.make_async_remote_copy(
                    src_ref=slot,
                    dst_ref=slot,
                    send_sem=sem_p.at[0, 0],
                    recv_sem=sem_p.at[1, j],
                    device_id=other_core(),
                    device_id_type=MESH,
                ).wait_recv()

        @pl.when(mine & (turns_z == 0))
        def _():
            trade(0, gp, gp, to_zu).start()
            trade(1, gp, gp, to_zd).start()

    def proj_further():
        @pl.when(mine & (turns_z == 1))
        def _():
            trade(0, gp, gp, to_core).wait_recv()
            trade(2, h0, h0, to_zu).start()

        @pl.when(mine & (turns_z == 3))
        def _():
            trade(1, gp, gp, to_core).wait_recv()
            trade(3, h1, h1, to_zd).start()

    def proj_across():
        @pl.when(mine & (turns_z == 2))
        def _():
            trade(2, h0, h0, to_core).wait_recv()
            trade(3, h1, h1, to_core).wait_recv()

        @pl.when(mine)
        def _():
            trade(4, gp, gp, to_core).start()

    def proj_end():
        @pl.when(jnp.logical_not(mine))
        def _():
            trade(4, gp, gp, to_core).wait_recv()

        put(gp, gp_out)

    def finish_out():
        proj_bias, down_bias = joined(2), joined(3)
        tail = pl.ds(128, 16)
        sums = zo[z, core, tail, :].astype(f32)
        sums = sums + zo_r2[0, tail, :].astype(f32) + zo_r2[1, tail, :].astype(f32)
        sums = sums[0:2, :] + sums[2:4, :]
        for h in range(32):
            lanes = slice((h % 16) * 128, (h % 16) * 128 + 128)
            lse_own[h : h + 1, :] = sums[h // 16 : h // 16 + 1, lanes]

        def finish_rows(i, carry):
            part = pl.ds(pl.multiple_of(i * 32, 32), 32)
            total = zo[z, core, part, :].astype(f32)
            total = total + zo_r2[0, part, :].astype(f32) + zo_r2[1, part, :].astype(f32)
            total = own_tokens[part, :].astype(f32) + total + proj_bias + down_bias
            zo_r2[0, part, :] = total.astype(bf16)
            return carry

        lax.fori_loop(0, 4, finish_rows, 0)
        put(zo_r2.at[0, pl.ds(0, 128)], block_out)
        put(lse_own, lse_out)

    def loop(first, last, body):
        return lambda: lax.fori_loop(first, last, body, 0)

    actions = dict(
        gather1=gather1,
        gather2=gather2,
        gather3=gather3,
        gather_t=gather_t,
        gather_u=gather_u,
        gather_s=gather_s,
        reduce1=reduce1,
        reduce2=reduce2,
        reduce2a=reduce2a,
        reduce2b=reduce2b,
        reduce3=reduce3,
        reduce_o=reduce_o,
        reduce_d=reduce_d,
        reduce_v=reduce_v,
        spread_q=spread_q,
        spread_u=spread_u,
        spread_d=spread_d,
        spread_da=spread_da,
        spread_db=spread_db,
        spread_v=spread_v,
        load_t=loads[0].wait,
        load_u=loads[1].wait,
        load_2=loads[2].wait,
        load_1=load_1,
        pack=pack,
        tables=tables,
        norm=norm,
        stats=statistics,
        up_bias=up_bias,
        project=project,
        dctx=context_grad,
        att3=lambda: attention(3),
        att2=lambda: attention(2),
        att1=lambda: attention(1),
        att0=lambda: attention(0),
        join=join,
        dn1a=loop(0, 2, normed_part),
        dn1b=loop(2, 4, normed_part),
        gqa=loop(0, 2, qkv_part),
        gqb=loop(2, 4, qkv_part),
        gp=proj_part,
        lse=log_sums,
        ff1a=loop(0, 1, feed),
        ff1b=loop(1, 2, feed),
        ff1c=loop(2, 3, feed),
        ff1d=loop(3, 4, feed),
        ff1=loop(0, 4, feed),
        ff2a=loop(0, 1, feed_back),
        ff2b=loop(1, 2, feed_back),
        ff2c=loop(2, 3, feed_back),
        ff2d=loop(3, 4, feed_back),
        ff2=loop(0, 4, feed_back),
        dn2a=loop(0, 2, normed_more),
        dn2b=loop(2, 4, normed_more),
        sent3=copies3.sent,
        gua=loop(0, 2, up_part),
        gub=loop(2, 4, up_part),
        free_n=free_n,
        free_rc=free_rc,
        oa=loop(0, 2, out_part),
        ob=loop(2, 4, out_part),
        wait_rc=lambda: pl.semaphore_wait(rc_free, 1),
        sent2=copies2.sent,
        gda=loop(0, 2, down_part),
        gdb=loop(2, 4, down_part),
        reload=reload,
        wait_n=lambda: pl.semaphore_wait(n_free, 4),
        fgrad=finish_grad,
        vec=vector_terms,
        proj_owner=proj_owner,
        proj_along=proj_along,
        proj_further=proj_further,
        proj_across=proj_across,
        proj_end=proj_end,
        fout=finish_out,
        put_u=lambda: put(w3.at[y, x], gu_out.at[z, core]),
        put_d=lambda: put(w2.at[y, x], gd_out.at[z, core]),
        put_da=lambda: put(w2.at[y, x, :, left], gd_out.at[z, core, :, left]),
        put_db=lambda: put(w2.at[y, x, :, right], gd_out.at[z, core, :, right]),
        put_v=lambda: put(gv.at[y, x], gv_out.at[z, core]),
    )
    for name in ORDER:
        action = actions[name]
        if callable(action):
            action()
        else:
            next(action)

    for copies in (
        copies_s, copies_r1, copies_r2, copies_r5, copies_r3, copies_v, copies_zo, copies_zd,
        copies_lq, copies_lu, copies_ld, copies_le, copies_lv,
    ):
        copies.sent()
    for j in range(8):
        target = (f % 2) * 8 + j

        @pl.when(own_rows & (target != f))
        def _():
            scatter(j, target).wait_send()

    @pl.when(owner != f)
    def _():
        to_owner(0).wait_send()

    @pl.when(mine & (turns_z == 0))
    def _():
        trade(0, gp, gp, to_zu).wait_send()
        trade(1, gp, gp, to_zd).wait_send()

    @pl.when(mine & (turns_z == 1))
    def _():
        trade(2, h0, h0, to_zu).wait_send()

    @pl.when(mine & (turns_z == 3))
    def _():
        trade(3, h1, h1, to_zd).wait_send()

    @pl.when(mine)
    def _():
        trade(4, gp, gp, to_core).wait_send()

    for copy in outs:
        copy.wait()


def layer_call(*operands):
    anyspace = pl.BlockSpec(memory_space=pl.ANY)
    vmem = pl.BlockSpec(memory_space=VM)
    dma = pltpu.SemaphoreType.DMA
    return pl.pallas_call(
        layer_kernel,
        out_shape=[
            jax.ShapeDtypeStruct((128, WIDTH), bf16),
            jax.ShapeDtypeStruct((128, WIDTH), bf16),
            jax.ShapeDtypeStruct((32, 128), f32),
            jax.ShapeDtypeStruct((4, 2, 128, 768), bf16),
            jax.ShapeDtypeStruct((4, 2, 128, UNITS), bf16),
            jax.ShapeDtypeStruct((4, 2, 64, WIDTH), bf16),
            jax.ShapeDtypeStruct((128, WIDTH), bf16),
            jax.ShapeDtypeStruct((4, 2, 16, 128), f32),
        ],
        in_specs=[anyspace] * 6 + [vmem] * 7,
        out_specs=[anyspace] * 8,
        scratch_shapes=[
            VM((4, 4, 192, 768), bf16),
            VM((4, 4, 64, WIDTH), bf16),
            VM((4, 4, 128, UNITS), bf16),
            VM((4, 2, 144, WIDTH), bf16),
            VM((4, 2, 16, 128), bf16),
            VM((4, 2, 128, WIDTH), bf16),
            VM((2, 2, 8, 32, WIDTH), bf16),
            VM((4, 2, 128, WIDTH), bf16),
            VM((4, 144, WIDTH), bf16),
            VM((2, 80, WIDTH), bf16),
            VM((2, 144, WIDTH), bf16),
            VM((2, 64, WIDTH), bf16),
            VM((2, 128, WIDTH), bf16),
            VM((2, 8, 96, 768), bf16),
            VM((2, 8, 80, 768), bf16),
            VM((2, 8, 64, UNITS), bf16),
            VM((2, 8, 64, UNITS), bf16),
            VM((16, 16, 128), f32),
            VM((3, SEQ, 128), f32),
            VM((128, 128), f32),
            VM((SEQ, COLS), bf16),
            VM((SEQ, COLS), bf16),
            VM((SEQ, COLS), bf16),
            VM((SEQ, COLS), bf16),
            VM((SEQ, COLS), bf16),
            VM((SEQ, COLS), f32),
            VM((SEQ, COLS), f32),
            VM((SEQ, 768), bf16),
            VM((SEQ, UNITS), bf16),
            VM((SEQ, UNITS), bf16),
            VM((8, SEQ), f32),
            VM((32, 128), f32),
            VM((16, WIDTH), bf16),
            VM((128, WIDTH), bf16),
            VM((4, 4, 16, 128), f32),
            VM((3, 4, 16, 128), f32),
            VM((3, 16, 128), f32),
            dma((2, 16)),
            dma((2, 16)),
            dma((2, 16)),
            dma((2, 8)),
            dma((2, 8)),
            dma((2, 8)),
            dma((2, 16)),
            dma((2, 16)),
            dma((2, 16)),
            dma((2, 6)),
            dma((2, 5)),
            dma((2, 5)),
            dma((2, 8)),
            dma((2, 8)),
            dma((2, 8)),
            dma((2, 8)),
            dma((2, 16)),
            dma((2, 8)),
            dma((2, 8)),
            dma((2, 8)),
            dma((2, 5)),
            dma((9,)),
            dma((9,)),
            pltpu.SemaphoreType.REGULAR,
            pltpu.SemaphoreType.REGULAR,
        ],
        compiler_params=pltpu.CompilerParams(
            collective_id=1, has_side_effects=True, vmem_limit_bytes=62 * 1024 * 1024
        ),
        cost_estimate=pl.CostEstimate(
            flops=45 * 10**9, bytes_accessed=40 * 10**6, transcendentals=4 * 10**6
        ),
        name="layer",
    )(*operands)


def finish_kernel(
    gq,
    gu,
    gd,
    gp,
    gv,
    out,
    grad,
    log_sums,
    qkv_out,
    up_out,
    down_out,
    proj_out,
    gain_out,
    shift_out,
    proj_bias_out,
    down_bias_out,
    qkv_bias_out,
    up_bias_out,
    out_out,
    grad_out,
    log_sums_out,
):
    lane = lax.broadcasted_iota(jnp.int32, (1, 128), 1)
    for which in range(3):
        for c in range(8):
            part = gq[c, :, which * COLS : which * COLS + COLS]
            qkv_out[:, which * WIDTH + c * COLS : which * WIDTH + (c + 1) * COLS] = part.astype(f32)
    for pair in range(4):
        for m in range(8):
            a = gu[2 * pair, :, 128 * m : 128 * m + 128].astype(f32)
            b = gu[2 * pair + 1, :, 128 * m : 128 * m + 128].astype(f32)
            for odd in range(2):
                at = (2 * m + odd) * 512 + pair * 128
                up_out[:, at : at + 128] = halves_packed(a, b, odd == 1, lane)
    down_out[...] = gd[0].astype(f32)
    proj_out[...] = gp[...].astype(f32)
    out_out[...] = out[...]
    grad_out[...] = grad[...]
    log_sums_out[...] = log_sums[...]
    sums = jnp.sum(gv[...], axis=0)
    gain_out[...] = sums[0]
    shift_out[...] = sums[1]
    proj_bias_out[...] = sums[2]
    down_bias_out[...] = sums[2]
    for i in range(3):
        qkv_bias_out[128 * i : 128 * i + 128] = sums[3 + i]
    for i in range(4):
        up_bias_out[128 * i : 128 * i + 128] = sums[6 + i]


def finish_call(*operands):
    steps = 4
    rows = 128 // steps
    return pl.pallas_call(
        finish_kernel,
        grid=(steps,),
        out_shape=[
            jax.ShapeDtypeStruct((128, 3 * WIDTH), f32),
            jax.ShapeDtypeStruct((128, HIDDEN), f32),
            jax.ShapeDtypeStruct((512, WIDTH), f32),
            jax.ShapeDtypeStruct((128, WIDTH), f32),
            jax.ShapeDtypeStruct((128,), f32),
            jax.ShapeDtypeStruct((128,), f32),
            jax.ShapeDtypeStruct((128,), f32),
            jax.ShapeDtypeStruct((128,), f32),
            jax.ShapeDtypeStruct((384,), f32),
            jax.ShapeDtypeStruct((512,), f32),
            jax.ShapeDtypeStruct((128, WIDTH), bf16),
            jax.ShapeDtypeStruct((128, WIDTH), bf16),
            jax.ShapeDtypeStruct((32, 128), f32),
        ],
        in_specs=[
            pl.BlockSpec((8, rows, 768), lambda i: (0, i, 0)),
            pl.BlockSpec((8, rows, UNITS), lambda i: (0, i, 0)),
            pl.BlockSpec((1, 128, WIDTH), lambda i: (i, 0, 0)),
            pl.BlockSpec((rows, WIDTH), lambda i: (i, 0)),
            pl.BlockSpec((8, 16, 128), lambda i: (0, 0, 0)),
            pl.BlockSpec((rows, WIDTH), lambda i: (i, 0)),
            pl.BlockSpec((rows, WIDTH), lambda i: (i, 0)),
            pl.BlockSpec((32, 128), lambda i: (0, 0)),
        ],
        out_specs=[
            pl.BlockSpec((rows, 3 * WIDTH), lambda i: (i, 0)),
            pl.BlockSpec((rows, HIDDEN), lambda i: (i, 0)),
            pl.BlockSpec((128, WIDTH), lambda i: (i, 0)),
            pl.BlockSpec((rows, WIDTH), lambda i: (i, 0)),
            pl.BlockSpec((128,), lambda i: (0,)),
            pl.BlockSpec((128,), lambda i: (0,)),
            pl.BlockSpec((128,), lambda i: (0,)),
            pl.BlockSpec((128,), lambda i: (0,)),
            pl.BlockSpec((384,), lambda i: (0,)),
            pl.BlockSpec((512,), lambda i: (0,)),
            pl.BlockSpec((rows, WIDTH), lambda i: (i, 0)),
            pl.BlockSpec((rows, WIDTH), lambda i: (i, 0)),
            pl.BlockSpec((32, 128), lambda i: (0, 0)),
        ],
        compiler_params=pltpu.CompilerParams(vmem_limit_bytes=62 * 1024 * 1024),
        cost_estimate=pl.CostEstimate(
            flops=10**6, bytes_accessed=20 * 10**6, transcendentals=0
        ),
        name="finish",
    )(*operands)


def local(
    tokens,
    segments,
    ln_gain,
    ln_shift,
    qkv_weight,
    qkv_bias,
    proj_weight,
    proj_bias,
    up_weight,
    up_bias,
    down_weight,
    down_bias,
    cotangent,
):
    block_out, token_grad, log_sums, gq, gu, gd, gp, gv = layer_call(
        tokens[0],
        cotangent[0],
        qkv_weight,
        proj_weight,
        up_weight,
        down_weight,
        segments,
        ln_gain[None],
        ln_shift[None],
        proj_bias[None],
        down_bias[None],
        qkv_bias,
        up_bias,
    )
    qkv_grad, up_grad, down_grad, proj_grad, *vectors = finish_call(
        gq.reshape(8, 128, 768),
        gu.reshape(8, 128, UNITS),
        gd.reshape(4, 128, WIDTH),
        gp,
        gv.reshape(8, 16, 128),
        block_out,
        token_grad,
        log_sums,
    )
    return (
        vectors[6][None],
        vectors[7][None],
        vectors[8][None],
        vectors[0],
        vectors[1],
        qkv_grad,
        vectors[4],
        proj_grad,
        vectors[2],
        up_grad,
        vectors[5],
        down_grad,
        vectors[3],
    )


def solution(mesh):
    in_specs = (
        P("fsdp", "ctx", None),
        P("fsdp", "ctx"),
        P("fsdp"),
        P("fsdp"),
        P("fsdp", None),
        P("fsdp"),
        P("fsdp", None),
        P("fsdp"),
        P("fsdp", None),
        P("fsdp"),
        P("fsdp", None),
        P("fsdp"),
        P("fsdp", "ctx", None),
    )
    out_specs = (
        P("fsdp", "ctx", None),
        P("fsdp", "ctx", None),
        P("fsdp", None, "ctx"),
        P("fsdp"),
        P("fsdp"),
        P("fsdp", None),
        P("fsdp"),
        P("fsdp", None),
        P("fsdp"),
        P("fsdp", None),
        P("fsdp"),
        P("fsdp", None),
        P("fsdp"),
    )
    return jax.shard_map(local, mesh=mesh, in_specs=in_specs, out_specs=out_specs, check_vma=False)
```

```python
from functools import partial
import math

import jax
import jax.numpy as jnp
from jax import lax
from jax.experimental import pallas as pl
from jax.experimental.pallas import tpu as pltpu
from jax.sharding import PartitionSpec as P

HEAD = 64
ROT_DIMS = 32
SEQ = 1024
WIDTH = 2048
HIDDEN = 8192
OWN_HEADS = 4
COLS = 256
UNITS = 1024

epsilon = 1e-05
masked_score = -1e30
f32 = jnp.float32
bf16 = jnp.bfloat16
MESH = pl.DeviceIdType.MESH
VM = pltpu.VMEM


def dot(a, b, ca, cb):
    return lax.dot_general(a, b, (((ca,), (cb,)), ((), ())), preferred_element_type=f32)


def place():
    c = lax.axis_index("ctx")
    f = lax.axis_index("fsdp")
    return c, f, c // 2, c % 2, f // 4, f % 4


def other_core():
    c, f, z, core, y, x = place()
    return (z * 2 + 1 - core, f)


def up1(i):
    return (i + 1) % 4


def down1(i):
    return (i + 3) % 4


def over(i):
    return (i + 2) % 4


class Copies:
    def __init__(self, send, recv):
        self.send, self.recv = send, recv
        self.started = []

    def start(self, k, src, dst, device):
        copy = pltpu.make_async_remote_copy(
            src_ref=src,
            dst_ref=dst,
            send_sem=self.send.at[k],
            recv_sem=self.recv.at[k],
            device_id=device,
            device_id_type=MESH,
        )
        copy.start()
        self.started.append(copy)

    def arrived(self, k, dst):
        pltpu.make_async_remote_copy(
            src_ref=dst,
            dst_ref=dst,
            send_sem=self.send.at[k],
            recv_sem=self.recv.at[k],
            device_id=other_core(),
            device_id_type=MESH,
        ).wait_recv()

    def sent(self):
        for copy in self.started:
            copy.wait_send()
        self.started = []


def plane_gather(w, cuts, copies):
    c, f, z, core, y, x = place()
    r0, r1, r2, r3, r4 = cuts
    first, last = pl.ds(r0, r2 - r0), pl.ds(r2, r4 - r2)
    q0, q1, q2, q3 = (pl.ds(a, b - a) for a, b in zip(cuts[:-1], cuts[1:]))
    xu, xd, xo = up1(x), down1(x), over(x)
    yu, yd, yo = up1(y), down1(y), over(y)
    to_xu, to_xd = (c, y * 4 + xu), (c, y * 4 + xd)
    to_yu, to_yd = (c, yu * 4 + x), (c, yd * 4 + x)
    lo, hi = pl.ds(0, 2), pl.ds(2, 2)
    every = pl.ds(0, 4)

    def send(k, part, device):
        copies.start(k, w.at[part], w.at[part], device)

    def got(k, part):
        copies.arrived(k, w.at[part])

    send(0, (y, x, first), to_xu)
    send(1, (y, x, first), to_xd)
    send(2, (y, x, last), to_yu)
    send(3, (y, x, last), to_yd)
    yield
    got(0, (y, xd, first))
    send(4, (y, xd, q0), to_xu)
    got(1, (y, xu, first))
    send(5, (y, xu, q1), to_xd)
    got(2, (yd, x, last))
    send(6, (yd, x, q2), to_yu)
    got(3, (yu, x, last))
    send(7, (yu, x, q3), to_yd)
    yield
    got(4, (y, xo, q0))
    got(5, (y, xo, q1))
    send(8, (y, every, first), to_yu)
    send(9, (y, every, first), to_yd)
    got(6, (yo, x, q2))
    got(7, (yo, x, q3))
    send(10, (every, x, last), to_xu)
    send(11, (every, x, last), to_xd)
    yield
    got(8, (yd, every, first))
    send(12, (yd, lo, first), to_yu)
    got(9, (yu, every, first))
    send(13, (yu, hi, first), to_yd)
    got(10, (every, xd, last))
    send(14, (lo, xd, last), to_xu)
    got(11, (every, xu, last))
    send(15, (hi, xu, last), to_xd)
    yield
    got(12, (yo, lo, first))
    got(13, (yo, hi, first))
    got(14, (lo, xo, last))
    got(15, (hi, xo, last))
    yield


def line_gather(t, cuts, copies, own=None):
    c, f, z, core, y, x = place()
    r0, r1, r2 = cuts
    h0, h1 = pl.ds(r0, r1 - r0), pl.ds(r1, r2 - r1)
    zu, zd, zo = up1(z), down1(z), over(z)
    to_zu, to_zd, to_core = (zu * 2 + core, f), (zd * 2 + core, f), (z * 2 + 1 - core, f)
    other = 1 - core

    def send(k, part, device):
        copies.start(k, t.at[part], t.at[part], device)

    def got(k, part):
        copies.arrived(k, t.at[part])

    mine = t.at[z, core]
    own = mine if own is None else own
    copies.start(0, own, mine, to_zu)
    copies.start(1, own, mine, to_zd)
    copies.start(2, own, mine, to_core)
    yield
    got(0, (zd, core))
    send(3, (zd, core, h0), to_zu)
    got(1, (zu, core))
    send(4, (zu, core, h1), to_zd)
    send(5, (zd, core), to_core)
    send(6, (zu, core), to_core)
    yield
    got(3, (zo, core, h0))
    got(4, (zo, core, h1))
    send(7, (zo, core), to_core)
    yield
    got(2, (z, other))
    got(5, (zd, other))
    got(6, (zu, other))
    got(7, (zo, other))
    yield


def enter():
    c, f, z, core, y, x = place()
    barrier = pltpu.get_barrier_semaphore()
    for device in (
        (c, y * 4 + up1(x)),
        (c, y * 4 + down1(x)),
        (c, up1(y) * 4 + x),
        (c, down1(y) * 4 + x),
        (up1(z) * 2 + core, f),
        (down1(z) * 2 + core, f),
        (z * 2 + 1 - core, f),
    ):
        pl.semaphore_signal(barrier, inc=1, device_id=device, device_id_type=MESH)
    owner = c * 2 + f // 8

    @pl.when(owner != f)
    def _():
        pl.semaphore_signal(barrier, inc=1, device_id=(c, owner), device_id_type=MESH)

    for j in range(8):
        target = (f % 2) * 8 + j

        @pl.when((f // 2 == c) & (target != f))
        def _():
            pl.semaphore_signal(barrier, inc=1, device_id=(c, target), device_id_type=MESH)

    count = 7 + jnp.where(f // 2 == c, jnp.where(f // 8 == f % 2, 7, 8), 0)
    count = count + jnp.where(owner != f, 1, 0)
    pl.semaphore_wait(barrier, count)


def turn(fields, cos, low_sin, high_sin):
    return (
        fields * cos + pltpu.roll(fields, 112, 1) * low_sin + pltpu.roll(fields, 16, 1) * high_sin
    )


def turn_back(grads, cos, low_sin, high_sin):
    return (
        grads * cos + pltpu.roll(grads * low_sin, 16, 1) + pltpu.roll(grads * high_sin, 112, 1)
    )


def halves_packed(a, b, odd, lane):
    moved_a, moved_b = pltpu.roll(a, 64, 1), pltpu.roll(b, 64, 1)
    return jnp.where(lane < 64, jnp.where(odd, moved_a, a), jnp.where(odd, b, moved_b))


def add_into(target, part, *others):
    total = target[part].astype(f32)
    for ref, piece in others:
        total = total + ref[piece].astype(f32)
    target[part] = total.astype(target.dtype)


def plane_reduce(g, cuts, ra, rb, copies):
    c, f, z, core, y, x = place()
    r0, r1, r2, r3, r4 = cuts
    first, last = pl.ds(r0, r2 - r0), pl.ds(r2, r4 - r2)
    q0, q1, q2, q3 = (pl.ds(a, b - a) for a, b in zip(cuts[:-1], cuts[1:]))
    s0, s1, s2, s3 = (pl.ds(0, b - a) for a, b in zip(cuts[:-1], cuts[1:]))
    xu, xd, xo = up1(x), down1(x), over(x)
    yu, yd, yo = up1(y), down1(y), over(y)
    to_xu, to_xd = (c, y * 4 + xu), (c, y * 4 + xd)
    to_yu, to_yd = (c, yu * 4 + x), (c, yd * 4 + x)
    lo, hi, every = pl.ds(0, 2), pl.ds(2, 2), pl.ds(0, 4)
    near, far = pl.ds(0, 2), pl.ds(2, 4)

    def send(k, part, ref, piece, device):
        copies.start(k, g.at[part], ref.at[piece], device)

    def got(k, ref, piece):
        copies.arrived(k, ref.at[piece])

    send(0, (yo, lo, first), ra, (0, near), to_yu)
    send(1, (yo, hi, first), ra, (1, near), to_yd)
    send(2, (lo, xo, last), rb, (0, near), to_xu)
    send(3, (hi, xo, last), rb, (1, near), to_xd)
    yield
    got(0, ra, (0, near))
    add_into(g, (yu, lo, first), (ra, (0, near)))
    send(4, (yu, every, first), ra, (0, far), to_yu)
    got(1, ra, (1, near))
    add_into(g, (yd, hi, first), (ra, (1, near)))
    send(5, (yd, every, first), ra, (1, far), to_yd)
    got(2, rb, (0, near))
    add_into(g, (lo, xu, last), (rb, (0, near)))
    send(6, (every, xu, last), rb, (0, far), to_xu)
    got(3, rb, (1, near))
    add_into(g, (hi, xd, last), (rb, (1, near)))
    send(7, (every, xd, last), rb, (1, far), to_xd)
    yield
    got(4, ra, (0, far))
    got(5, ra, (1, far))
    add_into(g, (y, every, first), (ra, (0, far)), (ra, (1, far)))
    send(8, (y, xo, q0), ra, (0, 6, s0), to_xu)
    send(9, (y, xo, q1), ra, (1, 6, s1), to_xd)
    got(6, rb, (0, far))
    got(7, rb, (1, far))
    add_into(g, (every, x, last), (rb, (0, far)), (rb, (1, far)))
    send(10, (yo, x, q2), rb, (0, 6, s2), to_yu)
    send(11, (yo, x, q3), rb, (1, 6, s3), to_yd)
    yield
    got(8, ra, (0, 6, s0))
    add_into(g, (y, xu, q0), (ra, (0, 6, s0)))
    send(12, (y, xu, first), ra, (0, 7), to_xu)
    got(9, ra, (1, 6, s1))
    add_into(g, (y, xd, q1), (ra, (1, 6, s1)))
    send(13, (y, xd, first), ra, (1, 7), to_xd)
    got(10, rb, (0, 6, s2))
    add_into(g, (yu, x, q2), (rb, (0, 6, s2)))
    send(14, (yu, x, last), rb, (0, 7), to_yu)
    got(11, rb, (1, 6, s3))
    add_into(g, (yd, x, q3), (rb, (1, 6, s3)))
    send(15, (yd, x, last), rb, (1, 7), to_yd)
    yield
    got(12, ra, (0, 7))
    got(13, ra, (1, 7))
    add_into(g, (y, x, first), (ra, (0, 7)), (ra, (1, 7)))
    got(14, rb, (0, 7))
    got(15, rb, (1, 7))
    add_into(g, (y, x, last), (rb, (0, 7)), (rb, (1, 7)))
    yield


def line_reduce(g, cuts, rc, r1, r2, copies):
    c, f, z, core, y, x = place()
    c0, c1, c2 = cuts
    h0, h1 = pl.ds(c0, c1 - c0), pl.ds(c1, c2 - c1)
    s0, s1 = pl.ds(0, c1 - c0), pl.ds(0, c2 - c1)
    zu, zd, zo = up1(z), down1(z), over(z)
    to_zu, to_zd, to_core = (zu * 2 + core, f), (zd * 2 + core, f), (z * 2 + 1 - core, f)
    every = pl.ds(0, 4)
    copies.start(0, g.at[every, 1 - core], rc, to_core)
    yield
    copies.arrived(0, rc)

    def add_row(i, carry):
        add_into(g, (i, core), (rc, (i,)))
        return carry

    lax.fori_loop(0, 4, add_row, 0)
    copies.start(1, g.at[zo, core, h0], r1.at[0, s0], to_zu)
    copies.start(2, g.at[zo, core, h1], r1.at[1, s1], to_zd)
    yield
    copies.arrived(1, r1.at[0, s0])
    add_into(g, (zu, core, h0), (r1, (0, s0)))
    copies.start(3, g.at[zu, core], r2.at[0], to_zu)
    copies.arrived(2, r1.at[1, s1])
    add_into(g, (zd, core, h1), (r1, (1, s1)))
    copies.start(4, g.at[zd, core], r2.at[1], to_zd)
    yield
    copies.arrived(3, r2.at[0])
    copies.arrived(4, r2.at[1])
    yield


def vector_reduce(g, ry, rx, copies):
    c, f, z, core, y, x = place()
    xu, xd, xo = up1(x), down1(x), over(x)
    yu, yd, yo = up1(y), down1(y), over(y)
    to_xu, to_xd = (c, y * 4 + xu), (c, y * 4 + xd)
    to_yu, to_yd = (c, yu * 4 + x), (c, yd * 4 + x)
    copies.start(0, g.at[yo], ry.at[0], to_yu)
    yield
    copies.arrived(0, ry.at[0])
    add_into(g, (yu,), (ry, (0,)))
    copies.start(1, g.at[yu], ry.at[1], to_yu)
    copies.start(2, g.at[yd], ry.at[2], to_yd)
    yield
    copies.arrived(1, ry.at[1])
    copies.arrived(2, ry.at[2])
    add_into(g, (y,), (ry, (1,)), (ry, (2,)))
    copies.start(3, g.at[y, xo], rx.at[0], to_xu)
    yield
    copies.arrived(3, rx.at[0])
    add_into(g, (y, xu), (rx, (0,)))
    copies.start(4, g.at[y, xu], rx.at[1], to_xu)
    copies.start(5, g.at[y, xd], rx.at[2], to_xd)
    yield
    copies.arrived(4, rx.at[1])
    copies.arrived(5, rx.at[2])
    add_into(g, (y, x), (rx, (1,)), (rx, (2,)))
    yield


GATHER1 = (0, 48, 96, 144, 192)
REDUCE1 = (0, 48, 96, 128, 176)
CUTS2 = (0, 16, 32, 48, 64)
CUTS3 = (0, 32, 64, 96, 128)
PROJ = ((0, 768), (768, 768), (1536, 512))


ORDER = (
    "load_t", "gather_t", "gather_s", "load_1", "gather1", "pack", "load_2", "gather2", "gather1",
    "gather3", "gather1", "gather_t", "gather_s", "gather3", "load_u", "gather_u", "gather_t",
    "gather_s", "gather2", "gather_t", "gather_s", "gather1", "gather2", "gather3", "tables",
    "gather_u", "gather1", "stats", "norm", "gather_u", "project", "gather_u", "dctx", "att3",
    "att2", "gather3", "att1", "gather2", "att0", "gp", "join", "dn1a", "dn1b", "gqa", "gqb",
    "gather3", "reduce1", "up_bias", "ff1a", "ff1b", "ff1c", "ff1d", "gather2", "reduce1", "ff2a",
    "ff2b", "ff2c", "ff2d", "dn2a", "dn2b", "reduce_d", "sent3", "gua", "reduce1", "gub",
    "free_n", "reduce3", "reduce_d", "free_rc", "lse", "reduce1", "oa", "reduce3", "reduce_d",
    "ob", "wait_rc", "reduce_o", "sent2", "gda", "reduce1", "spread_q", "proj_owner", "gdb",
    "reload", "wait_n", "reduce2", "reduce_d", "reduce_o", "reduce3", "fgrad", "reduce2", "vec",
    "spread_q", "proj_along", "reduce_o", "reduce3", "spread_q", "proj_further", "reduce_v",
    "reduce2", "reduce3", "reduce_v", "spread_u", "proj_across", "put_u", "reduce2", "reduce2",
    "reduce_v", "spread_d", "put_d", "spread_u", "reduce_v", "reduce_o", "fout", "reduce_v",
    "spread_v", "put_v", "spread_d", "spread_u", "spread_v", "spread_u", "spread_d", "spread_v",
    "spread_q", "spread_d", "spread_v", "proj_end",
)


def layer_kernel(
    tokens,
    cotangent,
    qkv_weight,
    proj_weight,
    up_weight,
    down_weight,
    seg,
    gain_in,
    shift_in,
    proj_bias_in,
    down_bias_in,
    qkv_bias_in,
    up_bias_in,
    block_out,
    token_grad,
    lse_out,
    gq_out,
    gu_out,
    gd_out,
    gp_out,
    gv_out,
    w1,
    w2,
    w3,
    t,
    ids,
    u,
    n,
    zd,
    rc,
    zo_r1,
    zo_r2,
    zd_r1,
    zd_r2,
    ra1,
    rb1,
    ra3,
    rb3,
    vecs,
    tab,
    begin_cols,
    q,
    k,
    v,
    dctx,
    ctx,
    dk,
    dv,
    dproj,
    act,
    dhid,
    lse,
    lse_own,
    pt,
    gp,
    gv,
    ry,
    rx,
    sem1,
    sem2,
    sem3,
    sem_t,
    sem_u,
    sem_i,
    sem_r1,
    sem_r2,
    sem_r3,
    sem_v,
    sem_zo,
    sem_zd,
    sem_lq,
    sem_lu,
    sem_ld,
    sem_lv,
    sem_r5,
    sem_le,
    sem_s,
    sem_p,
    sem_b,
    sem_l,
    sem_o,
    n_free,
    rc_free,
):
    c, f, z, core, y, x = place()
    lane = lax.broadcasted_iota(jnp.int32, (1, 128), 1)
    odd = core == 1
    owner = c * 2 + f // 8
    own_rows = f // 2 == c
    zo = t

    loads = [
        pltpu.make_async_copy(tokens, t.at[z, core, pl.ds(0, 128)], sem_l.at[0]),
        pltpu.make_async_copy(cotangent, u.at[z, core], sem_l.at[1]),
        pltpu.make_async_copy(
            down_weight.at[pl.ds(pl.multiple_of(c * 64, 64), 64)], w2.at[y, x], sem_l.at[2]
        ),
    ]
    for i in range(3):
        loads.append(
            pltpu.make_async_copy(
                qkv_weight.at[:, pl.ds(pl.multiple_of(i * WIDTH + c * COLS, 128), COLS)],
                w1.at[y, x, pl.ds(0, 128), pl.ds(i * COLS, COLS)],
                sem_l.at[3 + i],
            )
        )
    for copy in loads:
        copy.start()
    for i in range(16):
        pltpu.make_async_copy(
            up_weight.at[:, pl.ds(pl.multiple_of(i * 512 + (c // 2) * 128, 128), 128)],
            q.at[pl.ds(i // 2 * 128, 128), pl.ds(i % 2 * 128, 128)],
            sem_l.at[6],
        ).start()
    vector_list = [gain_in[...], shift_in[...], proj_bias_in[...], down_bias_in[...]]
    vector_list += [qkv_bias_in[128 * i : 128 * i + 128].reshape(1, 128) for i in range(3)]
    vector_list += [up_bias_in[128 * i : 128 * i + 128].reshape(1, 128) for i in range(4)]
    vector_list = [vector.astype(f32) for vector in vector_list] + [jnp.zeros((5, 128), f32)]
    w1[y, x, 176:192, 0:128] = jnp.concatenate(vector_list, axis=0).astype(bf16)
    w1[y, x, 176:192, 128:768] = jnp.zeros((16, 640), bf16)
    w1[y, x, 160:176, 512:768] = jnp.zeros((16, 256), bf16)
    seg_rows = jnp.broadcast_to(seg[...].astype(f32), (16, 128))
    ids[z, core] = seg_rows

    enter()

    def both_ways(sems):
        return Copies(sems.at[0], sems.at[1])

    copies1, copies2, copies3 = both_ways(sem1), both_ways(sem2), both_ways(sem3)
    copies_t, copies_u, copies_s = both_ways(sem_t), both_ways(sem_u), both_ways(sem_i)
    copies_r1, copies_r2, copies_r3 = both_ways(sem_r1), both_ways(sem_r2), both_ways(sem_r3)
    copies_v = both_ways(sem_v)
    copies_zo, copies_zd = both_ways(sem_zo), both_ways(sem_zd)
    copies_lq, copies_lu = both_ways(sem_lq), both_ways(sem_lu)
    copies_ld, copies_lv = both_ways(sem_ld), both_ways(sem_lv)
    copies_r5, copies_le = both_ways(sem_r5), both_ways(sem_le)
    gather1 = plane_gather(w1, GATHER1, copies1)
    gather2 = plane_gather(w2, CUTS2, copies2)
    gather3 = plane_gather(w3, CUTS3, copies3)
    gather_t = line_gather(t.at[:, :, pl.ds(0, 128)], (0, 64, 128), copies_t)
    gather_s = line_gather(ids, (0, 8, 16), copies_s)
    gather_u = line_gather(u, (0, 64, 128), copies_u)
    reduce1 = plane_reduce(w1, REDUCE1, ra1, rb1, copies_r1)
    left, right = pl.ds(0, 1024), pl.ds(1024, 1024)
    into = (slice(None),) * 3
    reduce2a, reduce2b = [
        plane_reduce(
            w2.at[into + (part,)],
            CUTS2,
            n.at[(0,) + into + (part,)],
            n.at[(1,) + into + (part,)],
            copies,
        )
        for part, copies in ((left, copies_r2), (right, copies_r5))
    ]
    reduce3 = plane_reduce(w3, CUTS3, ra3, rb3, copies_r3)
    reduce_v = vector_reduce(gv, ry, rx, copies_v)
    reduce_o = line_reduce(zo, (0, 64, 144), rc, zo_r1, zo_r2, copies_zo)
    reduce_d = line_reduce(zd, (0, 64, 128), rc.at[:, pl.ds(0, 128)], zd_r1, zd_r2, copies_zd)
    spread_q = line_gather(gq_out, (0, 64, 128), copies_lq, w1.at[y, x, pl.ds(0, 128)])
    spread_u = line_gather(gu_out, (0, 64, 128), copies_lu, w3.at[y, x])
    reduce2 = plane_reduce(w2, CUTS2, n.at[0], n.at[1], copies_r2)
    spread_d = line_gather(gd_out, (0, 32, 64), copies_ld, w2.at[y, x])
    spread_da, spread_db = [
        line_gather(gd_out.at[into + (part,)], (0, 32, 64), copies, w2.at[y, x, :, part])
        for part, copies in ((left, copies_ld), (right, copies_le))
    ]
    spread_v = line_gather(gv_out, (0, 8, 16), copies_lv, gv.at[y, x])

    outs = []

    def put(src, dst):
        copy = pltpu.make_async_copy(src, dst, sem_o.at[len(outs)])
        copy.start()
        outs.append(copy)

    kept = {}

    def scatter(j, target):
        return pltpu.make_async_remote_copy(
            src_ref=proj_weight.at[pl.ds(16 * j, 16)],
            dst_ref=pt,
            send_sem=sem_s.at[0, j],
            recv_sem=sem_s.at[1, 0],
            device_id=(c, target),
            device_id_type=MESH,
        )

    def load_1():
        for j in range(8):
            target = (f % 2) * 8 + j

            @pl.when(own_rows & (target != f))
            def _():
                scatter(j, target).start()

            @pl.when(own_rows & (target == f))
            def _():
                local = pltpu.make_async_copy(
                    proj_weight.at[pl.ds(16 * j, 16)], pt, sem_s.at[1, 1]
                )
                local.start()
                local.wait()

        for i in (3, 4, 5):
            loads[i].wait()

        @pl.when(owner != f)
        def _():
            pltpu.make_async_remote_copy(
                src_ref=pt,
                dst_ref=pt,
                send_sem=sem_s.at[0, 0],
                recv_sem=sem_s.at[1, 0],
                device_id=other_core(),
                device_id_type=MESH,
            ).wait_recv()

        for j, (start, size) in enumerate(PROJ):
            w1[y, x, 128 + 16 * j : 144 + 16 * j, 0:size] = pt[:, start : start + size]

    def pack():
        pltpu.make_async_copy(q, q, sem_l.at[6]).wait()
        for m in range(8):
            strip = q[128 * m : 128 * m + 128, :].astype(f32)
            packed = halves_packed(strip[:, :128], strip[:, 128:], odd, lane)
            w3[y, x, :, 128 * m : 128 * m + 128] = packed.astype(bf16)

    def tables():
        in_head = lane % 64
        inverse = jnp.exp((lane % 16).astype(f32) * (-math.log(10000.0) / (ROT_DIMS // 2)))
        inverse = jnp.where(in_head < ROT_DIMS, inverse, 0.0)
        row_angles = lax.broadcasted_iota(jnp.int32, (128, 1), 0).astype(f32) * inverse
        row_cos, row_sin = jnp.cos(row_angles), jnp.sin(row_angles)
        seg_all = jnp.concatenate(
            [ids[b // 2, b % 2, 0:1, :] for b in range(8)], axis=0
        )
        seg_cols = jnp.transpose(seg_all)
        firsts = [jnp.sum((seg_all < float(d)).astype(f32), keepdims=True) for d in range(1, 4)]
        begins = jnp.zeros((128, 8), f32)
        row = lax.broadcasted_iota(jnp.int32, (32, 1), 0)
        shifts = (row // 4 * 128).astype(f32)
        for d in range(1, 4):
            begins = jnp.where(seg_cols == float(d), firsts[d - 1], begins)
            shifts = shifts - jnp.where(row % 4 == d, firsts[d - 1], 0.0)
        begin_cols[:, 0:8] = begins
        shift_cos, shift_sin = jnp.cos(shifts * inverse), jnp.sin(shifts * inverse)
        for b in range(8):
            rows = pl.ds(b * 128, 128)
            own = seg_cols[:, b : b + 1]
            block_cos, block_sin = shift_cos[4 * b : 4 * b + 1], shift_sin[4 * b : 4 * b + 1]
            for d in range(1, 4):
                at = 4 * b + d
                block_cos = jnp.where(own == float(d), shift_cos[at : at + 1], block_cos)
                block_sin = jnp.where(own == float(d), shift_sin[at : at + 1], block_sin)
            sin = row_sin * block_cos + row_cos * block_sin
            tab[0, rows, :] = row_cos * block_cos - row_sin * block_sin
            tab[1, rows, :] = jnp.where(in_head < 16, -sin, 0.0)
            tab[2, rows, :] = jnp.where((in_head >= 16) & (in_head < 32), sin, 0.0)

    def joined(which):
        return jnp.concatenate([vecs[i, which : which + 1, :] for i in range(16)], axis=1)

    def norm_source(i):
        return t[i // 4, i // 2 % 2, pl.ds(pl.multiple_of(i % 2 * 64, 64), 64), :].astype(f32)

    def statistics():
        def row_statistics(i, carry):
            values = norm_source(i)
            average = jnp.mean(values, axis=-1, keepdims=True)
            centered = values - average
            variance = jnp.mean(centered * centered, axis=-1, keepdims=True)
            rows = pl.ds(pl.multiple_of(i * 64, 64), 64)
            dk[rows, 0:128] = jnp.broadcast_to(average, (64, 128))
            dk[rows, 128:256] = jnp.broadcast_to(lax.rsqrt(variance + epsilon), (64, 128))
            return carry

        lax.fori_loop(0, 16, row_statistics, 0)

    def norm():
        vecs[...] = w1[:, :, 176:192, 0:128].reshape(16, 16, 128).astype(f32)
        gain, shift = joined(0), joined(1)

        def norm_rows(i, carry):
            rows = pl.ds(pl.multiple_of(i * 64, 64), 64)
            standard = (norm_source(i) - dk[rows, 0:1]) * dk[rows, 128:129]
            normed = (standard * gain + shift).astype(bf16)
            n[i // 8, i // 4 % 2, pl.ds(i % 4 * 2, 2)] = normed.reshape(2, 32, WIDTH)
            return carry

        lax.fori_loop(0, 16, norm_rows, 0)

    def project():
        parts = []
        for which in range(3):
            for i in range(2):
                at = which * 16 + c * 2 + i
                parts.append(vecs[at // 3, pl.ds(4 + at % 3, 1), :])
        qkv_bias = jnp.concatenate(parts, axis=1)

        def project_rows(m, carry):
            rows = pl.ds(pl.multiple_of(m * 512, 512), 512)
            turns = [tab[i, rows, :] for i in range(3)]
            right = w1[:, :, pl.ds(0, 128), :].reshape(WIDTH, 768)
            fields = dot(n[m].reshape(512, WIDTH), right, 1, 0) + qkv_bias
            for which, target in enumerate((q, k, v)):
                for pair in range(2):
                    at = which * COLS + pair * 128
                    both = fields[:, at : at + 128]
                    if which < 2:
                        both = turn(both, *turns)
                    if which == 0:
                        both = both * 0.125
                    target[rows, pair * 128 : pair * 128 + 128] = both.astype(bf16)
            return carry

        lax.fori_loop(0, 2, project_rows, 0)

    def context_grad():
        grads = jnp.zeros((SEQ, COLS), f32)
        for j, (start, size) in enumerate(PROJ):
            left = u[:, :, :, pl.ds(start, size)].reshape(SEQ, size)
            right = w1[:, :, pl.ds(128 + 16 * j, 16), pl.ds(0, size)].reshape(COLS, size)
            grads = grads + dot(left, right, 1, 1)
        dctx[...] = grads.astype(bf16)

    def attention(block):
        reach = (block + 1) * 256
        rows = pl.ds(block * 256, 256)
        keys = pl.ds(0, reach)
        begin = jnp.concatenate(
            [begin_cols[:, 2 * block + i : 2 * block + i + 1] for i in range(2)], axis=0
        )
        key_index = lax.broadcasted_iota(jnp.int32, (1, reach), 1).astype(f32)
        row_index = (lax.broadcasted_iota(jnp.int32, (256, 1), 0) + block * 256).astype(f32)

        def attend(pair, carry):
            lanes = pl.ds(pl.multiple_of(pair * 128, 128), 128)
            qp, kp, vp, dp = q[rows, lanes], k[keys, lanes], v[keys, lanes], dctx[rows, lanes]
            results = []
            for half in range(2):
                here = (lane >= 64) == (half == 1)
                qh = jnp.where(here, qp, jnp.zeros((), bf16))
                dh = jnp.where(here, dp, jnp.zeros((), bf16))
                scores = dot(qh, kp, 1, 1)
                allowed = (key_index >= begin) & (key_index <= row_index)
                scores = jnp.where(allowed, scores, masked_score)
                highest = jnp.max(scores, axis=1, keepdims=True)
                weights = jnp.exp(scores - highest)
                total = jnp.sum(weights, axis=1, keepdims=True)
                probs = weights * (1.0 / total)
                log_sum = jnp.broadcast_to(highest + jnp.log(total), (256, 128))
                lse[pl.ds(pair * 2 + half, 1), rows] = jnp.transpose(log_sum)[0:1, :]
                probs_low = probs.astype(bf16)
                d_probs = dot(dh, vp, 1, 1)
                delta = jnp.sum(probs * d_probs, axis=1, keepdims=True)
                d_scores = (probs * (d_probs - delta)).astype(bf16)
                results.append(
                    (
                        dot(probs_low, vp, 1, 0),
                        dot(d_scores, kp, 1, 0),
                        dot(d_scores, qp, 0, 0),
                        dot(probs_low, dp, 0, 0),
                    )
                )
            context, d_queries, d_keys, d_values = [
                jnp.where(lane < 64, a, b) for a, b in zip(*results)
            ]
            ctx[rows, lanes] = context.astype(bf16)
            turns = [tab[i, rows, :] for i in range(3)]
            dproj[rows, lanes] = turn_back(d_queries * 0.125, *turns).astype(bf16)
            if block == 3:
                dk[keys, lanes] = d_keys
                dv[keys, lanes] = d_values
            else:
                dk[keys, lanes] += d_keys
                dv[keys, lanes] += d_values
            return carry

        lax.fori_loop(0, 2, attend, 0)

    def join():
        def join_rows(m, carry):
            rows = pl.ds(pl.multiple_of(m * 256, 256), 256)
            turns = [tab[i, rows, :] for i in range(3)]
            for pair in range(2):
                lanes = pl.ds(pair * 128, 128)
                turned = turn_back(dk[rows, lanes], *turns)
                dproj[rows, pl.ds(COLS + pair * 128, 128)] = turned.astype(bf16)
                dproj[rows, pl.ds(2 * COLS + pair * 128, 128)] = dv[rows, lanes].astype(bf16)
            return carry

        lax.fori_loop(0, 4, join_rows, 0)

    def normed_part(i, carry):
        columns = pl.ds(pl.multiple_of(i * 512, 512), 512)
        total = dot(dproj[...], w1[i, :, pl.ds(0, 128), :].reshape(512, 768), 1, 1)
        zd[:, :, :, columns] = total.astype(bf16).reshape(4, 2, 128, 512)
        return carry

    def qkv_part(i, carry):
        columns = pl.ds(pl.multiple_of(i * 512, 512), 512)
        grads = dot(n[:, :, :, :, columns].reshape(SEQ, 512), dproj[...], 0, 0).astype(bf16)
        w1[i, :, pl.ds(0, 128), :] = grads.reshape(4, 128, 768)
        return carry

    def proj_part():
        copies1.sent()
        copies_t.sent()
        for j, (start, size) in enumerate(PROJ):
            columns = pl.ds(start, size)
            part = (slice(None), slice(None), pl.ds(128 + 16 * j, 16), pl.ds(0, size))
            total = dot(ctx[...], w1[part].reshape(COLS, size), 1, 0)
            zo[:, :, pl.ds(0, 128), columns] = total.astype(bf16).reshape(4, 2, 128, size)
            right = u[:, :, :, columns].reshape(SEQ, size)
            w1[part] = dot(ctx[...], right, 0, 0).astype(bf16).reshape(4, 4, 16, size)

    def log_sums():
        for b in range(8):
            part = jnp.concatenate(
                [lse[j : j + 1, b * 128 : b * 128 + 128] for j in range(4)], axis=1
            )
            wide = jnp.concatenate([jnp.where(c % 4 == s, part, 0.0) for s in range(4)], axis=1)
            high = wide.astype(bf16).astype(f32)
            at = lax.broadcasted_iota(jnp.int32, (16, 1), 0)
            both = jnp.where(at == c // 4, high, jnp.where(at == 2 + c // 4, wide - high, 0.0))
            zo[b // 2, b % 2, 128:144, :] = both.astype(bf16)

    def feed(i, carry):
        rows = pl.ds(pl.multiple_of(i // 2 * 512, 512), 512)
        columns = pl.ds(pl.multiple_of(i % 2 * 512, 512), 512)
        right = w3[:, :, :, columns].reshape(WIDTH, 512)
        bias = jnp.where(i % 2 == 0, kept["up_bias"][:, 0:512], kept["up_bias"][:, 512:1024])
        h = dot(n[i // 2].reshape(512, WIDTH), right, 1, 0) + bias
        square = h * h
        tanh = jnp.tanh(0.7978845608028654 * (h + 0.044715 * square * h))
        half = 0.5 * (1.0 + tanh)
        slope = half + 0.5 * h * (1.0 - tanh * tanh) * (
            0.7978845608028654 * (1.0 + 3.0 * 0.044715 * square)
        )
        act[rows, columns] = (h * half).astype(bf16)
        dhid[rows, columns] = slope.astype(bf16)
        return carry

    def up_bias():
        parts = []
        for m in range(8):
            a = vecs[2 * m, pl.ds(7 + c // 2, 1), :]
            b = vecs[2 * m + 1, pl.ds(7 + c // 2, 1), :]
            parts.append(halves_packed(a, b, odd, lane))
        kept["up_bias"] = jnp.concatenate(parts, axis=1)

    def feed_back(i, carry):
        rows = pl.ds(pl.multiple_of(i // 2 * 512, 512), 512)
        columns = pl.ds(pl.multiple_of(i % 2 * 512, 512), 512)
        left = u[pl.ds(i // 2 * 2, 2)].reshape(512, WIDTH)
        d_act = dot(left, w2[pl.ds(i % 2 * 2, 2)].reshape(512, WIDTH), 1, 1)
        dhid[rows, columns] = (d_act * dhid[rows, columns].astype(f32)).astype(bf16)
        return carry

    def normed_more(i, carry):
        columns = pl.ds(pl.multiple_of(i * 512, 512), 512)
        total = dot(dhid[...], w3[i].reshape(512, UNITS), 1, 1).reshape(4, 2, 128, 512)
        total = total + zd[:, :, :, columns].astype(f32)
        zd[:, :, :, columns] = total.astype(bf16)
        return carry

    def up_part(i, carry):
        columns = pl.ds(pl.multiple_of(i * 512, 512), 512)
        grads = dot(n[:, :, :, :, columns].reshape(SEQ, 512), dhid[...], 0, 0).astype(bf16)
        w3[i] = grads.reshape(4, 128, UNITS)
        return carry

    def free_n():
        for device in (
            (c, y * 4 + up1(x)),
            (c, y * 4 + down1(x)),
            (c, up1(y) * 4 + x),
            (c, down1(y) * 4 + x),
        ):
            pl.semaphore_signal(n_free, inc=1, device_id=device, device_id_type=MESH)

    def free_rc():
        pl.semaphore_signal(rc_free, inc=1, device_id=other_core(), device_id_type=MESH)

    def out_part(i, carry):
        columns = pl.ds(pl.multiple_of(i * 512, 512), 512)
        total = dot(act[...], w2[:, :, :, columns].reshape(UNITS, 512), 1, 0)
        total = total.reshape(4, 2, 128, 512) + zo[:, :, pl.ds(0, 128), columns].astype(f32)
        zo[:, :, pl.ds(0, 128), columns] = total.astype(bf16)
        return carry

    def down_part(i, carry):
        columns = pl.ds(pl.multiple_of(i * 512, 512), 512)
        right = u[:, :, :, columns].reshape(SEQ, 512)
        w2[:, :, :, columns] = dot(act[...], right, 0, 0).astype(bf16).reshape(4, 4, 64, 512)
        return carry

    own_tokens, own_cot = u.at[0, 0], u.at[0, 1]
    again = [
        pltpu.make_async_copy(tokens, own_tokens, sem_l.at[7]),
        pltpu.make_async_copy(cotangent, own_cot, sem_l.at[8]),
    ]

    def reload():
        copies_u.sent()
        for copy in again:
            copy.start()

    def finish_grad():
        for copy in again:
            copy.wait()
        gain = joined(0)
        zero = jnp.zeros((1, WIDTH), f32)

        def finish_rows(i, carry):
            d_gain, d_shift, d_bias = carry
            part = pl.ds(pl.multiple_of(i * 32, 32), 32)
            grads = zd[z, core, part, :].astype(f32)
            grads = grads + zd_r2[0, part, :].astype(f32) + zd_r2[1, part, :].astype(f32)
            values = own_tokens[part, :].astype(f32)
            average = jnp.mean(values, axis=-1, keepdims=True)
            centered = values - average
            variance = jnp.mean(centered * centered, axis=-1, keepdims=True)
            scale = lax.rsqrt(variance + epsilon)
            standard = centered * scale
            d_gain = d_gain + jnp.sum(grads * standard, axis=0, keepdims=True)
            d_shift = d_shift + jnp.sum(grads, axis=0, keepdims=True)
            scaled = grads * gain
            inner = scaled - jnp.mean(scaled, axis=-1, keepdims=True)
            inner = inner - standard * jnp.mean(scaled * standard, axis=-1, keepdims=True)
            upstream = own_cot[part, :].astype(f32)
            d_bias = d_bias + jnp.sum(upstream, axis=0, keepdims=True)
            zd_r2[0, part, :] = (upstream + scale * inner).astype(bf16)
            return d_gain, d_shift, d_bias

        kept["sums"] = lax.fori_loop(0, 4, finish_rows, (zero, zero, zero))
        put(zd_r2.at[0], token_grad)

    def vector_terms():
        gv[...] = jnp.zeros((4, 4, 16, 128), f32)
        for i in range(16):
            lanes = slice(i * 128, i * 128 + 128)
            for at, sums in enumerate(kept["sums"]):
                gv[i // 4, i % 4, at : at + 1, :] = sums[:, lanes]
        ones = jnp.ones((8, SEQ), bf16)
        d_qkv = dot(ones, dproj[...], 1, 0)[0:1, :]
        d_up = dot(ones, dhid[...], 1, 0)[0:1, :]
        for which in range(3):
            for i in range(2):
                at = which * 16 + c * 2 + i
                start = which * COLS + i * 128
                target = at // 3
                term = d_qkv[:, start : start + 128]
                gv[target // 4, target % 4, pl.ds(3 + at % 3, 1), :] = term
        for m in range(8):
            both = d_up[:, m * 128 : m * 128 + 128]
            moved = pltpu.roll(both, 64, 1)
            here = (lane >= 64) == odd
            for i, (even_place, odd_place) in enumerate(((both, moved), (moved, both))):
                at = 2 * m + i
                term = jnp.where(here, jnp.where(odd, odd_place, even_place), 0.0)
                gv[at // 4, at % 4, pl.ds(6 + c // 2, 1), :] = term

    def to_owner(j):
        return pltpu.make_async_remote_copy(
            src_ref=pt,
            dst_ref=gp.at[pl.ds(16 * j, 16)],
            send_sem=sem_p.at[0, 0],
            recv_sem=sem_p.at[1, j],
            device_id=(c, owner),
            device_id_type=MESH,
        )

    def trade(k, src, dst, device):
        return pltpu.make_async_remote_copy(
            src_ref=src,
            dst_ref=dst,
            send_sem=sem_b.at[0, k],
            recv_sem=sem_b.at[1, k],
            device_id=device,
            device_id_type=MESH,
        )

    mine = core == x // 2
    turns_z = (z - y + 4) % 4
    to_zu, to_zd = (up1(z) * 2 + core, f), (down1(z) * 2 + core, f)
    to_core = other_core()
    h0, h1 = gp.at[pl.ds(0, 64)], gp.at[pl.ds(64, 64)]

    def proj_owner():
        put(w1.at[y, x, pl.ds(0, 128)], gq_out.at[z, core])
        for j, (start, size) in enumerate(PROJ):
            pt[:, start : start + size] = w1[y, x, 128 + 16 * j : 144 + 16 * j, 0:size]
        for j in range(8):

            @pl.when((f % 8 == j) & (owner != f))
            def _():
                to_owner(j).start()

            @pl.when((f % 8 == j) & (owner == f))
            def _():
                local = pltpu.make_async_copy(pt, gp.at[pl.ds(16 * j, 16)], sem_p.at[0, 1])
                local.start()
                local.wait()

    def proj_along():
        for j in range(8):

            @pl.when(own_rows & ((f % 2) * 8 + j != f))
            def _():
                slot = gp.at[pl.ds(16 * j, 16)]
                pltpu.make_async_remote_copy(
                    src_ref=slot,
                    dst_ref=slot,
                    send_sem=sem_p.at[0, 0],
                    recv_sem=sem_p.at[1, j],
                    device_id=other_core(),
                    device_id_type=MESH,
                ).wait_recv()

        @pl.when(mine & (turns_z == 0))
        def _():
            trade(0, gp, gp, to_zu).start()
            trade(1, gp, gp, to_zd).start()

    def proj_further():
        @pl.when(mine & (turns_z == 1))
        def _():
            trade(0, gp, gp, to_core).wait_recv()
            trade(2, h0, h0, to_zu).start()

        @pl.when(mine & (turns_z == 3))
        def _():
            trade(1, gp, gp, to_core).wait_recv()
            trade(3, h1, h1, to_zd).start()

    def proj_across():
        @pl.when(mine & (turns_z == 2))
        def _():
            trade(2, h0, h0, to_core).wait_recv()
            trade(3, h1, h1, to_core).wait_recv()

        @pl.when(mine)
        def _():
            trade(4, gp, gp, to_core).start()

    def proj_end():
        @pl.when(jnp.logical_not(mine))
        def _():
            trade(4, gp, gp, to_core).wait_recv()

        put(gp, gp_out)

    def finish_out():
        proj_bias, down_bias = joined(2), joined(3)
        tail = pl.ds(128, 16)
        sums = zo[z, core, tail, :].astype(f32)
        sums = sums + zo_r2[0, tail, :].astype(f32) + zo_r2[1, tail, :].astype(f32)
        sums = sums[0:2, :] + sums[2:4, :]
        for h in range(32):
            lanes = slice((h % 16) * 128, (h % 16) * 128 + 128)
            lse_own[h : h + 1, :] = sums[h // 16 : h // 16 + 1, lanes]

        def finish_rows(i, carry):
            part = pl.ds(pl.multiple_of(i * 32, 32), 32)
            total = zo[z, core, part, :].astype(f32)
            total = total + zo_r2[0, part, :].astype(f32) + zo_r2[1, part, :].astype(f32)
            total = own_tokens[part, :].astype(f32) + total + proj_bias + down_bias
            zo_r2[0, part, :] = total.astype(bf16)
            return carry

        lax.fori_loop(0, 4, finish_rows, 0)
        put(zo_r2.at[0, pl.ds(0, 128)], block_out)
        put(lse_own, lse_out)

    def loop(first, last, body):
        return lambda: lax.fori_loop(first, last, body, 0)

    actions = dict(
        gather1=gather1,
        gather2=gather2,
        gather3=gather3,
        gather_t=gather_t,
        gather_u=gather_u,
        gather_s=gather_s,
        reduce1=reduce1,
        reduce2=reduce2,
        reduce2a=reduce2a,
        reduce2b=reduce2b,
        reduce3=reduce3,
        reduce_o=reduce_o,
        reduce_d=reduce_d,
        reduce_v=reduce_v,
        spread_q=spread_q,
        spread_u=spread_u,
        spread_d=spread_d,
        spread_da=spread_da,
        spread_db=spread_db,
        spread_v=spread_v,
        load_t=loads[0].wait,
        load_u=loads[1].wait,
        load_2=loads[2].wait,
        load_1=load_1,
        pack=pack,
        tables=tables,
        norm=norm,
        stats=statistics,
        up_bias=up_bias,
        project=project,
        dctx=context_grad,
        att3=lambda: attention(3),
        att2=lambda: attention(2),
        att1=lambda: attention(1),
        att0=lambda: attention(0),
        join=join,
        dn1a=loop(0, 2, normed_part),
        dn1b=loop(2, 4, normed_part),
        gqa=loop(0, 2, qkv_part),
        gqb=loop(2, 4, qkv_part),
        gp=proj_part,
        lse=log_sums,
        ff1a=loop(0, 1, feed),
        ff1b=loop(1, 2, feed),
        ff1c=loop(2, 3, feed),
        ff1d=loop(3, 4, feed),
        ff1=loop(0, 4, feed),
        ff2a=loop(0, 1, feed_back),
        ff2b=loop(1, 2, feed_back),
        ff2c=loop(2, 3, feed_back),
        ff2d=loop(3, 4, feed_back),
        ff2=loop(0, 4, feed_back),
        dn2a=loop(0, 2, normed_more),
        dn2b=loop(2, 4, normed_more),
        sent3=copies3.sent,
        gua=loop(0, 2, up_part),
        gub=loop(2, 4, up_part),
        free_n=free_n,
        free_rc=free_rc,
        oa=loop(0, 2, out_part),
        ob=loop(2, 4, out_part),
        wait_rc=lambda: pl.semaphore_wait(rc_free, 1),
        sent2=copies2.sent,
        gda=loop(0, 2, down_part),
        gdb=loop(2, 4, down_part),
        reload=reload,
        wait_n=lambda: pl.semaphore_wait(n_free, 4),
        fgrad=finish_grad,
        vec=vector_terms,
        proj_owner=proj_owner,
        proj_along=proj_along,
        proj_further=proj_further,
        proj_across=proj_across,
        proj_end=proj_end,
        fout=finish_out,
        put_u=lambda: put(w3.at[y, x], gu_out.at[z, core]),
        put_d=lambda: put(w2.at[y, x], gd_out.at[z, core]),
        put_da=lambda: put(w2.at[y, x, :, left], gd_out.at[z, core, :, left]),
        put_db=lambda: put(w2.at[y, x, :, right], gd_out.at[z, core, :, right]),
        put_v=lambda: put(gv.at[y, x], gv_out.at[z, core]),
    )
    for name in ORDER:
        action = actions[name]
        if callable(action):
            action()
        else:
            next(action)

    for copies in (
        copies_s, copies_r1, copies_r2, copies_r5, copies_r3, copies_v, copies_zo, copies_zd,
        copies_lq, copies_lu, copies_ld, copies_le, copies_lv,
    ):
        copies.sent()
    for j in range(8):
        target = (f % 2) * 8 + j

        @pl.when(own_rows & (target != f))
        def _():
            scatter(j, target).wait_send()

    @pl.when(owner != f)
    def _():
        to_owner(0).wait_send()

    @pl.when(mine & (turns_z == 0))
    def _():
        trade(0, gp, gp, to_zu).wait_send()
        trade(1, gp, gp, to_zd).wait_send()

    @pl.when(mine & (turns_z == 1))
    def _():
        trade(2, h0, h0, to_zu).wait_send()

    @pl.when(mine & (turns_z == 3))
    def _():
        trade(3, h1, h1, to_zd).wait_send()

    @pl.when(mine)
    def _():
        trade(4, gp, gp, to_core).wait_send()

    for copy in outs:
        copy.wait()


def layer_call(*operands):
    anyspace = pl.BlockSpec(memory_space=pl.ANY)
    vmem = pl.BlockSpec(memory_space=VM)
    dma = pltpu.SemaphoreType.DMA
    return pl.pallas_call(
        layer_kernel,
        out_shape=[
            jax.ShapeDtypeStruct((128, WIDTH), bf16),
            jax.ShapeDtypeStruct((128, WIDTH), bf16),
            jax.ShapeDtypeStruct((32, 128), f32),
            jax.ShapeDtypeStruct((4, 2, 128, 768), bf16),
            jax.ShapeDtypeStruct((4, 2, 128, UNITS), bf16),
            jax.ShapeDtypeStruct((4, 2, 64, WIDTH), bf16),
            jax.ShapeDtypeStruct((128, WIDTH), bf16),
            jax.ShapeDtypeStruct((4, 2, 16, 128), f32),
        ],
        in_specs=[anyspace] * 6 + [vmem] * 7,
        out_specs=[anyspace] * 8,
        scratch_shapes=[
            VM((4, 4, 192, 768), bf16),
            VM((4, 4, 64, WIDTH), bf16),
            VM((4, 4, 128, UNITS), bf16),
            VM((4, 2, 144, WIDTH), bf16),
            VM((4, 2, 16, 128), f32),
            VM((4, 2, 128, WIDTH), bf16),
            VM((2, 2, 8, 32, WIDTH), bf16),
            VM((4, 2, 128, WIDTH), bf16),
            VM((4, 144, WIDTH), bf16),
            VM((2, 80, WIDTH), bf16),
            VM((2, 144, WIDTH), bf16),
            VM((2, 64, WIDTH), bf16),
            VM((2, 128, WIDTH), bf16),
            VM((2, 8, 96, 768), bf16),
            VM((2, 8, 80, 768), bf16),
            VM((2, 8, 64, UNITS), bf16),
            VM((2, 8, 64, UNITS), bf16),
            VM((16, 16, 128), f32),
            VM((3, SEQ, 128), f32),
            VM((128, 128), f32),
            VM((SEQ, COLS), bf16),
            VM((SEQ, COLS), bf16),
            VM((SEQ, COLS), bf16),
            VM((SEQ, COLS), bf16),
            VM((SEQ, COLS), bf16),
            VM((SEQ, COLS), f32),
            VM((SEQ, COLS), f32),
            VM((SEQ, 768), bf16),
            VM((SEQ, UNITS), bf16),
            VM((SEQ, UNITS), bf16),
            VM((8, SEQ), f32),
            VM((32, 128), f32),
            VM((16, WIDTH), bf16),
            VM((128, WIDTH), bf16),
            VM((4, 4, 16, 128), f32),
            VM((3, 4, 16, 128), f32),
            VM((3, 16, 128), f32),
            dma((2, 16)),
            dma((2, 16)),
            dma((2, 16)),
            dma((2, 8)),
            dma((2, 8)),
            dma((2, 8)),
            dma((2, 16)),
            dma((2, 16)),
            dma((2, 16)),
            dma((2, 6)),
            dma((2, 5)),
            dma((2, 5)),
            dma((2, 8)),
            dma((2, 8)),
            dma((2, 8)),
            dma((2, 8)),
            dma((2, 16)),
            dma((2, 8)),
            dma((2, 8)),
            dma((2, 8)),
            dma((2, 5)),
            dma((9,)),
            dma((9,)),
            pltpu.SemaphoreType.REGULAR,
            pltpu.SemaphoreType.REGULAR,
        ],
        compiler_params=pltpu.CompilerParams(
            collective_id=1, has_side_effects=True, vmem_limit_bytes=62 * 1024 * 1024
        ),
        cost_estimate=pl.CostEstimate(
            flops=45 * 10**9, bytes_accessed=40 * 10**6, transcendentals=4 * 10**6
        ),
        name="layer",
    )(*operands)


def finish_kernel(
    gq,
    gu,
    gd,
    gp,
    gv,
    out,
    grad,
    log_sums,
    qkv_out,
    up_out,
    down_out,
    proj_out,
    gain_out,
    shift_out,
    proj_bias_out,
    down_bias_out,
    qkv_bias_out,
    up_bias_out,
    out_out,
    grad_out,
    log_sums_out,
):
    lane = lax.broadcasted_iota(jnp.int32, (1, 128), 1)
    for which in range(3):
        for c in range(8):
            part = gq[c, :, which * COLS : which * COLS + COLS]
            qkv_out[:, which * WIDTH + c * COLS : which * WIDTH + (c + 1) * COLS] = part.astype(f32)
    for pair in range(4):
        for m in range(8):
            a = gu[2 * pair, :, 128 * m : 128 * m + 128].astype(f32)
            b = gu[2 * pair + 1, :, 128 * m : 128 * m + 128].astype(f32)
            for odd in range(2):
                at = (2 * m + odd) * 512 + pair * 128
                up_out[:, at : at + 128] = halves_packed(a, b, odd == 1, lane)
    down_out[...] = gd[0].astype(f32)
    proj_out[...] = gp[...].astype(f32)
    out_out[...] = out[...]
    grad_out[...] = grad[...]
    log_sums_out[...] = log_sums[...]
    sums = jnp.sum(gv[...], axis=0)
    gain_out[...] = sums[0]
    shift_out[...] = sums[1]
    proj_bias_out[...] = sums[2]
    down_bias_out[...] = sums[2]
    for i in range(3):
        qkv_bias_out[128 * i : 128 * i + 128] = sums[3 + i]
    for i in range(4):
        up_bias_out[128 * i : 128 * i + 128] = sums[6 + i]


def finish_call(*operands):
    steps = 4
    rows = 128 // steps
    return pl.pallas_call(
        finish_kernel,
        grid=(steps,),
        out_shape=[
            jax.ShapeDtypeStruct((128, 3 * WIDTH), f32),
            jax.ShapeDtypeStruct((128, HIDDEN), f32),
            jax.ShapeDtypeStruct((512, WIDTH), f32),
            jax.ShapeDtypeStruct((128, WIDTH), f32),
            jax.ShapeDtypeStruct((128,), f32),
            jax.ShapeDtypeStruct((128,), f32),
            jax.ShapeDtypeStruct((128,), f32),
            jax.ShapeDtypeStruct((128,), f32),
            jax.ShapeDtypeStruct((384,), f32),
            jax.ShapeDtypeStruct((512,), f32),
            jax.ShapeDtypeStruct((128, WIDTH), bf16),
            jax.ShapeDtypeStruct((128, WIDTH), bf16),
            jax.ShapeDtypeStruct((32, 128), f32),
        ],
        in_specs=[
            pl.BlockSpec((8, rows, 768), lambda i: (0, i, 0)),
            pl.BlockSpec((8, rows, UNITS), lambda i: (0, i, 0)),
            pl.BlockSpec((1, 128, WIDTH), lambda i: (i, 0, 0)),
            pl.BlockSpec((rows, WIDTH), lambda i: (i, 0)),
            pl.BlockSpec((8, 16, 128), lambda i: (0, 0, 0)),
            pl.BlockSpec((rows, WIDTH), lambda i: (i, 0)),
            pl.BlockSpec((rows, WIDTH), lambda i: (i, 0)),
            pl.BlockSpec((32, 128), lambda i: (0, 0)),
        ],
        out_specs=[
            pl.BlockSpec((rows, 3 * WIDTH), lambda i: (i, 0)),
            pl.BlockSpec((rows, HIDDEN), lambda i: (i, 0)),
            pl.BlockSpec((128, WIDTH), lambda i: (i, 0)),
            pl.BlockSpec((rows, WIDTH), lambda i: (i, 0)),
            pl.BlockSpec((128,), lambda i: (0,)),
            pl.BlockSpec((128,), lambda i: (0,)),
            pl.BlockSpec((128,), lambda i: (0,)),
            pl.BlockSpec((128,), lambda i: (0,)),
            pl.BlockSpec((384,), lambda i: (0,)),
            pl.BlockSpec((512,), lambda i: (0,)),
            pl.BlockSpec((rows, WIDTH), lambda i: (i, 0)),
            pl.BlockSpec((rows, WIDTH), lambda i: (i, 0)),
            pl.BlockSpec((32, 128), lambda i: (0, 0)),
        ],
        compiler_params=pltpu.CompilerParams(vmem_limit_bytes=62 * 1024 * 1024),
        cost_estimate=pl.CostEstimate(
            flops=10**6, bytes_accessed=20 * 10**6, transcendentals=0
        ),
        name="finish",
    )(*operands)


def local(
    tokens,
    segments,
    ln_gain,
    ln_shift,
    qkv_weight,
    qkv_bias,
    proj_weight,
    proj_bias,
    up_weight,
    up_bias,
    down_weight,
    down_bias,
    cotangent,
):
    block_out, token_grad, log_sums, gq, gu, gd, gp, gv = layer_call(
        tokens[0],
        cotangent[0],
        qkv_weight,
        proj_weight,
        up_weight,
        down_weight,
        segments,
        ln_gain[None],
        ln_shift[None],
        proj_bias[None],
        down_bias[None],
        qkv_bias,
        up_bias,
    )
    qkv_grad, up_grad, down_grad, proj_grad, *vectors = finish_call(
        gq.reshape(8, 128, 768),
        gu.reshape(8, 128, UNITS),
        gd.reshape(4, 128, WIDTH),
        gp,
        gv.reshape(8, 16, 128),
        block_out,
        token_grad,
        log_sums,
    )
    return (
        vectors[6][None],
        vectors[7][None],
        vectors[8][None],
        vectors[0],
        vectors[1],
        qkv_grad,
        vectors[4],
        proj_grad,
        vectors[2],
        up_grad,
        vectors[5],
        down_grad,
        vectors[3],
    )


def solution(mesh):
    in_specs = (
        P("fsdp", "ctx", None),
        P("fsdp", "ctx"),
        P("fsdp"),
        P("fsdp"),
        P("fsdp", None),
        P("fsdp"),
        P("fsdp", None),
        P("fsdp"),
        P("fsdp", None),
        P("fsdp"),
        P("fsdp", None),
        P("fsdp"),
        P("fsdp", "ctx", None),
    )
    out_specs = (
        P("fsdp", "ctx", None),
        P("fsdp", "ctx", None),
        P("fsdp", None, "ctx"),
        P("fsdp"),
        P("fsdp"),
        P("fsdp", None),
        P("fsdp"),
        P("fsdp", None),
        P("fsdp"),
        P("fsdp", None),
        P("fsdp"),
        P("fsdp", None),
        P("fsdp"),
    )
    return jax.shard_map(local, mesh=mesh, in_specs=in_specs, out_specs=out_specs, check_vma=False)
```
